512 devices in a mesh: seq: 64 (over y, z), chan: 8 (over x, core).
Axes of the slice: x: 4, y: 8, z: 8, core: 2. Of those that a mesh axis runs over, the one named last changes fastest.
Arguments:
- qkv: bfloat16 [3, 24576, 8192], P(None, 'seq', 'chan'), may hold values from -6 to 6
- feat_taps: float32 [3, 7, 8192], P(None, None, 'chan'), may hold values from -2.5 to 2.5
- long_filter: bfloat16 [128, 512], P(None, 'chan'), may hold values from -0.5 to 0.5
- skip_gain: float32 [8192], P('chan'), may hold values from -6 to 6
- out_weight: bfloat16 [8192, 4096], P('chan', 'seq'), may hold values from -0.1875 to 0.1875
Outputs:
- mixed: bfloat16 [24576, 4096], P('seq', 'chan')
The draws below stay inside these ranges and needn't reach their ends.
All inputs are finite; a program needn't handle non-finite values.
Results may differ from the reference program's by a relative error of at most 0.017.
Values may be sent and summed in bfloat16 or wider, within the bound.
A program may use at most 64 MiB of HBM per device.

```python
import jax
import jax.numpy as jnp
from jax import lax

D = 8192
DOUT = 4096
GROUP = 16
TAPS = 128
FTAPS = 7
TOKENS = 24576
GROUPS = 512
N_CHAN = 8


def strengthened(drawn, rng, source, target, parts, factor):
    owner, partner = [(jnp.arange(drawn.shape[axis_at]) // (drawn.shape[axis_at] // parts)).reshape([-1 if axis == axis_at else 1 for axis in range(drawn.ndim)]) for axis_at in (source, target)]
    chosen = jax.random.permutation(rng, parts)[partner]
    strong = (owner == chosen) | (owner == (partner + parts // 2) % parts)
    return jnp.where(strong, factor * drawn, drawn)


def block_levels(stream_key, shape, shards, smallest, top_value):
    def one(axis_at, blocks):
        steps = jax.random.uniform(jax.random.fold_in(jax.random.fold_in(stream_key, 6), axis_at), (blocks,), jnp.float32, smallest / len(shards), top_value / len(shards))
        return jnp.repeat(jnp.exp(steps), shape[axis_at] // blocks).reshape((-1,) + (1,) * (len(shape) - axis_at - 1))

    level = one(*shards[0])
    for cut in shards[1:]:
        level = level * one(*cut)
    return level


def gaussian(rng, dims, scale, most, pieces=(), kind=jnp.bfloat16):
    values = jax.random.normal(rng, dims, jnp.float32) * scale
    if len(pieces) > 0:
        values = block_levels(rng, dims, pieces, -0.22, 0.18) * values
    return jnp.clip(values, min=-most, max=most).astype(kind)


def bell_draw_with(own_key, dims, scale, bound, cuts, heavy, kind=jnp.bfloat16):
    values = scale * jax.random.normal(own_key, dims, jnp.float32)
    if cuts:
        values = values * block_levels(own_key, dims, cuts, -0.22, 0.18)
    return jnp.clip(strengthened(values, jax.random.fold_in(own_key, 3), *heavy), -bound, bound).astype(kind)


def setup_inputs(seed: int = 0) -> dict:
    keys = jax.random.split(jax.random.key(seed), 6)
    qkv = gaussian(keys[0], (3, TOKENS, D), 1.0, 6.0, ((1, 64), (2, 8)))
    feat_taps = gaussian(keys[1], (3, FTAPS, D), 0.4, 2.5, ((2, 8),), jnp.float32)
    long_filter = gaussian(keys[2], (TAPS, GROUPS), 0.09, 0.5, ((1, 8),))
    skip_gain = gaussian(keys[3], (D,), 1.0, 6.0, ((0, 8),), jnp.float32)
    out_weight = bell_draw_with(keys[4], (D, DOUT), D ** -0.5, 0.1875, ((0, 8), (1, 64)), (0, 1, 64, 4.0))
    return {"qkv": qkv, "feat_taps": feat_taps, "long_filter": long_filter, "skip_gain": skip_gain, "out_weight": out_weight}


def causal_sum(values, taps, count):
    padded = jnp.concatenate([jnp.zeros((count - 1, values.shape[1]), jnp.float32), values], axis=0)

    def add_tap(j, total):
        part = lax.dynamic_slice_in_dim(padded, (count - 1 - j).astype(jnp.int32), values.shape[0], 0)
        return total + taps[j] * part

    return lax.fori_loop(0, count, add_tap, jnp.zeros(values.shape, jnp.float32))


def reference(qkv, feat_taps, long_filter, skip_gain, out_weight):
    width = D // N_CHAN
    narrow = width // GROUP

    def block_term(carry, index):
        start = (index * width).astype(jnp.int32)
        cols = lax.dynamic_slice_in_dim(qkv, start, width, 2).astype(jnp.float32)
        taps = lax.dynamic_slice_in_dim(feat_taps, start, width, 2)
        feats = [causal_sum(cols[i], taps[i], FTAPS) for i in range(3)]
        rounded = (feats[1] * feats[2]).astype(jnp.bfloat16)
        rounded = lax.optimization_barrier(rounded).astype(jnp.float32)
        filt = lax.dynamic_slice_in_dim(long_filter, (index * narrow).astype(jnp.int32), narrow, 1)
        filt = jnp.repeat(filt.astype(jnp.float32), GROUP, axis=1)
        skip = lax.dynamic_slice_in_dim(skip_gain, start, width, 0)
        z = causal_sum(rounded, filt, TAPS) + skip * rounded
        y = (feats[0] * z).astype(jnp.bfloat16)
        rows = lax.dynamic_slice_in_dim(out_weight, start, width, 0)
        part = jnp.dot(y, rows, preferred_element_type=jnp.float32).astype(jnp.bfloat16)
        part = lax.optimization_barrier(part).astype(jnp.float32)
        return carry + part, None

    total, unused = lax.scan(block_term, jnp.zeros((TOKENS, DOUT), jnp.float32), jnp.arange(N_CHAN, dtype=jnp.int32))
    return total.astype(jnp.bfloat16)
```

```python
import jax
import jax.numpy as jnp
from jax import lax
from jax.experimental import pallas as pl
from jax.experimental.pallas import tpu as pltpu
from jax.sharding import PartitionSpec as P

MESH = pl.DeviceIdType.MESH
F32 = jnp.float32
BF16 = jnp.bfloat16

RING = 8
GROUP = 16
SPAN = 128
FTAPS = 7
ROWS = 384
WIDTH = 1024
BLOCKS = ROWS // SPAN
LANES = 128
STRIPS = WIDTH // LANES
PIECE = 32
HALO = 16
PAD = 8

OFF = (0, 1, -1, 2, -2, 3, -3, 4)
SLOT = {off: slot for slot, off in enumerate(OFF)}
PACKS = ((0, 1), (1, 3), (3, 5), (5, 7), (7, 8))
FAR_UP = (0, 1, 4)
ROUNDS = ((1, 2), (3, 4), (5, 6), (0, 7))


def origin(direction, step):
    return SLOT[4 if step == 4 else -direction * step]


def kernel(
    qkv_ref, taps_ref, filt_ref, skip_ref, w_ref, out_ref,
    w_all, qkv_v, halo, ext, ut, qt, skt, hf, yt,
    ta, sa, qa, tb, sb, qb, ra, rb, fin,
    load_sem, own_sem, halo_sem, tail_sem,
    s1, r1, s2, r2, as1, ar1, as2, ar2, bs1, br1, bs2, br2,
):
    s = lax.axis_index("seq")
    c = lax.axis_index("chan")
    y = lax.div(s, RING)
    z = lax.rem(s, RING)
    x = lax.div(c, 2)
    p = lax.rem(c, 2)

    def y_at(d):
        return {"seq": lax.rem(y + d + RING, RING) * RING + z}

    def z_at(d):
        return {"seq": y * RING + lax.rem(z + d + RING, RING)}

    def seq_at(d):
        return {"seq": lax.rem(s + d + RING * RING, RING * RING)}

    sibling = {"chan": c + 1 - 2 * p}
    minor_at = (z_at, y_at)
    major_at = (y_at, z_at)
    started = []

    def remote(src, dst, send, recv, to):
        return pltpu.make_async_remote_copy(
            src_ref=src, dst_ref=dst, send_sem=send, recv_sem=recv, device_id=to, device_id_type=MESH
        )

    def go(copy):
        copy.start()
        started.append(copy)

    loads = [
        pltpu.make_async_copy(qkv_ref.at[i], qkv_v.at[i], load_sem.at[i]) for i in (1, 2, 0)
    ]
    own = [
        pltpu.make_async_copy(
            w_ref.at[PIECE * kind : PIECE * (kind + 1)], w_all.at[kind, 0, 0], own_sem.at[kind]
        )
        for kind in range(2)
    ]
    for copy in loads + own:
        copy.start()

    barrier = pltpu.get_barrier_semaphore()
    greeted = [{"chan": lax.rem(c + d, 8)} for d in range(1, 8)]
    greeted += [z_at(1), z_at(-1), y_at(1), y_at(-1), seq_at(1), seq_at(-1)]
    for to in greeted:
        pl.semaphore_signal(barrier, inc=1, device_id=to, device_id_type=MESH)
    pl.semaphore_wait(barrier, len(greeted))

    def first(kind, direction, step):
        lane = 0 if direction == 1 else 1
        into = origin(direction, step)
        if step == 1:
            src, dst = w_ref.at[PIECE * kind : PIECE * (kind + 1)], w_all.at[kind, 0, into]
        elif step < 4:
            src, dst = w_all.at[kind, 0, origin(direction, step - 1)], w_all.at[kind, 0, into]
        else:
            half = pl.ds(lane * (PIECE // 2), PIECE // 2)
            src = w_all.at[kind, 0, origin(direction, 3), half]
            dst = w_all.at[kind, 0, into, half]
        at = kind, lane, step - 1
        return remote(src, dst, s1.at[at], r1.at[at], minor_at[kind](direction))

    def second(kind, direction, step, pack):
        lane = 0 if direction == 1 else 1
        lo, hi = PACKS[pack]
        into = origin(direction, step)
        if step == 1 and pack == 0:
            src, dst = w_ref.at[PIECE * kind : PIECE * (kind + 1)], w_all.at[kind, into, 0]
        else:
            came = 0 if step == 1 else origin(direction, step - 1)
            src = w_all.at[kind, came, pl.ds(lo, hi - lo)]
            dst = w_all.at[kind, into, pl.ds(lo, hi - lo)]
        at = kind, lane, step - 1, pack
        return remote(src, dst, s2.at[at], r2.at[at], major_at[kind](direction))

    def lanes_of(step, pack):
        if step < 4:
            return (1, -1)
        return (1,) if pack in FAR_UP else (-1,)

    def first_arrives(step):
        for kind in range(2):
            for direction in (1, -1):
                first(kind, direction, step).wait_recv()
                if step < 4:
                    go(first(kind, direction, step + 1))
        for kind in range(2):
            for direction in (1, -1):
                go(second(kind, direction, 1, step))

    def second_arrives(step, pack):
        for kind in range(2):
            for direction in lanes_of(step, pack):
                second(kind, direction, step, pack).wait_recv()
                if step < 4 and direction in lanes_of(step + 1, pack):
                    go(second(kind, direction, step + 1, pack))

    events = [(2.2 * k, first_arrives, (k,)) for k in range(1, 5)]
    events += [
        (2.6 + 10.5 * (k - 1) + 2.4 * g, second_arrives, (k, g)) for k in range(1, 5) for g in range(5)
    ]
    events.sort(key=lambda e: e[0])
    events = [(at, fn, args) for at, fn, args in events]
    clock = [0.0]
    seen = set()

    def take_event():
        at, fn, args = events.pop(0)
        fn(*args)
        if fn is second_arrives:
            seen.add(args)
        else:
            seen.add(args[0])
        clock[0] = max(clock[0], at)

    def work(cost, fn, *args):
        while events and events[0][0] <= clock[0]:
            take_event()
        fn(*args)
        clock[0] += cost

    def need(step):
        wanted = {(step, g) for g in range(5)}
        while not wanted <= seen:
            take_event()

    halo_copy = remote(
        qkv_ref.at[:, ROWS - HALO : ROWS], halo, halo_sem.at[0], halo_sem.at[1], seq_at(1)
    )
    go(halo_copy)
    for kind in range(2):
        for direction in (1, -1):
            go(first(kind, direction, 1))
    for kind in range(2):
        for direction in (1, -1):
            go(second(kind, direction, 1, 0))

    def widen(strip):
        at = pl.ds(pl.multiple_of(strip * LANES, LANES), LANES)
        for i in range(3):
            ext[i, strip, PAD:, :] = qkv_v[i, :, at].astype(F32)

    def widen_halo(strip):
        at = pl.ds(pl.multiple_of(strip * LANES, LANES), LANES)
        for i in range(3):
            before = halo[i, :, at].astype(F32)[HALO - PAD :]
            ext[i, strip, :PAD, :] = jnp.where(s == 0, 0.0, before)

    def feature(i, block, strip, at):
        total = None
        for j in range(FTAPS):
            term = taps_ref[i, j : j + 1, at] * ext[i, strip, pl.ds(PAD + SPAN * block - j, SPAN), :]
            total = term if total is None else total + term
        return total

    def features(block, strips):
        def body(strip, carry):
            at = pl.ds(pl.multiple_of(strip * LANES, LANES), LANES)
            u = (feature(1, block, strip, at) * feature(2, block, strip, at)).astype(BF16).astype(F32)
            ut[block + 1, at, :] = u.T.astype(BF16)
            qt[block, at, :] = feature(0, block, strip, at).T
            return carry

        lax.fori_loop(strips[0], strips[1], body, 0)

    def widen_all():
        for copy in loads:
            copy.wait()

        def body(strip, carry):
            widen(strip)
            return carry

        lax.fori_loop(0, STRIPS, body, 0)
        hf[...] = filt_ref[...].astype(F32)

    def halo_arrives():
        halo_copy.wait_recv()

        def body(strip, carry):
            widen_halo(strip)
            at = pl.ds(pl.multiple_of(strip * LANES, LANES), LANES)
            skt[at, :] = jnp.broadcast_to(skip_ref[:, at], (LANES, LANES)).T
            return carry

        lax.fori_loop(0, STRIPS, body, 0)

    tail_copy = remote(ut.at[BLOCKS], ut.at[0], tail_sem.at[0], tail_sem.at[1], seq_at(1))

    def send_tail():
        go(tail_copy)

    def tail_arrives():
        tail_copy.wait_recv()

        @pl.when(s == 0)
        def clear():
            ut[0] = jnp.zeros((WIDTH, SPAN), BF16)

    def conv(lo, hi):
        def body(g, carry):
            row = lax.broadcasted_iota(jnp.int32, (SPAN, SPAN), 0)
            col = lax.broadcasted_iota(jnp.int32, (SPAN, SPAN), 1)
            taps = jnp.broadcast_to(hf[pl.ds(g, 1), :], (SPAN, SPAN))
            ring = pltpu.roll(taps, 0, 1, stride=1, stride_axis=0)
            here = jnp.where(row <= col, ring, 0.0)
            before = jnp.where(row > col, ring, 0.0)
            matrix = jnp.concatenate([before, here], axis=0).astype(BF16)
            at = pl.ds(pl.multiple_of(g * GROUP, GROUP), GROUP)
            parts = [ut[b, at, :] for b in range(BLOCKS + 1)]
            window = jnp.concatenate(
                [jnp.concatenate(parts[:BLOCKS], axis=0), jnp.concatenate(parts[1:], axis=0)], axis=1
            )
            mixed = jnp.dot(window, matrix, preferred_element_type=F32)
            for b in range(BLOCKS):
                field = mixed[GROUP * b : GROUP * (b + 1)] + skt[at, :] * parts[b + 1].astype(F32)
                yt[at, SPAN * b : SPAN * (b + 1)] = (qt[b, at, :] * field).astype(BF16)
            return carry

        lax.fori_loop(lo, hi, body, 0, unroll=4)

    def project(pieces):
        rows = jnp.concatenate(pieces, axis=0) if len(pieces) > 1 else pieces[0]
        return jnp.dot(rows, yt[...], preferred_element_type=F32)

    def four(kind, major, half):
        return w_all[kind, major, pl.ds(4 * half, 4)].reshape(4 * PIECE, WIDTH)

    def a_swap(slot):
        return remote(ta.at[slot], sa.at[slot], as1.at[slot], ar1.at[slot], sibling)

    def a_first(slots):
        got = project([four(0, m, 1 - p) for m in slots]).astype(BF16)
        for i, m in enumerate(slots):
            ta[m] = got[4 * PIECE * i : 4 * PIECE * (i + 1)]
            go(a_swap(m))

    def target(slot):
        return lax.rem(y + OFF[slot] + RING, RING)

    def deliver(src, dst, send, recv, to):
        copy = remote(src, dst, send, recv, {"chan": to})

        @pl.when(to == c)
        def keep():
            pltpu.make_async_copy(src, dst, recv).start()

        @pl.when(to != c)
        def post():
            copy.start()

        return to, copy

    delivered = []

    def a_second(slots):
        got = project([four(0, m, p) for m in slots])
        for i, m in enumerate(slots):
            a_swap(m).wait_recv()
            qa[m] = (got[4 * PIECE * i : 4 * PIECE * (i + 1)] + sa[m].astype(F32)).astype(BF16)
            delivered.append(deliver(qa.at[m], ra.at[x, p], as2.at[m], ar2.at[x, p], target(m)))

    def b_swap(turn):
        return remote(tb.at[turn], sb.at[turn], bs1.at[turn], br1.at[turn], sibling)

    def b_rows(turn, half):
        low, high = ROUNDS[turn]
        return w_all[1, low + half * (high - low)].reshape(RING * PIECE, WIDTH)

    def b_first(turn):
        tb[turn] = project([b_rows(turn, 1 - p)]).astype(BF16)
        go(b_swap(turn))

    def b_second(turn):
        got = project([b_rows(turn, p)])
        b_swap(turn).wait_recv()
        qb[turn] = (got + sb[turn].astype(F32)).astype(BF16)
        for m in range(RING):
            delivered.append(
                deliver(
                    qb.at[turn, PIECE * m : PIECE * (m + 1)], rb.at[turn, x, p],
                    bs2.at[turn, m], br2.at[turn, x, p], target(m),
                )
            )

    def own_wait():
        for copy in own:
            copy.wait()

    work(1.0, widen_all)
    for lo in (0, 4):
        work(1.0, features, BLOCKS - 1, (lo, lo + 4))
    work(0.1, send_tail)
    for lo in (0, 4):
        work(1.0, features, 1, (lo, lo + 4))
    work(0.3, halo_arrives)
    for lo in (0, 4):
        work(1.0, features, 0, (lo, lo + 4))
    work(0.1, tail_arrives)
    for lo in range(0, 64, 16):
        work(1.2, conv, lo, lo + 16)
    work(0.1, own_wait)
    need(1)
    work(0.4, a_first, (0,))
    work(0.8, a_first, (1, 2))
    work(0.8, b_first, 0)
    work(0.4, a_second, (0,))
    work(0.8, a_second, (1, 2))
    work(0.8, b_second, 0)
    need(2)
    work(0.8, a_first, (3, 4))
    work(0.8, b_first, 1)
    work(0.8, a_second, (3, 4))
    work(0.8, b_second, 1)
    need(3)
    work(0.8, a_first, (5, 6))
    work(0.8, b_first, 2)
    work(0.8, a_second, (5, 6))
    work(0.8, b_second, 2)
    need(4)
    work(0.4, a_first, (7,))
    work(0.8, b_first, 3)
    work(0.4, a_second, (7,))
    work(0.8, b_second, 3)

    def place(kind, slot, rows):
        at = lax.rem(z + OFF[slot] + RING, RING) * (2 * PIECE) + kind * PIECE
        fin[pl.ds(pl.multiple_of(at, PIECE), PIECE), :] = rows

    def total(ref, half, lead=()):
        found = None
        for chip in range(4):
            term = ref[lead + (chip, half)].astype(F32)
            found = term if found is None else found + term
        return found

    for half in range(2):
        for chip in range(4):
            remote(ra.at[chip, half], ra.at[chip, half], as2.at[0], ar2.at[chip, half], sibling).wait_recv()
    for half in range(2):
        found = total(ra, half)
        for i in range(4):
            place(0, 4 * half + i, found[PIECE * i : PIECE * (i + 1)])
    for turn in range(4):
        for half in range(2):
            for chip in range(4):
                here = rb.at[turn, chip, half]
                remote(here, here, bs2.at[turn, 0], br2.at[turn, chip, half], sibling).wait_recv()
            place(1, ROUNDS[turn][half], total(rb, half, (turn,)))
    for a in range(BLOCKS):
        for n in range(4):
            tile = fin[LANES * n : LANES * (n + 1), SPAN * a : SPAN * (a + 1)]
            out_ref[SPAN * a : SPAN * (a + 1), LANES * n : LANES * (n + 1)] = tile.T.astype(BF16)

    for copy in started:
        copy.wait_send()
    for to, copy in delivered:
        @pl.when(to != c)
        def drain(copy=copy):
            copy.wait_send()


def local(qkv, feat_taps, long_filter, skip_gain, out_weight):
    vmem = pl.BlockSpec(memory_space=pltpu.VMEM)
    anywhere = pl.BlockSpec(memory_space=pl.ANY)
    dma = pltpu.SemaphoreType.DMA
    half_piece = (4 * PIECE, ROWS)
    return pl.pallas_call(
        kernel,
        out_shape=jax.ShapeDtypeStruct((ROWS, 512), BF16),
        in_specs=[anywhere, vmem, vmem, vmem, anywhere],
        out_specs=vmem,
        scratch_shapes=[
            pltpu.VMEM((2, RING, RING, PIECE, WIDTH), BF16),
            pltpu.VMEM((3, ROWS, WIDTH), BF16),
            pltpu.VMEM((3, HALO, WIDTH), BF16),
            pltpu.VMEM((3, STRIPS, PAD + ROWS, LANES), F32),
            pltpu.VMEM((BLOCKS + 1, WIDTH, SPAN), BF16),
            pltpu.VMEM((BLOCKS, WIDTH, SPAN), F32),
            pltpu.VMEM((WIDTH, SPAN), F32),
            pltpu.VMEM((WIDTH // GROUP, SPAN), F32),
            pltpu.VMEM((WIDTH, ROWS), BF16),
            pltpu.VMEM((RING,) + half_piece, BF16),
            pltpu.VMEM((RING,) + half_piece, BF16),
            pltpu.VMEM((RING,) + half_piece, BF16),
            pltpu.VMEM((4, RING * PIECE, ROWS), BF16),
            pltpu.VMEM((4, RING * PIECE, ROWS), BF16),
            pltpu.VMEM((4, RING * PIECE, ROWS), BF16),
            pltpu.VMEM((4, 2) + half_piece, BF16),
            pltpu.VMEM((4, 4, 2, PIECE, ROWS), BF16),
            pltpu.VMEM((512, ROWS), F32),
            dma((3,)), dma((2,)), dma((2,)), dma((2,)),
            dma((2, 2, 4)), dma((2, 2, 4)),
            dma((2, 2, 4, 5)), dma((2, 2, 4, 5)),
            dma((RING,)), dma((RING,)), dma((RING,)), dma((4, 2)),
            dma((4,)), dma((4,)), dma((4, RING)), dma((4, 4, 2)),
        ],
        compiler_params=pltpu.CompilerParams(
            collective_id=0, has_side_effects=True, vmem_limit_bytes=56 * 2**20
        ),
    )(qkv, feat_taps, long_filter.T, skip_gain.reshape(1, WIDTH), out_weight.T)


def solution(mesh):
    return jax.shard_map(
        local,
        mesh=mesh,
        in_specs=(
            P(None, "seq", "chan"),
            P(None, None, "chan"),
            P(None, "chan"),
            P("chan"),
            P("chan", "seq"),
        ),
        out_specs=P("seq", "chan"),
        check_vma=False,
    )
```

```python
import jax
import jax.numpy as jnp
from jax import lax
from jax.experimental import pallas as pl
from jax.experimental.pallas import tpu as pltpu
from jax.sharding import PartitionSpec as P

MESH = pl.DeviceIdType.MESH
F32 = jnp.float32
BF16 = jnp.bfloat16

RING = 8
GROUP = 16
SPAN = 128
FTAPS = 7
ROWS = 384
WIDTH = 1024
BLOCKS = ROWS // SPAN
LANES = 128
STRIPS = WIDTH // LANES
PIECE = 32
HALO = 16
PAD = 8

OFF = (1, -1, 2, -2, 3, -3, 4, 0)
SLOT = {off: slot for slot, off in enumerate(OFF)}
PACKS = ((7, 8), (0, 2), (2, 4), (4, 6), (6, 7))
FAR_UP = (0, 1, 4)
OWN = SLOT[0]
FAR = SLOT[4]
PAIRS = 3


def origin(direction, step):
    return SLOT[4 if step == 4 else -direction * step]


def kernel(
    qkv_ref, taps_hbm, filt_hbm, skip_hbm, w_ref, out_ref,
    taps_ref, filt_ref, skip_ref,
    w_all, qkv_v, halo, ext, ut, qt, skt, hf, yt,
    ta, sa, qa, tb, sb, qb, tc, sc, qc, ra, rb, rc, fin,
    load_sem, own_sem, halo_sem, tail_sem,
    s1, r1, s2, r2, as1, ar1, as2, ar2, bs1, br1, bs2, br2, cs1, cr1, cs2, cr2,
):
    s = lax.axis_index("seq")
    c = lax.axis_index("chan")
    y = lax.div(s, RING)
    z = lax.rem(s, RING)
    x = lax.div(c, 2)
    p = lax.rem(c, 2)

    def y_at(d):
        return {"seq": lax.rem(y + d + RING, RING) * RING + z}

    def z_at(d):
        return {"seq": y * RING + lax.rem(z + d + RING, RING)}

    def seq_at(d):
        return {"seq": lax.rem(s + d + RING * RING, RING * RING)}

    sibling = {"chan": c + 1 - 2 * p}
    minor_at = (z_at, y_at)
    major_at = (y_at, z_at)
    started = []

    def remote(src, dst, send, recv, to):
        return pltpu.make_async_remote_copy(
            src_ref=src, dst_ref=dst, send_sem=send, recv_sem=recv, device_id=to, device_id_type=MESH
        )

    def go(copy):
        copy.start()
        started.append(copy)

    loads = [
        pltpu.make_async_copy(qkv_ref.at[i], qkv_v.at[i], load_sem.at[i]) for i in (1, 2, 0)
    ]
    loads += [
        pltpu.make_async_copy(taps_hbm, taps_ref, load_sem.at[3]),
        pltpu.make_async_copy(filt_hbm, filt_ref, load_sem.at[4]),
        pltpu.make_async_copy(skip_hbm, skip_ref, load_sem.at[5]),
    ]
    own = [
        pltpu.make_async_copy(
            w_ref.at[PIECE * kind : PIECE * (kind + 1)], w_all.at[kind, OWN, OWN], own_sem.at[kind]
        )
        for kind in range(2)
    ]
    for copy in loads + own:
        copy.start()

    barrier = pltpu.get_barrier_semaphore()
    greeted = [{"chan": lax.rem(c + d, 8)} for d in range(1, 8)]
    greeted += [z_at(1), z_at(-1), y_at(1), y_at(-1), seq_at(1), seq_at(-1)]
    for to in greeted:
        pl.semaphore_signal(barrier, inc=1, device_id=to, device_id_type=MESH)
    pl.semaphore_wait(barrier, len(greeted))

    def first(kind, direction, step):
        lane = 0 if direction == 1 else 1
        into = origin(direction, step)
        if step == 1:
            src, dst = w_ref.at[PIECE * kind : PIECE * (kind + 1)], w_all.at[kind, OWN, into]
        elif step < 4:
            src, dst = w_all.at[kind, OWN, origin(direction, step - 1)], w_all.at[kind, OWN, into]
        else:
            half = pl.ds(lane * (PIECE // 2), PIECE // 2)
            src = w_all.at[kind, OWN, origin(direction, 3), half]
            dst = w_all.at[kind, OWN, into, half]
        at = kind, lane, step - 1
        return remote(src, dst, s1.at[at], r1.at[at], minor_at[kind](direction))

    def second(kind, direction, step, pack):
        lane = 0 if direction == 1 else 1
        lo, hi = PACKS[pack]
        into = origin(direction, step)
        if step == 1 and pack == 0:
            src, dst = w_ref.at[PIECE * kind : PIECE * (kind + 1)], w_all.at[kind, into, OWN]
        else:
            came = OWN if step == 1 else origin(direction, step - 1)
            src = w_all.at[kind, came, pl.ds(lo, hi - lo)]
            dst = w_all.at[kind, into, pl.ds(lo, hi - lo)]
        at = kind, lane, step - 1, pack
        return remote(src, dst, s2.at[at], r2.at[at], major_at[kind](direction))

    def lanes_of(step, pack):
        if step < 4:
            return (1, -1)
        return (1,) if pack in FAR_UP else (-1,)

    def first_arrives(step):
        for kind in range(2):
            for direction in (1, -1):
                first(kind, direction, step).wait_recv()
                if step < 4:
                    go(first(kind, direction, step + 1))
        for kind in range(2):
            for direction in (1, -1):
                go(second(kind, direction, 1, step))

    def second_arrives(step, pack):
        for kind in range(2):
            for direction in lanes_of(step, pack):
                second(kind, direction, step, pack).wait_recv()
                if step < 4 and direction in lanes_of(step + 1, pack):
                    go(second(kind, direction, step + 1, pack))

    events = [(2.2 * k, first_arrives, (k,)) for k in range(1, 5)]
    events += [
        (2.6 + 10.5 * (k - 1) + 2.4 * g, second_arrives, (k, g)) for k in range(1, 5) for g in range(5)
    ]
    events.sort(key=lambda e: e[0])
    events = [(at, fn, args) for at, fn, args in events]
    clock = [0.0]
    seen = set()

    def take_event():
        at, fn, args = events.pop(0)
        fn(*args)
        if fn is second_arrives:
            seen.add(args)
        else:
            seen.add(args[0])
        clock[0] = max(clock[0], at)

    def work(cost, fn, *args):
        while events and events[0][0] <= clock[0]:
            take_event()
        fn(*args)
        clock[0] += cost

    def need(step):
        wanted = {(step, g) for g in range(5)}
        while not wanted <= seen:
            take_event()

    halo_copy = remote(
        qkv_ref.at[:, ROWS - HALO : ROWS], halo, halo_sem.at[0], halo_sem.at[1], seq_at(1)
    )
    go(halo_copy)
    for kind in range(2):
        for direction in (1, -1):
            go(first(kind, direction, 1))
    for kind in range(2):
        for direction in (1, -1):
            go(second(kind, direction, 1, 0))

    def widen(strip):
        at = pl.ds(pl.multiple_of(strip * LANES, LANES), LANES)
        for i in range(3):
            ext[i, strip, PAD:, :] = qkv_v[i, :, at].astype(F32)

    def widen_halo(strip):
        at = pl.ds(pl.multiple_of(strip * LANES, LANES), LANES)
        for i in range(3):
            before = halo[i, :, at].astype(F32)[HALO - PAD :]
            ext[i, strip, :PAD, :] = jnp.where(s == 0, 0.0, before)

    def feature(i, block, strip, at):
        total = None
        for j in range(FTAPS):
            term = taps_ref[i, j : j + 1, at] * ext[i, strip, pl.ds(PAD + SPAN * block - j, SPAN), :]
            total = term if total is None else total + term
        return total

    def features(block, strips):
        def body(strip, carry):
            at = pl.ds(pl.multiple_of(strip * LANES, LANES), LANES)
            u = (feature(1, block, strip, at) * feature(2, block, strip, at)).astype(BF16).astype(F32)
            ut[block + 1, at, :] = u.T.astype(BF16)
            qt[block, at, :] = feature(0, block, strip, at).T
            return carry

        lax.fori_loop(strips[0], strips[1], body, 0)

    def widen_all():
        for copy in loads:
            copy.wait()

        def body(strip, carry):
            widen(strip)
            return carry

        lax.fori_loop(0, STRIPS, body, 0)
        hf[...] = filt_ref[...].astype(F32)

    def halo_arrives():
        halo_copy.wait_recv()

        def body(strip, carry):
            widen_halo(strip)
            at = pl.ds(pl.multiple_of(strip * LANES, LANES), LANES)
            skt[at, :] = jnp.broadcast_to(skip_ref[:, at], (LANES, LANES)).T
            return carry

        lax.fori_loop(0, STRIPS, body, 0)

    tail_copy = remote(ut.at[BLOCKS], ut.at[0], tail_sem.at[0], tail_sem.at[1], seq_at(1))

    def send_tail():
        go(tail_copy)

    def tail_arrives():
        tail_copy.wait_recv()

        @pl.when(s == 0)
        def clear():
            ut[0] = jnp.zeros((WIDTH, SPAN), BF16)

    def conv(lo, hi):
        def body(g, carry):
            row = lax.broadcasted_iota(jnp.int32, (SPAN, SPAN), 0)
            col = lax.broadcasted_iota(jnp.int32, (SPAN, SPAN), 1)
            taps = jnp.broadcast_to(hf[pl.ds(g, 1), :], (SPAN, SPAN))
            ring = pltpu.roll(taps, 0, 1, stride=1, stride_axis=0)
            here = jnp.where(row <= col, ring, 0.0)
            before = jnp.where(row > col, ring, 0.0)
            matrix = jnp.concatenate([before, here], axis=0).astype(BF16)
            at = pl.ds(pl.multiple_of(g * GROUP, GROUP), GROUP)
            parts = [ut[b, at, :] for b in range(BLOCKS + 1)]
            window = jnp.concatenate(
                [jnp.concatenate(parts[:BLOCKS], axis=0), jnp.concatenate(parts[1:], axis=0)], axis=1
            )
            mixed = jnp.dot(window, matrix, preferred_element_type=F32)
            for b in range(BLOCKS):
                field = mixed[GROUP * b : GROUP * (b + 1)] + skt[at, :] * parts[b + 1].astype(F32)
                yt[at, SPAN * b : SPAN * (b + 1)] = (qt[b, at, :] * field).astype(BF16)
            return carry

        lax.fori_loop(lo, hi, body, 0, unroll=4)

    def project(pieces):
        rows = jnp.concatenate(pieces, axis=0) if len(pieces) > 1 else pieces[0]
        return jnp.dot(rows, yt[...], preferred_element_type=F32)

    def two(kind, major, batch, half):
        return w_all[kind, major, pl.ds(4 * batch + 2 * half, 2)].reshape(2 * PIECE, WIDTH)

    def four(kind, major, half):
        return [two(kind, major, batch, half) for batch in range(2)]

    def target(slot):
        return lax.rem(y + OFF[slot] + RING, RING)

    delivered = []

    def deliver(src, dst, send, recv, to):
        copy = remote(src, dst, send, recv, {"chan": to})

        @pl.when(to == c)
        def keep():
            pltpu.make_async_copy(src, dst, recv).start()

        @pl.when(to != c)
        def post():
            copy.start()

        delivered.append((to, copy))

    def a_swap(slot):
        return remote(ta.at[slot], sa.at[slot], as1.at[slot], ar1.at[slot], sibling)

    def a_first(slots):
        got = project(sum([four(0, m, 1 - p) for m in slots], [])).astype(BF16)
        for i, m in enumerate(slots):
            ta[m] = got[4 * PIECE * i : 4 * PIECE * (i + 1)]
            go(a_swap(m))

    def a_second(slots):
        got = project(sum([four(0, m, p) for m in slots], []))
        for i, m in enumerate(slots):
            a_swap(m).wait_recv()
            qa[m] = (got[4 * PIECE * i : 4 * PIECE * (i + 1)] + sa[m].astype(F32)).astype(BF16)
            deliver(qa.at[m], ra.at[x, p], as2.at[m, 0], ar2.at[x, p], target(m))

    def b_swap(turn):
        return remote(tb.at[turn], sb.at[turn], bs1.at[turn], br1.at[turn], sibling)

    def b_rows(turn, half):
        return w_all[1, 2 * turn + half].reshape(RING * PIECE, WIDTH)

    def b_first(turn):
        tb[turn] = project([b_rows(turn, 1 - p)]).astype(BF16)
        go(b_swap(turn))

    def b_second(turn):
        got = project([b_rows(turn, p)])
        b_swap(turn).wait_recv()
        qb[turn] = (got + sb[turn].astype(F32)).astype(BF16)
        for m in range(RING):
            deliver(
                qb.at[turn, PIECE * m : PIECE * (m + 1)], rb.at[turn, x, p],
                bs2.at[turn, m], br2.at[turn, x, p], target(m),
            )

    def o_swap(part):
        at = pl.ds(4 * PIECE * part, 4 * PIECE)
        return remote(tc.at[at], sc.at[at], cs1.at[part], cr1.at[part], sibling)

    def o_post(single, batch, at):
        for i in range(2):
            to = lax.rem(y + jnp.where(p == 0, OFF[4 * batch + i], OFF[4 * batch + 2 + i]) + RING, RING)
            deliver(
                qc.at[pl.ds(at + PIECE * i, PIECE)], rc.at[single, x],
                cs2.at[single, batch, i], cr2.at[single, x], to,
            )

    def o_first():
        tc[: 4 * PIECE] = project(four(1, OWN, 1 - p)).astype(BF16)
        go(o_swap(0))

    def o_second():
        got = project(four(1, OWN, p))
        o_swap(0).wait_recv()
        qc[: 4 * PIECE] = (got + sc[: 4 * PIECE].astype(F32)).astype(BF16)
        for batch in range(2):
            o_post(0, batch, 2 * PIECE * batch)

    def far_first(batch):
        at = pl.ds(4 * PIECE * (batch + 1), 4 * PIECE)
        tc[at] = project([two(0, FAR, batch, 1 - p), two(1, FAR, batch, 1 - p)]).astype(BF16)
        go(o_swap(batch + 1))

    def far_second(batch):
        base = 4 * PIECE * (batch + 1)
        got = project([two(0, FAR, batch, p), two(1, FAR, batch, p)])
        o_swap(batch + 1).wait_recv()
        qc[base : base + 4 * PIECE] = (got + sc[base : base + 4 * PIECE].astype(F32)).astype(BF16)
        deliver(
            qc.at[base : base + 2 * PIECE], ra.at[x, p, pl.ds(2 * PIECE * batch, 2 * PIECE)],
            as2.at[FAR, batch], ar2.at[x, p], target(FAR),
        )
        o_post(1, batch, base + 2 * PIECE)

    def own_wait():
        for copy in own:
            copy.wait()

    work(1.0, widen_all)
    for lo in (0, 4):
        work(1.4, features, BLOCKS - 1, (lo, lo + 4))
    work(0.1, send_tail)
    for lo in (0, 4):
        work(1.4, features, 1, (lo, lo + 4))
    work(0.3, halo_arrives)
    for lo in (0, 4):
        work(1.4, features, 0, (lo, lo + 4))
    work(0.1, tail_arrives)
    for lo in range(0, 64, 16):
        work(1.5, conv, lo, lo + 16)
    work(0.1, own_wait)
    work(0.6, a_first, (OWN,))
    work(0.6, o_first)
    work(0.6, a_second, (OWN,))
    work(0.6, o_second)
    for k in (1, 2, 3):
        low, high = SLOT[k], SLOT[-k]
        need(k)
        work(1.0, a_first, (low, high))
        work(1.0, b_first, k - 1)
        work(1.0, a_second, (low, high))
        work(1.2, b_second, k - 1)
    while not {(4, g) for g in (0, 1, 2)} <= seen:
        take_event()
    far_first(0)
    far_second(0)
    need(4)
    far_first(1)
    far_second(1)

    def place(kind, slot, rows):
        at = lax.rem(z + OFF[slot] + RING, RING) * (2 * PIECE) + kind * PIECE
        fin[pl.ds(pl.multiple_of(at, PIECE), PIECE), :] = rows

    def total(refs):
        found = None
        for ref in refs:
            term = ref[...].astype(F32)
            found = term if found is None else found + term
        return found

    def arrived(ref, sem):
        remote(ref, ref, cs2.at[0, 0, 0], sem, sibling).wait_recv()

    for turn in range(PAIRS):
        for half in range(2):
            for chip in range(4):
                arrived(rb.at[turn, chip, half], br2.at[turn, chip, half])
            place(1, 2 * turn + half, total([rb.at[turn, chip, half] for chip in range(4)]))
    for single, slot in ((0, OWN), (1, FAR)):
        for chip in range(4):
            arrived(rc.at[single, chip], cr2.at[single, chip])
        place(1, slot, total([rc.at[single, chip] for chip in range(4)]))
    for half in range(2):
        for chip in range(4):
            arrived(ra.at[chip, half], ar2.at[chip, half])
        found = total([ra.at[chip, half] for chip in range(4)])
        for i in range(4):
            slot = 4 * (i // 2) + 2 * half + i % 2
            place(0, slot, found[PIECE * i : PIECE * (i + 1)])
    for a in range(BLOCKS):
        for n in range(4):
            tile = fin[LANES * n : LANES * (n + 1), SPAN * a : SPAN * (a + 1)]
            out_ref[SPAN * a : SPAN * (a + 1), LANES * n : LANES * (n + 1)] = tile.T.astype(BF16)

    for copy in started:
        copy.wait_send()
    for to, copy in delivered:
        @pl.when(to != c)
        def drain(copy=copy):
            copy.wait_send()


def local(qkv, feat_taps, long_filter, skip_gain, out_weight):
    vmem = pl.BlockSpec(memory_space=pltpu.VMEM)
    anywhere = pl.BlockSpec(memory_space=pl.ANY)
    dma = pltpu.SemaphoreType.DMA
    half_piece = (4 * PIECE, ROWS)
    return pl.pallas_call(
        kernel,
        out_shape=jax.ShapeDtypeStruct((ROWS, 512), BF16),
        in_specs=[anywhere] * 5,
        out_specs=vmem,
        scratch_shapes=[
            pltpu.VMEM((3, FTAPS, WIDTH), F32),
            pltpu.VMEM((WIDTH // GROUP, SPAN), BF16),
            pltpu.VMEM((1, WIDTH), F32),
            pltpu.VMEM((2, RING, RING, PIECE, WIDTH), BF16),
            pltpu.VMEM((3, ROWS, WIDTH), BF16),
            pltpu.VMEM((3, HALO, WIDTH), BF16),
            pltpu.VMEM((3, STRIPS, PAD + ROWS, LANES), F32),
            pltpu.VMEM((BLOCKS + 1, WIDTH, SPAN), BF16),
            pltpu.VMEM((BLOCKS, WIDTH, SPAN), F32),
            pltpu.VMEM((WIDTH, SPAN), F32),
            pltpu.VMEM((WIDTH // GROUP, SPAN), F32),
            pltpu.VMEM((WIDTH, ROWS), BF16),
            pltpu.VMEM((RING,) + half_piece, BF16),
            pltpu.VMEM((RING,) + half_piece, BF16),
            pltpu.VMEM((RING,) + half_piece, BF16),
            pltpu.VMEM((PAIRS, RING * PIECE, ROWS), BF16),
            pltpu.VMEM((PAIRS, RING * PIECE, ROWS), BF16),
            pltpu.VMEM((PAIRS, RING * PIECE, ROWS), BF16),
            pltpu.VMEM((12 * PIECE, ROWS), BF16),
            pltpu.VMEM((12 * PIECE, ROWS), BF16),
            pltpu.VMEM((12 * PIECE, ROWS), BF16),
            pltpu.VMEM((4, 2) + half_piece, BF16),
            pltpu.VMEM((PAIRS, 4, 2, PIECE, ROWS), BF16),
            pltpu.VMEM((2, 4, PIECE, ROWS), BF16),
            pltpu.VMEM((512, ROWS), F32),
            dma((6,)), dma((2,)), dma((2,)), dma((2,)),
            dma((2, 2, 4)), dma((2, 2, 4)),
            dma((2, 2, 4, 5)), dma((2, 2, 4, 5)),
            dma((RING,)), dma((RING,)), dma((RING, 2)), dma((4, 2)),
            dma((PAIRS,)), dma((PAIRS,)), dma((PAIRS, RING)), dma((PAIRS, 4, 2)),
            dma((3,)), dma((3,)), dma((2, 2, 2)), dma((2, 4)),
        ],
        compiler_params=pltpu.CompilerParams(
            collective_id=0, has_side_effects=True, vmem_limit_bytes=56 * 2**20
        ),
    )(qkv, feat_taps, long_filter.T, skip_gain.reshape(1, WIDTH), out_weight.T)


def solution(mesh):
    return jax.shard_map(
        local,
        mesh=mesh,
        in_specs=(
            P(None, "seq", "chan"),
            P(None, None, "chan"),
            P(None, "chan"),
            P("chan"),
            P("chan", "seq"),
        ),
        out_specs=P("seq", "chan"),
        check_vma=False,
    )
```

```python
import jax
import jax.numpy as jnp
from jax import lax
from jax.experimental import pallas as pl
from jax.experimental.pallas import tpu as pltpu
from jax.sharding import PartitionSpec as P

MESH = pl.DeviceIdType.MESH
F32 = jnp.float32
BF16 = jnp.bfloat16

RING = 8
GROUP = 16
SPAN = 128
FTAPS = 7
ROWS = 384
WIDTH = 1024
BLOCKS = ROWS // SPAN
LANES = 128
STRIPS = WIDTH // LANES
PIECE = 32
HALO = 16
PAD = 8

OFF = (1, -1, 2, -2, 3, -3, 4, 0)
SLOT = {off: slot for slot, off in enumerate(OFF)}
OWN = SLOT[0]
GROUPS = ((7,), (0, 1), (2, 3), (4, 5), (6,))
NEAR, CROSS, NEAR_EXT, CROSS_EXT = (pl.ds(2 * PIECE * i, 2 * PIECE) for i in range(4))
PARTS = (NEAR, pl.ds(4 * PIECE, PIECE), CROSS, pl.ds(6 * PIECE, PIECE))
HALF = 4 * PIECE


def origin(direction, step):
    return SLOT[4 if step == 4 else -direction * step]


def kernel(
    qkv_ref, taps_hbm, filt_hbm, skip_hbm, w_ref, out_ref,
    taps_ref, filt_ref, skip_ref,
    w_all, qkv_v, halo, ext_v, ut, qt, skt, hf, yt, yp,
    ta, sa, qa, ra, qp, rp, fin,
    load_sem, own_sem, halo_sem, tail_sem,
    xs, es, er, s2, r2, ys, yr, as1, ar1, as2, ar2, ps,
):
    s = lax.axis_index("seq")
    c = lax.axis_index("chan")
    y = lax.div(s, RING)
    z = lax.rem(s, RING)
    x = lax.div(c, 2)
    p = lax.rem(c, 2)

    def y_at(d):
        return {"seq": lax.rem(y + d + RING, RING) * RING + z}

    def z_at(d):
        return {"seq": y * RING + lax.rem(z + d + 2 * RING, RING)}

    def seq_at(d):
        return {"seq": lax.rem(s + d + RING * RING, RING * RING)}

    sibling = {"chan": c + 1 - 2 * p}
    outer = 2 * lax.rem(z, 2) - 1
    inner = -outer
    started = []

    def remote(src, dst, send, recv, to):
        return pltpu.make_async_remote_copy(
            src_ref=src, dst_ref=dst, send_sem=send, recv_sem=recv, device_id=to, device_id_type=MESH
        )

    def go(copy):
        copy.start()
        started.append(copy)

    loads = [
        pltpu.make_async_copy(qkv_ref.at[i], qkv_v.at[i], load_sem.at[i]) for i in (1, 2, 0)
    ]
    loads += [
        pltpu.make_async_copy(taps_hbm, taps_ref, load_sem.at[3]),
        pltpu.make_async_copy(filt_hbm, filt_ref, load_sem.at[4]),
        pltpu.make_async_copy(skip_hbm, skip_ref, load_sem.at[5]),
    ]
    own = pltpu.make_async_copy(w_ref, w_all.at[OWN, NEAR], own_sem)
    for copy in loads + [own]:
        copy.start()

    barrier = pltpu.get_barrier_semaphore()
    greeted = [{"chan": lax.rem(c + d, 8)} for d in range(1, 8)]
    greeted += [z_at(outer), z_at(inner), z_at(3 * inner), y_at(1), y_at(-1), seq_at(1), seq_at(-1)]
    for to in greeted:
        pl.semaphore_signal(barrier, inc=1, device_id=to, device_id_type=MESH)
    pl.semaphore_wait(barrier, len(greeted))

    def cross():
        return remote(w_ref, w_all.at[OWN, CROSS], xs.at[0], xs.at[1], z_at(3 * inner))

    def ext(which, slot):
        src, dst = ((NEAR, NEAR_EXT), (CROSS, CROSS_EXT))[which]
        if slot != OWN:
            src, dst = [pl.ds(at.start + PIECE, PIECE) for at in (src, dst)]
        found = w_ref if slot == OWN and which == 0 else w_all.at[slot, src]
        return remote(found, w_all.at[slot, dst], es.at[which, slot], er.at[which, slot], z_at(outer))

    def ring(direction, step, part):
        lane = 0 if direction == 1 else 1
        rows = PARTS[part]
        into = origin(direction, step)
        came = OWN if step == 1 else origin(direction, step - 1)
        src = w_ref if step == 1 and part == 0 else w_all.at[came, rows]
        at = lane, step - 1, part
        return remote(src, w_all.at[into, rows], s2.at[at], r2.at[at], y_at(direction))

    def lanes_of(step, part):
        if step < 4:
            return (1, -1)
        return (1,) if part < 2 else (-1,)

    def start_part(part):
        for direction in (1, -1):
            go(ring(direction, 1, part))

    def near_arrives():
        ext(0, OWN).wait_recv()
        start_part(1)

    def cross_arrives():
        cross().wait_recv()
        start_part(2)
        go(ext(1, OWN))

    def cross_ext_arrives():
        ext(1, OWN).wait_recv()
        start_part(3)

    def part_arrives(step, part):
        for direction in lanes_of(step, part):
            ring(direction, step, part).wait_recv()
            if step < 4 and direction in lanes_of(step + 1, part):
                go(ring(direction, step + 1, part))
            if part in (0, 2):
                go(ext(part // 2, origin(direction, step)))

    reach = (2.0, 3.4, 5.0, 6.4)
    events = [(2.2, near_arrives, ()), (3.6, cross_arrives, ()), (5.6, cross_ext_arrives, ())]
    events += [
        (2.0 + 8.5 * (k - 1) + reach[part], part_arrives, (k, part)) for k in range(1, 5) for part in range(4)
    ]
    events.sort(key=lambda e: e[0])
    clock = [0.0]
    seen = set()

    def take_event():
        at, fn, args = events.pop(0)
        fn(*args)
        seen.add(args)
        clock[0] = max(clock[0], at)

    def work(cost, fn, *args):
        while events and events[0][0] <= clock[0]:
            take_event()
        fn(*args)
        clock[0] += cost

    def need(step):
        wanted = {(step, part) for part in range(4)}
        while not wanted <= seen:
            take_event()
        for slot in GROUPS[step]:
            for which in range(2):
                ext(which, slot).wait_recv()

    halo_copy = remote(
        qkv_ref.at[:, ROWS - HALO : ROWS], halo, halo_sem.at[0], halo_sem.at[1], seq_at(1)
    )
    go(cross())
    go(ext(0, OWN))
    start_part(0)
    go(halo_copy)

    def widen(strip):
        at = pl.ds(pl.multiple_of(strip * LANES, LANES), LANES)
        for i in range(3):
            ext_v[i, strip, PAD:, :] = qkv_v[i, :, at].astype(F32)

    def widen_halo(strip):
        at = pl.ds(pl.multiple_of(strip * LANES, LANES), LANES)
        for i in range(3):
            before = halo[i, :, at].astype(F32)[HALO - PAD :]
            ext_v[i, strip, :PAD, :] = jnp.where(s == 0, 0.0, before)

    def feature(i, block, strip, at):
        total = None
        for j in range(FTAPS):
            term = taps_ref[i, j : j + 1, at] * ext_v[i, strip, pl.ds(PAD + SPAN * block - j, SPAN), :]
            total = term if total is None else total + term
        return total

    def features(block, strips):
        def body(strip, carry):
            at = pl.ds(pl.multiple_of(strip * LANES, LANES), LANES)
            u = (feature(1, block, strip, at) * feature(2, block, strip, at)).astype(BF16).astype(F32)
            ut[block + 1, at, :] = u.T.astype(BF16)
            qt[block, at, :] = feature(0, block, strip, at).T
            return carry

        lax.fori_loop(strips[0], strips[1], body, 0)

    def widen_all():
        for copy in loads:
            copy.wait()

        def body(strip, carry):
            widen(strip)
            return carry

        lax.fori_loop(0, STRIPS, body, 0)
        hf[...] = filt_ref[...].astype(F32)

    def halo_arrives():
        halo_copy.wait_recv()

        def body(strip, carry):
            widen_halo(strip)
            at = pl.ds(pl.multiple_of(strip * LANES, LANES), LANES)
            skt[at, :] = jnp.broadcast_to(skip_ref[:, at], (LANES, LANES)).T
            return carry

        lax.fori_loop(0, STRIPS, body, 0)

    tail_copy = remote(ut.at[BLOCKS], ut.at[0], tail_sem.at[0], tail_sem.at[1], seq_at(1))

    def send_tail():
        go(tail_copy)

    def tail_arrives():
        tail_copy.wait_recv()

        @pl.when(s == 0)
        def clear():
            ut[0] = jnp.zeros((WIDTH, SPAN), BF16)

    def conv(lo, hi):
        def body(g, carry):
            row = lax.broadcasted_iota(jnp.int32, (SPAN, SPAN), 0)
            col = lax.broadcasted_iota(jnp.int32, (SPAN, SPAN), 1)
            taps = jnp.broadcast_to(hf[pl.ds(g, 1), :], (SPAN, SPAN))
            ring = pltpu.roll(taps, 0, 1, stride=1, stride_axis=0)
            here = jnp.where(row <= col, ring, 0.0)
            before = jnp.where(row > col, ring, 0.0)
            matrix = jnp.concatenate([before, here], axis=0).astype(BF16)
            at = pl.ds(pl.multiple_of(g * GROUP, GROUP), GROUP)
            parts = [ut[b, at, :] for b in range(BLOCKS + 1)]
            window = jnp.concatenate(
                [jnp.concatenate(parts[:BLOCKS], axis=0), jnp.concatenate(parts[1:], axis=0)], axis=1
            )
            mixed = jnp.dot(window, matrix, preferred_element_type=F32)
            for b in range(BLOCKS):
                field = mixed[GROUP * b : GROUP * (b + 1)] + skt[at, :] * parts[b + 1].astype(F32)
                yt[at, SPAN * b : SPAN * (b + 1)] = (qt[b, at, :] * field).astype(BF16)
            return carry

        lax.fori_loop(lo, hi, body, 0, unroll=4)

    def swap_y(quarter):
        at = pl.ds(quarter * (WIDTH // 4), WIDTH // 4)
        return remote(yt.at[at], yp.at[at], ys.at[quarter], yr.at[quarter], z_at(inner))

    def send_y(quarter):
        go(swap_y(quarter))

    def project(slots, half, tokens):
        rows = [w_all[m, pl.ds(pl.multiple_of(half * HALF, HALF), HALF)] for m in slots]
        rows = jnp.concatenate(rows, axis=0) if len(rows) > 1 else rows[0]
        return jnp.dot(rows, (yt, yp)[tokens][...], preferred_element_type=F32)

    def swap(group, tokens):
        low = GROUPS[group][0]
        at = pl.ds(low * HALF, len(GROUPS[group]) * HALF)
        return remote(
            ta.at[tokens, at], sa.at[tokens, at],
            as1.at[tokens, group], ar1.at[tokens, group], sibling,
        )

    def give(group, tokens):
        low, many = GROUPS[group][0], len(GROUPS[group])
        ta[tokens, low * HALF : (low + many) * HALF] = project(GROUPS[group], 1 - p, tokens).astype(BF16)
        go(swap(group, tokens))

    delivered = []

    def deliver(src, dst, send, recv, to):
        copy = remote(src, dst, send, recv, {"chan": to})

        @pl.when(to == c)
        def keep():
            pltpu.make_async_copy(src, dst, recv).start()

        @pl.when(to != c)
        def post():
            copy.start()

        delivered.append((to, copy))

    def take(group, tokens):
        low, many = GROUPS[group][0], len(GROUPS[group])
        at = slice(low * HALF, (low + many) * HALF)
        got = project(GROUPS[group], p, tokens)
        swap(group, tokens).wait_recv()
        qa[tokens, at] = (got + sa[tokens, at].astype(F32)).astype(BF16)
        for m in GROUPS[group]:
            deliver(
                qa.at[tokens, m * HALF : (m + 1) * HALF], ra.at[tokens, x, p],
                as2.at[tokens, m], ar2.at[tokens, x, p], lax.rem(y + OFF[m] + RING, RING),
            )

    def gathered(tokens, half):
        found = None
        for chip in range(4):
            here = ra.at[tokens, chip, half]
            remote(here, here, as2.at[tokens, 0], ar2.at[tokens, chip, half], sibling).wait_recv()
        for chip in range(4):
            term = ra[tokens, chip, half].astype(F32)
            found = term if found is None else found + term
        return found

    hand = remote(qp, rp, ps.at[0], ps.at[1], z_at(inner))
    ahead = lax.rem(c - y + RING, RING)
    my_group = jnp.minimum(ahead, RING - ahead)

    def finish(group):
        @pl.when(my_group == group)
        def partner_sum():
            for half in range(2):
                qp[half * HALF : (half + 1) * HALF] = gathered(1, half).astype(BF16)
            hand.start()

    def own_wait():
        own.wait()

    work(1.0, widen_all)
    for lo in (0, 4):
        work(1.4, features, BLOCKS - 1, (lo, lo + 4))
    work(0.1, send_tail)
    for lo in (0, 4):
        work(1.4, features, 1, (lo, lo + 4))
    work(0.3, halo_arrives)
    for lo in (0, 4):
        work(1.4, features, 0, (lo, lo + 4))
    work(0.1, tail_arrives)
    for quarter in range(4):
        work(1.5, conv, 16 * quarter, 16 * quarter + 16)
        work(0.1, send_y, quarter)
    work(0.1, own_wait)
    work(0.6, give, 0, 0)
    need(1)
    work(1.0, give, 1, 0)
    work(0.6, take, 0, 0)
    work(1.0, take, 1, 0)
    need(2)
    work(1.0, give, 2, 0)
    work(1.0, take, 2, 0)
    for quarter in range(4):
        swap_y(quarter).wait_recv()
    work(0.6, give, 0, 1)
    work(1.0, give, 1, 1)
    work(0.6, take, 0, 1)
    work(1.0, take, 1, 1)
    work(1.0, give, 2, 1)
    work(1.0, take, 2, 1)
    need(3)
    work(1.0, give, 3, 1)
    work(1.0, give, 3, 0)
    work(0.1, finish, 0)
    work(0.1, finish, 1)
    work(1.0, take, 3, 1)
    work(1.0, take, 3, 0)
    need(4)
    give(4, 1)
    give(4, 0)
    finish(2)
    take(4, 1)
    take(4, 0)
    finish(3)
    finish(4)

    def place(z_from, rows):
        at = lax.rem(z + z_from + 2 * RING, RING) * (2 * PIECE)
        fin[pl.ds(pl.multiple_of(at, 2 * PIECE), 2 * PIECE), :] = rows

    for half in range(2):
        found = gathered(0, half)
        for i, z_from in enumerate(((0, outer + 4), (outer, 4))[half]):
            place(z_from, found[2 * PIECE * i : 2 * PIECE * (i + 1)])
    hand.wait_recv()
    for i, z_from in enumerate((inner, 2 * inner + 4, 2 * inner, inner + 4)):
        place(z_from, rp[2 * PIECE * i : 2 * PIECE * (i + 1)].astype(F32))
    for a in range(BLOCKS):
        for n in range(4):
            tile = fin[LANES * n : LANES * (n + 1), SPAN * a : SPAN * (a + 1)]
            out_ref[SPAN * a : SPAN * (a + 1), LANES * n : LANES * (n + 1)] = tile.T.astype(BF16)

    for copy in started:
        copy.wait_send()
    hand.wait_send()
    for to, copy in delivered:
        @pl.when(to != c)
        def drain(copy=copy):
            copy.wait_send()


def local(qkv, feat_taps, long_filter, skip_gain, out_weight):
    vmem = pl.BlockSpec(memory_space=pltpu.VMEM)
    anywhere = pl.BlockSpec(memory_space=pl.ANY)
    dma = pltpu.SemaphoreType.DMA
    return pl.pallas_call(
        kernel,
        out_shape=jax.ShapeDtypeStruct((ROWS, 512), BF16),
        in_specs=[anywhere] * 5,
        out_specs=vmem,
        scratch_shapes=[
            pltpu.VMEM((3, FTAPS, WIDTH), F32),
            pltpu.VMEM((WIDTH // GROUP, SPAN), BF16),
            pltpu.VMEM((1, WIDTH), F32),
            pltpu.VMEM((RING, 8 * PIECE, WIDTH), BF16),
            pltpu.VMEM((3, ROWS, WIDTH), BF16),
            pltpu.VMEM((3, HALO, WIDTH), BF16),
            pltpu.VMEM((3, STRIPS, PAD + ROWS, LANES), F32),
            pltpu.VMEM((BLOCKS + 1, WIDTH, SPAN), BF16),
            pltpu.VMEM((BLOCKS, WIDTH, SPAN), F32),
            pltpu.VMEM((WIDTH, SPAN), F32),
            pltpu.VMEM((WIDTH // GROUP, SPAN), F32),
            pltpu.VMEM((WIDTH, ROWS), BF16),
            pltpu.VMEM((WIDTH, ROWS), BF16),
            pltpu.VMEM((2, RING * HALF, ROWS), BF16),
            pltpu.VMEM((2, RING * HALF, ROWS), BF16),
            pltpu.VMEM((2, RING * HALF, ROWS), BF16),
            pltpu.VMEM((2, 4, 2, HALF, ROWS), BF16),
            pltpu.VMEM((2 * HALF, ROWS), BF16),
            pltpu.VMEM((2 * HALF, ROWS), BF16),
            pltpu.VMEM((512, ROWS), F32),
            dma((6,)), dma, dma((2,)), dma((2,)),
            dma((2,)), dma((2, RING)), dma((2, RING)),
            dma((2, 4, 4)), dma((2, 4, 4)), dma((4,)), dma((4,)),
            dma((2, 5)), dma((2, 5)), dma((2, RING)), dma((2, 4, 2)), dma((2,)),
        ],
        compiler_params=pltpu.CompilerParams(
            collective_id=0, has_side_effects=True, vmem_limit_bytes=56 * 2**20
        ),
    )(qkv, feat_taps, long_filter.T, skip_gain.reshape(1, WIDTH), out_weight.T)


def solution(mesh):
    return jax.shard_map(
        local,
        mesh=mesh,
        in_specs=(
            P(None, "seq", "chan"),
            P(None, None, "chan"),
            P(None, "chan"),
            P("chan"),
            P("chan", "seq"),
        ),
        out_specs=P("seq", "chan"),
        check_vma=False,
    )
```

```python
import jax
import jax.numpy as jnp
from jax import lax
from jax.experimental import pallas as pl
from jax.experimental.pallas import tpu as pltpu
from jax.sharding import PartitionSpec as P

MESH = pl.DeviceIdType.MESH
F32 = jnp.float32
BF16 = jnp.bfloat16

RING = 8
GROUP = 16
SPAN = 128
FTAPS = 7
ROWS = 384
WIDTH = 1024
BLOCKS = ROWS // SPAN
LANES = 128
STRIPS = WIDTH // LANES
PIECE = 32
HALO = 16
PAD = 8
PITCH = 49
SUBS = 8
TALL = PITCH * SUBS

OFF = (1, -1, 2, -2, 3, -3, 4, 0)
SLOT = {off: slot for slot, off in enumerate(OFF)}
OWN = SLOT[0]
GROUPS = ((7,), (0, 1), (2, 3), (4, 5), (6,))
NEAR, CROSS, NEAR_EXT, CROSS_EXT = (pl.ds(2 * PIECE * i, 2 * PIECE) for i in range(4))
PARTS = (NEAR, pl.ds(4 * PIECE, PIECE), CROSS, pl.ds(6 * PIECE, PIECE))
HALF = 4 * PIECE
BATCH = 8


def origin(direction, step):
    return SLOT[4 if step == 4 else -direction * step]


def kernel(
    qkv_ref, taps_hbm, filt_hbm, skip_hbm, w_ref, out_ref,
    taps_ref, filt_ref, skip_ref,
    w_all, qkv_v, halo, ext_v, ub, qb, ut, qt, skt, hf, mats, yt, yp,
    ta, sa, qa, ra, qp, rp, fin,
    load_sem, own_sem, halo_sem, tail_sem,
    xs, es, er, s2, r2, ys, yr, as1, ar1, as2, ar2, ps,
):
    s = lax.axis_index("seq")
    c = lax.axis_index("chan")
    y = lax.div(s, RING)
    z = lax.rem(s, RING)
    x = lax.div(c, 2)
    p = lax.rem(c, 2)

    def y_at(d):
        return {"seq": lax.rem(y + d + RING, RING) * RING + z}

    def z_at(d):
        return {"seq": y * RING + lax.rem(z + d + 2 * RING, RING)}

    def seq_at(d):
        return {"seq": lax.rem(s + d + RING * RING, RING * RING)}

    sibling = {"chan": c + 1 - 2 * p}
    outer = 2 * lax.rem(z, 2) - 1
    inner = -outer
    started = []

    def remote(src, dst, send, recv, to):
        return pltpu.make_async_remote_copy(
            src_ref=src, dst_ref=dst, send_sem=send, recv_sem=recv, device_id=to, device_id_type=MESH
        )

    def go(copy):
        copy.start()
        started.append(copy)

    loads = [
        pltpu.make_async_copy(qkv_ref.at[i], qkv_v.at[i], load_sem.at[i]) for i in (1, 2, 0)
    ]
    loads += [
        pltpu.make_async_copy(taps_hbm, taps_ref, load_sem.at[3]),
        pltpu.make_async_copy(skip_hbm, skip_ref, load_sem.at[5]),
        pltpu.make_async_copy(filt_hbm, filt_ref, load_sem.at[4]),
    ]
    own = pltpu.make_async_copy(w_ref, w_all.at[OWN, NEAR], own_sem)
    for copy in loads[::-1] + [own]:
        copy.start()

    barrier = pltpu.get_barrier_semaphore()
    greeted = [{"chan": lax.rem(c + d, 8)} for d in range(1, 8)]
    greeted += [z_at(outer), z_at(inner), z_at(3 * inner), y_at(1), y_at(-1), seq_at(1), seq_at(-1)]
    for to in greeted:
        pl.semaphore_signal(barrier, inc=1, device_id=to, device_id_type=MESH)

    def toeplitz(low, high):
        def body(step, carry):
            row = lax.broadcasted_iota(jnp.int32, (SPAN, SPAN), 0)
            col = lax.broadcasted_iota(jnp.int32, (SPAN, SPAN), 1)
            for i in range(4):
                g = step * 4 + i
                taps = jnp.broadcast_to(hf[pl.ds(g, 1), :], (SPAN, SPAN))
                turned = pltpu.roll(taps, 0, 1, stride=1, stride_axis=0)
                mats[g, :SPAN] = jnp.where(row > col, turned, 0.0).astype(BF16)
                mats[g, SPAN:] = jnp.where(row <= col, turned, 0.0).astype(BF16)
            return carry

        lax.fori_loop(low // 4, high // 4, body, 0)

    for copy in loads[5:]:
        copy.wait()
    hf[...] = filt_ref[...].astype(F32)
    toeplitz(0, 32)

    pl.semaphore_wait(barrier, len(greeted))

    def cross():
        return remote(w_ref, w_all.at[OWN, CROSS], xs.at[0], xs.at[1], z_at(3 * inner))

    def ext(which, slot):
        src, dst = ((NEAR, NEAR_EXT), (CROSS, CROSS_EXT))[which]
        if slot != OWN:
            src, dst = [pl.ds(at.start + PIECE, PIECE) for at in (src, dst)]
        found = w_ref if slot == OWN and which == 0 else w_all.at[slot, src]
        return remote(found, w_all.at[slot, dst], es.at[which, slot], er.at[which, slot], z_at(outer))

    def ring(direction, step, part):
        lane = 0 if direction == 1 else 1
        rows = PARTS[part]
        into = origin(direction, step)
        came = OWN if step == 1 else origin(direction, step - 1)
        src = w_ref if step == 1 and part == 0 else w_all.at[came, rows]
        at = lane, step - 1, part
        return remote(src, w_all.at[into, rows], s2.at[at], r2.at[at], y_at(direction))

    def lanes_of(step, part):
        if step < 4:
            return (1, -1)
        return (1,) if part < 2 else (-1,)

    def start_part(part):
        for direction in (1, -1):
            go(ring(direction, 1, part))

    def near_arrives():
        ext(0, OWN).wait_recv()
        start_part(1)

    def cross_arrives():
        cross().wait_recv()
        start_part(2)
        go(ext(1, OWN))

    def cross_ext_arrives():
        ext(1, OWN).wait_recv()
        start_part(3)

    def part_arrives(step, part):
        for direction in lanes_of(step, part):
            ring(direction, step, part).wait_recv()
            if step < 4 and direction in lanes_of(step + 1, part):
                go(ring(direction, step + 1, part))
            if part in (0, 2):
                go(ext(part // 2, origin(direction, step)))

    reach = (2.0, 3.4, 5.0, 6.4)
    events = [(2.2, near_arrives, ()), (3.6, cross_arrives, ()), (5.6, cross_ext_arrives, ())]
    events += [
        (2.0 + 8.5 * (k - 1) + reach[part], part_arrives, (k, part)) for k in range(1, 5) for part in range(4)
    ]
    events.sort(key=lambda e: e[0])
    clock = [0.0]
    seen = set()

    def take_event():
        at, fn, args = events.pop(0)
        fn(*args)
        seen.add(args)
        clock[0] = max(clock[0], at)

    def work(cost, fn, *args):
        while events and events[0][0] <= clock[0]:
            take_event()
        fn(*args)
        clock[0] += cost

    def need(step):
        wanted = {(step, part) for part in range(4)}
        while not wanted <= seen:
            take_event()
        for slot in GROUPS[step]:
            for which in range(2):
                ext(which, slot).wait_recv()

    halo_copy = remote(
        qkv_ref.at[:, ROWS - HALO : ROWS], halo, halo_sem.at[0], halo_sem.at[1], seq_at(1)
    )
    go(cross())
    go(ext(0, OWN))
    start_part(0)
    go(halo_copy)

    def widen():
        for copy in loads[:5]:
            copy.wait()

        def body(strip, carry):
            at = pl.ds(pl.multiple_of(strip * LANES, LANES), LANES)
            for i in range(3):
                ext_v[i, strip, PAD : PAD + ROWS, :] = qkv_v[i, :, at].astype(F32)
                ext_v[i, strip, PAD + ROWS :, :] = jnp.zeros((TALL - ROWS, LANES), F32)
            skt[at, :] = jnp.broadcast_to(skip_ref[:, at], (LANES, LANES)).T
            return carry

        lax.fori_loop(0, STRIPS, body, 0)

    def halo_arrives():
        halo_copy.wait_recv()

        def body(strip, carry):
            at = pl.ds(pl.multiple_of(strip * LANES, LANES), LANES)
            for i in range(3):
                before = halo[i, :, at].astype(F32)[HALO - PAD :]
                ext_v[i, strip, :PAD, :] = jnp.where(s == 0, 0.0, before)
            return carry

        lax.fori_loop(0, STRIPS, body, 0)

    def features(low, high):
        def body(strip, carry):
            at = pl.ds(pl.multiple_of(strip * LANES, LANES), LANES)
            taps = [
                [jnp.broadcast_to(taps_ref[i, j : j + 1, at], (SUBS, LANES)) for j in range(FTAPS)]
                for i in range(3)
            ]

            def load(i, r):
                return ext_v[i, strip, pl.ds(PAD + r, SUBS, stride=PITCH), :]

            def line(i, window):
                total = taps[i][0] * window[-1]
                for j in range(1, FTAPS):
                    total = total + taps[i][j] * window[-1 - j]
                return total

            windows = [[load(i, r) for r in range(1 - FTAPS, 0)] for i in (1, 2)]
            for r in range(PITCH):
                found = []
                for i in (1, 2):
                    windows[i - 1] = windows[i - 1][1 - FTAPS :] + [load(i, r)]
                    found.append(line(i, windows[i - 1]))
                ub[strip, pl.ds(r, SUBS, stride=PITCH), :] = found[0] * found[1]
            window = [load(0, r) for r in range(1 - FTAPS, 0)]
            for r in range(PITCH):
                window = window[1 - FTAPS :] + [load(0, r)]
                qb[strip, pl.ds(r, SUBS, stride=PITCH), :] = line(0, window)
            for b in range(BLOCKS):
                ut[b + 1, at, :] = ub[strip, SPAN * b : SPAN * (b + 1), :].T.astype(BF16)
                qt[b, at, :] = qb[strip, SPAN * b : SPAN * (b + 1), :].T
            return carry

        lax.fori_loop(low, high, body, 0)

    def tail(quarter):
        at = pl.ds(quarter * (WIDTH // 4), WIDTH // 4)
        return remote(
            ut.at[BLOCKS, at], ut.at[0, at], tail_sem.at[0, quarter], tail_sem.at[1, quarter], seq_at(1)
        )

    def send_tail(quarter):
        go(tail(quarter))

    def tail_arrives(quarter):
        tail(quarter).wait_recv()

        @pl.when(s == 0)
        def clear():
            ut[0, quarter * (WIDTH // 4) : (quarter + 1) * (WIDTH // 4)] = jnp.zeros((WIDTH // 4, SPAN), BF16)

    def conv(low, high):
        def body(step, carry):
            base = step * BATCH
            spots = [pl.ds(pl.multiple_of((base + i) * GROUP, GROUP), GROUP) for i in range(BATCH)]
            parts = [[ut[b, at, :] for b in range(BLOCKS + 1)] for at in spots]
            mixed = []
            for i in range(BATCH):
                window = jnp.concatenate(
                    [
                        jnp.concatenate(parts[i][:BLOCKS], axis=0),
                        jnp.concatenate(parts[i][1:], axis=0),
                    ],
                    axis=1,
                )
                mixed.append(jnp.dot(window, mats[base + i], preferred_element_type=F32))
            found = []
            for i, at in enumerate(spots):
                for b in range(BLOCKS):
                    field = mixed[i][GROUP * b : GROUP * (b + 1)] + skt[at, :] * parts[i][b + 1].astype(F32)
                    found.append((qt[b, at, :] * field).astype(BF16))
            for i, at in enumerate(spots):
                for b in range(BLOCKS):
                    yt[at, SPAN * b : SPAN * (b + 1)] = found[BLOCKS * i + b]
            return carry

        lax.fori_loop(low // BATCH, high // BATCH, body, 0)

    def swap_y(quarter):
        at = pl.ds(quarter * (WIDTH // 4), WIDTH // 4)
        return remote(yt.at[at], yp.at[at], ys.at[quarter], yr.at[quarter], z_at(inner))

    def send_y(quarter):
        go(swap_y(quarter))

    def project(slots, half, tokens):
        rows = [w_all[m, pl.ds(pl.multiple_of(half * HALF, HALF), HALF)] for m in slots]
        rows = jnp.concatenate(rows, axis=0) if len(rows) > 1 else rows[0]
        return jnp.dot(rows, (yt, yp)[tokens][...], preferred_element_type=F32)

    def swap(group, tokens):
        low = GROUPS[group][0]
        at = pl.ds(low * HALF, len(GROUPS[group]) * HALF)
        return remote(
            ta.at[tokens, at], sa.at[tokens, at],
            as1.at[tokens, group], ar1.at[tokens, group], sibling,
        )

    def give(group, tokens):
        low, many = GROUPS[group][0], len(GROUPS[group])
        ta[tokens, low * HALF : (low + many) * HALF] = project(GROUPS[group], 1 - p, tokens).astype(BF16)
        go(swap(group, tokens))

    delivered = []

    def deliver(src, dst, send, recv, to):
        copy = remote(src, dst, send, recv, {"chan": to})

        @pl.when(to == c)
        def keep():
            pltpu.make_async_copy(src, dst, recv).start()

        @pl.when(to != c)
        def post():
            copy.start()

        delivered.append((to, copy))

    def take(group, tokens):
        low, many = GROUPS[group][0], len(GROUPS[group])
        at = slice(low * HALF, (low + many) * HALF)
        got = project(GROUPS[group], p, tokens)
        swap(group, tokens).wait_recv()
        qa[tokens, at] = (got + sa[tokens, at].astype(F32)).astype(BF16)
        for m in GROUPS[group]:
            deliver(
                qa.at[tokens, m * HALF : (m + 1) * HALF], ra.at[tokens, x, p],
                as2.at[tokens, m], ar2.at[tokens, x, p], lax.rem(y + OFF[m] + RING, RING),
            )

    def gathered(tokens, half):
        found = None
        for chip in range(4):
            here = ra.at[tokens, chip, half]
            remote(here, here, as2.at[tokens, 0], ar2.at[tokens, chip, half], sibling).wait_recv()
        for chip in range(4):
            term = ra[tokens, chip, half].astype(F32)
            found = term if found is None else found + term
        return found

    hand = remote(qp, rp, ps.at[0], ps.at[1], z_at(inner))
    ahead = lax.rem(c - y + RING, RING)
    my_group = jnp.minimum(ahead, RING - ahead)

    def finish(group):
        @pl.when(my_group == group)
        def partner_sum():
            for half in range(2):
                qp[half * HALF : (half + 1) * HALF] = gathered(1, half).astype(BF16)
            hand.start()

    def own_wait():
        own.wait()

    work(0.8, widen)
    work(1.0, toeplitz, 32, 64)
    work(0.2, halo_arrives)
    for quarter in range(4):
        work(0.9, features, 2 * quarter, 2 * quarter + 2)
        work(0.1, send_tail, quarter)
    for quarter in range(4):
        work(0.1, tail_arrives, quarter)
        work(0.8, conv, 16 * quarter, 16 * quarter + 16)
        work(0.1, send_y, quarter)
    work(0.1, own_wait)
    work(0.6, give, 0, 0)
    need(1)
    work(1.0, give, 1, 0)
    work(0.6, take, 0, 0)
    work(1.0, take, 1, 0)
    need(2)
    work(1.0, give, 2, 0)
    work(1.0, take, 2, 0)
    for quarter in range(4):
        swap_y(quarter).wait_recv()
    work(0.6, give, 0, 1)
    work(1.0, give, 1, 1)
    work(0.6, take, 0, 1)
    work(1.0, take, 1, 1)
    work(1.0, give, 2, 1)
    work(1.0, take, 2, 1)
    need(3)
    work(1.0, give, 3, 1)
    work(1.0, give, 3, 0)
    work(0.1, finish, 0)
    work(0.1, finish, 1)
    work(1.0, take, 3, 1)
    work(1.0, take, 3, 0)
    need(4)
    give(4, 1)
    give(4, 0)
    finish(2)
    take(4, 1)
    take(4, 0)
    finish(3)
    finish(4)

    def place(z_from, rows):
        at = lax.rem(z + z_from + 2 * RING, RING) * (2 * PIECE)
        fin[pl.ds(pl.multiple_of(at, 2 * PIECE), 2 * PIECE), :] = rows

    for half in range(2):
        found = gathered(0, half)
        for i, z_from in enumerate(((0, outer + 4), (outer, 4))[half]):
            place(z_from, found[2 * PIECE * i : 2 * PIECE * (i + 1)])
    hand.wait_recv()
    for i, z_from in enumerate((inner, 2 * inner + 4, 2 * inner, inner + 4)):
        place(z_from, rp[2 * PIECE * i : 2 * PIECE * (i + 1)].astype(F32))
    for a in range(BLOCKS):
        for n in range(4):
            tile = fin[LANES * n : LANES * (n + 1), SPAN * a : SPAN * (a + 1)]
            out_ref[SPAN * a : SPAN * (a + 1), LANES * n : LANES * (n + 1)] = tile.T.astype(BF16)

    for copy in started:
        copy.wait_send()
    hand.wait_send()
    for to, copy in delivered:
        @pl.when(to != c)
        def drain(copy=copy):
            copy.wait_send()


def local(qkv, feat_taps, long_filter, skip_gain, out_weight):
    vmem = pl.BlockSpec(memory_space=pltpu.VMEM)
    anywhere = pl.BlockSpec(memory_space=pl.ANY)
    dma = pltpu.SemaphoreType.DMA
    return pl.pallas_call(
        kernel,
        out_shape=jax.ShapeDtypeStruct((ROWS, 512), BF16),
        in_specs=[anywhere] * 5,
        out_specs=vmem,
        scratch_shapes=[
            pltpu.VMEM((3, FTAPS, WIDTH), F32),
            pltpu.VMEM((WIDTH // GROUP, SPAN), BF16),
            pltpu.VMEM((1, WIDTH), F32),
            pltpu.VMEM((RING, 8 * PIECE, WIDTH), BF16),
            pltpu.VMEM((3, ROWS, WIDTH), BF16),
            pltpu.VMEM((3, HALO, WIDTH), BF16),
            pltpu.VMEM((3, STRIPS, PAD + TALL, LANES), F32),
            pltpu.VMEM((STRIPS, TALL, LANES), F32),
            pltpu.VMEM((STRIPS, TALL, LANES), F32),
            pltpu.VMEM((BLOCKS + 1, WIDTH, SPAN), BF16),
            pltpu.VMEM((BLOCKS, WIDTH, SPAN), F32),
            pltpu.VMEM((WIDTH, SPAN), F32),
            pltpu.VMEM((WIDTH // GROUP, SPAN), F32),
            pltpu.VMEM((WIDTH // GROUP, 2 * SPAN, SPAN), BF16),
            pltpu.VMEM((WIDTH, ROWS), BF16),
            pltpu.VMEM((WIDTH, ROWS), BF16),
            pltpu.VMEM((2, RING * HALF, ROWS), BF16),
            pltpu.VMEM((2, RING * HALF, ROWS), BF16),
            pltpu.VMEM((2, RING * HALF, ROWS), BF16),
            pltpu.VMEM((2, 4, 2, HALF, ROWS), BF16),
            pltpu.VMEM((2 * HALF, ROWS), BF16),
            pltpu.VMEM((2 * HALF, ROWS), BF16),
            pltpu.VMEM((512, ROWS), F32),
            dma((6,)), dma, dma((2,)), dma((2, 4)),
            dma((2,)), dma((2, RING)), dma((2, RING)),
            dma((2, 4, 4)), dma((2, 4, 4)), dma((4,)), dma((4,)),
            dma((2, 5)), dma((2, 5)), dma((2, RING)), dma((2, 4, 2)), dma((2,)),
        ],
        compiler_params=pltpu.CompilerParams(
            collective_id=0, has_side_effects=True, vmem_limit_bytes=56 * 2**20
        ),
    )(qkv, feat_taps, long_filter.T, skip_gain.reshape(1, WIDTH), out_weight.T)


def solution(mesh):
    return jax.shard_map(
        local,
        mesh=mesh,
        in_specs=(
            P(None, "seq", "chan"),
            P(None, None, "chan"),
            P(None, "chan"),
            P("chan"),
            P("chan", "seq"),
        ),
        out_specs=P("seq", "chan"),
        check_vma=False,
    )
```

```python
import jax
import jax.numpy as jnp
from jax import lax
from jax.experimental import pallas as pl
from jax.experimental.pallas import tpu as pltpu
from jax.sharding import PartitionSpec as P

MESH = pl.DeviceIdType.MESH
F32 = jnp.float32
BF16 = jnp.bfloat16

RING = 8
GROUP = 16
SPAN = 128
FTAPS = 7
ROWS = 384
WIDTH = 1024
BLOCKS = ROWS // SPAN
LANES = 128
STRIPS = WIDTH // LANES
PIECE = 32
HALO = 16
PAD = 8
PITCH = 49
SUBS = 8
TALL = PITCH * SUBS

OFF = (1, -1, 2, -2, 3, -3, 4, 0)
SLOT = {off: slot for slot, off in enumerate(OFF)}
OWN = SLOT[0]
GROUPS = ((7,), (0, 1), (2, 3), (4, 5), (6,))
NEAR, CROSS, NEAR_EXT, CROSS_EXT = (pl.ds(2 * PIECE * i, 2 * PIECE) for i in range(4))
PARTS = (NEAR, pl.ds(4 * PIECE, PIECE), CROSS, pl.ds(6 * PIECE, PIECE))
HALF = 4 * PIECE
BATCH = 8
JOBS = 16


def origin(direction, step):
    return SLOT[4 if step == 4 else -direction * step]


def kernel(
    qkv_ref, taps_hbm, filt_hbm, skip_hbm, w_ref, out_ref,
    taps_ref, filt_ref, skip_ref,
    w_all, qkv_v, halo, ext_v, ub, qb, ut, qt, skt, hf, mats, y2,
    ta, sa, qa, ra, qp, rp, fin,
    load_sem, own_sem, halo_sem, tail_sem,
    xs, es, er, s2, r2, ys, yr, as1, ar1, as2, ar2, ps,
):
    s = lax.axis_index("seq")
    c = lax.axis_index("chan")
    y = lax.div(s, RING)
    z = lax.rem(s, RING)
    x = lax.div(c, 2)
    p = lax.rem(c, 2)

    def y_at(d):
        return {"seq": lax.rem(y + d + RING, RING) * RING + z}

    def z_at(d):
        return {"seq": y * RING + lax.rem(z + d + 2 * RING, RING)}

    def seq_at(d):
        return {"seq": lax.rem(s + d + RING * RING, RING * RING)}

    sibling = {"chan": c + 1 - 2 * p}
    outer = 2 * lax.rem(z, 2) - 1
    inner = -outer
    started = []

    def remote(src, dst, send, recv, to):
        return pltpu.make_async_remote_copy(
            src_ref=src, dst_ref=dst, send_sem=send, recv_sem=recv, device_id=to, device_id_type=MESH
        )

    def go(make, *args):
        make(*args).start()
        if (make, args) not in started:
            started.append((make, args))

    loads = [
        pltpu.make_async_copy(qkv_ref.at[i], qkv_v.at[i], load_sem.at[i]) for i in (1, 2, 0)
    ]
    loads += [
        pltpu.make_async_copy(taps_hbm, taps_ref, load_sem.at[3]),
        pltpu.make_async_copy(skip_hbm, skip_ref, load_sem.at[5]),
        pltpu.make_async_copy(filt_hbm, filt_ref, load_sem.at[4]),
    ]
    own = pltpu.make_async_copy(w_ref, w_all.at[OWN, NEAR], own_sem)
    for copy in loads[::-1] + [own]:
        copy.start()

    barrier = pltpu.get_barrier_semaphore()
    greeted = [{"chan": lax.rem(c + d, 8)} for d in range(1, 8)]
    greeted += [z_at(outer), z_at(inner), z_at(3 * inner), y_at(1), y_at(-1), seq_at(1), seq_at(-1)]
    for to in greeted:
        pl.semaphore_signal(barrier, inc=1, device_id=to, device_id_type=MESH)

    def toeplitz():
        loads[5].wait()
        hf[...] = filt_ref[...].astype(F32)

        def body(step, carry):
            row = lax.broadcasted_iota(jnp.int32, (SPAN, SPAN), 0)
            col = lax.broadcasted_iota(jnp.int32, (SPAN, SPAN), 1)
            for i in range(4):
                g = step * 4 + i
                taps = jnp.broadcast_to(hf[pl.ds(g, 1), :], (SPAN, SPAN))
                turned = pltpu.roll(taps, 0, 1, stride=1, stride_axis=0)
                mats[g, :SPAN] = jnp.where(row > col, turned, 0.0).astype(BF16)
                mats[g, SPAN:] = jnp.where(row <= col, turned, 0.0).astype(BF16)
            return carry

        lax.fori_loop(0, 16, body, 0)

    def widen():
        for copy in loads[:5]:
            copy.wait()

        def body(strip, carry):
            at = pl.ds(pl.multiple_of(strip * LANES, LANES), LANES)
            for i in range(3):
                ext_v[i, strip, PAD : PAD + ROWS, :] = qkv_v[i, :, at].astype(F32)
                ext_v[i, strip, PAD + ROWS :, :] = jnp.zeros((TALL - ROWS, LANES), F32)
            skt[at, :] = jnp.broadcast_to(skip_ref[:, at], (LANES, LANES)).T
            return carry

        lax.fori_loop(0, STRIPS, body, 0)

    widen()
    pl.semaphore_wait(barrier, len(greeted))

    def cross():
        return remote(w_ref, w_all.at[OWN, CROSS], xs.at[0], xs.at[1], z_at(3 * inner))

    def ext(which, slot):
        src, dst = ((NEAR, NEAR_EXT), (CROSS, CROSS_EXT))[which]
        if slot != OWN:
            src, dst = [pl.ds(at.start + PIECE, PIECE) for at in (src, dst)]
        found = w_ref if slot == OWN and which == 0 else w_all.at[slot, src]
        return remote(found, w_all.at[slot, dst], es.at[which, slot], er.at[which, slot], z_at(outer))

    def ring(direction, step, part):
        lane = 0 if direction == 1 else 1
        rows = PARTS[part]
        into = origin(direction, step)
        came = OWN if step == 1 else origin(direction, step - 1)
        src = w_ref if step == 1 and part == 0 else w_all.at[came, rows]
        at = lane, step - 1, part
        return remote(src, w_all.at[into, rows], s2.at[at], r2.at[at], y_at(direction))

    def lanes_of(step, part):
        if step < 4:
            return (1, -1)
        return (1,) if part < 2 else (-1,)

    def start_part(part):
        for direction in (1, -1):
            go(ring, direction, 1, part)

    def near_arrives():
        ext(0, OWN).wait_recv()
        start_part(1)

    def cross_arrives():
        cross().wait_recv()
        start_part(2)
        go(ext, 1, OWN)

    def cross_ext_arrives():
        ext(1, OWN).wait_recv()
        start_part(3)

    def part_arrives(step, part):
        for direction in lanes_of(step, part):
            ring(direction, step, part).wait_recv()
            if step < 4 and direction in lanes_of(step + 1, part):
                go(ring, direction, step + 1, part)
            if part in (0, 2):
                go(ext, part // 2, origin(direction, step))

    def settle(step):
        for slot in GROUPS[step]:
            for which in range(2):
                ext(which, slot).wait_recv()

    def happen(step, table):
        for at, calls in table.items():
            @pl.when(step == at)
            def run(calls=calls):
                for fn, *args in calls:
                    fn(*args)

    def halo_copy():
        return remote(
            qkv_ref.at[:, ROWS - HALO : ROWS], halo, halo_sem.at[0], halo_sem.at[1], seq_at(1)
        )

    go(cross)
    go(ext, 0, OWN)
    start_part(0)
    go(halo_copy)
    toeplitz()
    near_arrives()

    def halo_arrives():
        halo_copy().wait_recv()

        def body(strip, carry):
            at = pl.ds(pl.multiple_of(strip * LANES, LANES), LANES)
            for i in range(3):
                before = halo[i, :, at].astype(F32)[HALO - PAD :]
                ext_v[i, strip, :PAD, :] = jnp.where(s == 0, 0.0, before)
            return carry

        lax.fori_loop(0, STRIPS, body, 0)

    def features(strip):
        at = pl.ds(pl.multiple_of(strip * LANES, LANES), LANES)
        taps = [
            [jnp.broadcast_to(taps_ref[i, j : j + 1, at], (SUBS, LANES)) for j in range(FTAPS)]
            for i in range(3)
        ]

        def load(i, r):
            return ext_v[i, strip, pl.ds(PAD + r, SUBS, stride=PITCH), :]

        def line(i, window):
            total = taps[i][0] * window[-1]
            for j in range(1, FTAPS):
                total = total + taps[i][j] * window[-1 - j]
            return total

        def some(turn, windows):
            windows = [list(w) for w in windows]
            for step in range(FTAPS):
                r = turn * FTAPS + step
                found = []
                for i in range(3):
                    windows[i] = windows[i][1 - FTAPS :] + [load(i, r)]
                    found.append(line(i, windows[i]))
                ub[strip, pl.ds(r, SUBS, stride=PITCH), :] = found[1] * found[2]
                qb[strip, pl.ds(r, SUBS, stride=PITCH), :] = found[0]
            return tuple(tuple(w[1 - FTAPS :]) for w in windows)

        start = tuple(tuple(load(i, r) for r in range(1 - FTAPS, 0)) for i in range(3))
        lax.fori_loop(0, PITCH // FTAPS, some, start)
        for b in range(BLOCKS):
            ut[b + 1, at, :] = ub[strip, SPAN * b : SPAN * (b + 1), :].T.astype(BF16)
            qt[b, at, :] = qb[strip, SPAN * b : SPAN * (b + 1), :].T

    def tail(quarter):
        at = pl.ds(pl.multiple_of(quarter * (WIDTH // 4), WIDTH // 4), WIDTH // 4)
        return remote(
            ut.at[BLOCKS, at], ut.at[0, at], tail_sem.at[0, quarter], tail_sem.at[1, quarter], seq_at(1)
        )

    def tail_arrives(quarter):
        tail(quarter).wait_recv()

        @pl.when(s == 0)
        def clear():
            at = pl.ds(pl.multiple_of(quarter * (WIDTH // 4), WIDTH // 4), WIDTH // 4)
            ut[0, at] = jnp.zeros((WIDTH // 4, SPAN), BF16)

    def conv(quarter):
        def body(step, carry):
            base = step * BATCH
            spots = [pl.ds(pl.multiple_of((base + i) * GROUP, GROUP), GROUP) for i in range(BATCH)]
            parts = [[ut[b, at, :] for b in range(BLOCKS + 1)] for at in spots]
            mixed = []
            for i in range(BATCH):
                window = jnp.concatenate(
                    [
                        jnp.concatenate(parts[i][:BLOCKS], axis=0),
                        jnp.concatenate(parts[i][1:], axis=0),
                    ],
                    axis=1,
                )
                mixed.append(jnp.dot(window, mats[base + i], preferred_element_type=F32))
            found = []
            for i, at in enumerate(spots):
                for b in range(BLOCKS):
                    field = mixed[i][GROUP * b : GROUP * (b + 1)] + skt[at, :] * parts[i][b + 1].astype(F32)
                    found.append((qt[b, at, :] * field).astype(BF16))
            for i, at in enumerate(spots):
                for b in range(BLOCKS):
                    y2[0, at, SPAN * b : SPAN * (b + 1)] = found[BLOCKS * i + b]
            return carry

        lax.fori_loop(quarter * 2, quarter * 2 + 2, body, 0)

    def swap_y(quarter):
        at = pl.ds(pl.multiple_of(quarter * (WIDTH // 4), WIDTH // 4), WIDTH // 4)
        return remote(y2.at[0, at], y2.at[1, at], ys.at[quarter], yr.at[quarter], z_at(inner))

    def slot_of(job):
        late = lax.div(job - 10, 2) + 4
        return jnp.where(job >= 10, late, lax.rem(lax.rem(job, 5) + 7, RING))

    def tokens_of(job):
        late = 1 - lax.rem(job, 2)
        return jnp.where(job >= 10, late, jnp.where(job >= 5, 1, 0))

    def target_of(job):
        slot = slot_of(job)
        off = (lax.div(slot, 2) + 1) * (1 - 2 * lax.rem(slot, 2))
        return lax.rem(y + jnp.where(slot == OWN, 0, off) + RING, RING)

    def project(job, half):
        rows = w_all[slot_of(job), pl.ds(pl.multiple_of(half * HALF, HALF), HALF)]
        return jnp.dot(rows, y2[tokens_of(job)], preferred_element_type=F32)

    def swap(job):
        return remote(ta.at[job], sa.at[job], as1.at[job], ar1.at[job], sibling)

    def give(job):
        ta[job] = project(job, 1 - p).astype(BF16)
        swap(job).start()

    def delivery(job):
        tokens = tokens_of(job)
        return remote(
            qa.at[job], ra.at[tokens, x, p], as2.at[job], ar2.at[tokens, x, p], {"chan": target_of(job)}
        )

    def take(job):
        got = project(job, p)
        swap(job).wait_recv()
        qa[job] = (got + sa[job].astype(F32)).astype(BF16)
        to, tokens = target_of(job), tokens_of(job)

        @pl.when(to == c)
        def keep():
            pltpu.make_async_copy(qa.at[job], ra.at[tokens, x, p], ar2.at[tokens, x, p]).start()

        @pl.when(to != c)
        def post():
            delivery(job).start()

    def gathered(tokens, half):
        found = None
        for chip in range(4):
            here = ra.at[tokens, chip, half]
            remote(here, here, as2.at[0], ar2.at[tokens, chip, half], sibling).wait_recv()
        for chip in range(4):
            term = ra[tokens, chip, half].astype(F32)
            found = term if found is None else found + term
        return found

    def hand():
        return remote(qp, rp, ps.at[0], ps.at[1], z_at(inner))

    ahead = lax.rem(c - y + RING, RING)
    my_group = jnp.minimum(ahead, RING - ahead)
    ready = jnp.where(my_group <= 1, 13, jnp.where(my_group == 2, 14, jnp.where(my_group == 3, 17, 18)))

    def finish():
        for half in range(2):
            qp[half * HALF : (half + 1) * HALF] = gathered(1, half).astype(BF16)
        hand().start()

    def partner_y():
        for quarter in range(4):
            swap_y(quarter).wait_recv()

    halo_arrives()
    cross_arrives()

    def feature_quarter(quarter, carry):
        lax.fori_loop(quarter * 2, quarter * 2 + 2, lambda strip, carry: (features(strip), carry)[1], 0)
        tail(quarter).start()
        happen(quarter, {
            0: [(part_arrives, 1, 0)],
            1: [(cross_ext_arrives,), (part_arrives, 1, 1)],
            2: [(part_arrives, 1, 2)],
            3: [(part_arrives, 1, 3)],
        })
        return carry

    lax.fori_loop(0, 4, feature_quarter, 0)

    def conv_quarter(quarter, carry):
        tail_arrives(quarter)
        conv(quarter)
        swap_y(quarter).start()
        happen(quarter, {2: [(part_arrives, 2, 0)], 3: [(part_arrives, 2, 1)]})
        return carry

    lax.fori_loop(0, 4, conv_quarter, 0)
    own.wait()

    def turn(n, carry):
        @pl.when((n >= 2) & (n < JOBS + 2))
        def second():
            take(n - 2)

        @pl.when(n == ready)
        def partner_sum():
            finish()

        happen(n, {
            1: [(settle, 1)],
            2: [(part_arrives, 2, 2), (part_arrives, 2, 3)],
            3: [(settle, 2)],
            5: [(partner_y,), (part_arrives, 3, 0)],
            6: [(part_arrives, 3, 1)],
            7: [(part_arrives, 3, 2)],
            8: [(part_arrives, 3, 3)],
            10: [(settle, 3)],
            11: [(part_arrives, 4, 0)],
            12: [(part_arrives, 4, 1), (part_arrives, 4, 2)],
            13: [(part_arrives, 4, 3)],
            14: [(settle, 4)],
        })

        @pl.when(n < JOBS)
        def first():
            give(n)

        return carry

    lax.fori_loop(0, JOBS + 3, turn, 0)

    def place(z_from, rows):
        at = lax.rem(z + z_from + 2 * RING, RING) * (2 * PIECE)
        fin[pl.ds(pl.multiple_of(at, 2 * PIECE), 2 * PIECE), :] = rows

    for half in range(2):
        found = gathered(0, half)
        for i, z_from in enumerate(((0, outer + 4), (outer, 4))[half]):
            place(z_from, found[2 * PIECE * i : 2 * PIECE * (i + 1)])
    hand().wait_recv()
    for i, z_from in enumerate((inner, 2 * inner + 4, 2 * inner, inner + 4)):
        place(z_from, rp[2 * PIECE * i : 2 * PIECE * (i + 1)].astype(F32))
    for a in range(BLOCKS):
        for n in range(4):
            tile = fin[LANES * n : LANES * (n + 1), SPAN * a : SPAN * (a + 1)]
            out_ref[SPAN * a : SPAN * (a + 1), LANES * n : LANES * (n + 1)] = tile.T.astype(BF16)

    for make, args in started:
        make(*args).wait_send()
    hand().wait_send()

    def drain_quarter(quarter, carry):
        tail(quarter).wait_send()
        swap_y(quarter).wait_send()
        return carry

    lax.fori_loop(0, 4, drain_quarter, 0)

    def drain(job, carry):
        swap(job).wait_send()

        @pl.when(target_of(job) != c)
        def sent():
            delivery(job).wait_send()

        return carry

    lax.fori_loop(0, JOBS, drain, 0)


def local(qkv, feat_taps, long_filter, skip_gain, out_weight):
    vmem = pl.BlockSpec(memory_space=pltpu.VMEM)
    anywhere = pl.BlockSpec(memory_space=pl.ANY)
    dma = pltpu.SemaphoreType.DMA
    return pl.pallas_call(
        kernel,
        out_shape=jax.ShapeDtypeStruct((ROWS, 512), BF16),
        in_specs=[anywhere] * 5,
        out_specs=vmem,
        scratch_shapes=[
            pltpu.VMEM((3, FTAPS, WIDTH), F32),
            pltpu.VMEM((WIDTH // GROUP, SPAN), BF16),
            pltpu.VMEM((1, WIDTH), F32),
            pltpu.VMEM((RING, 8 * PIECE, WIDTH), BF16),
            pltpu.VMEM((3, ROWS, WIDTH), BF16),
            pltpu.VMEM((3, HALO, WIDTH), BF16),
            pltpu.VMEM((3, STRIPS, PAD + TALL, LANES), F32),
            pltpu.VMEM((STRIPS, TALL, LANES), F32),
            pltpu.VMEM((STRIPS, TALL, LANES), F32),
            pltpu.VMEM((BLOCKS + 1, WIDTH, SPAN), BF16),
            pltpu.VMEM((BLOCKS, WIDTH, SPAN), F32),
            pltpu.VMEM((WIDTH, SPAN), F32),
            pltpu.VMEM((WIDTH // GROUP, SPAN), F32),
            pltpu.VMEM((WIDTH // GROUP, 2 * SPAN, SPAN), BF16),
            pltpu.VMEM((2, WIDTH, ROWS), BF16),
            pltpu.VMEM((JOBS, HALF, ROWS), BF16),
            pltpu.VMEM((JOBS, HALF, ROWS), BF16),
            pltpu.VMEM((JOBS, HALF, ROWS), BF16),
            pltpu.VMEM((2, 4, 2, HALF, ROWS), BF16),
            pltpu.VMEM((2 * HALF, ROWS), BF16),
            pltpu.VMEM((2 * HALF, ROWS), BF16),
            pltpu.VMEM((512, ROWS), F32),
            dma((6,)), dma, dma((2,)), dma((2, 4)),
            dma((2,)), dma((2, RING)), dma((2, RING)),
            dma((2, 4, 4)), dma((2, 4, 4)), dma((4,)), dma((4,)),
            dma((JOBS,)), dma((JOBS,)), dma((JOBS,)), dma((2, 4, 2)), dma((2,)),
        ],
        compiler_params=pltpu.CompilerParams(
            collective_id=0, has_side_effects=True, vmem_limit_bytes=56 * 2**20
        ),
    )(qkv, feat_taps, long_filter.T, skip_gain.reshape(1, WIDTH), out_weight.T)


def solution(mesh):
    return jax.shard_map(
        local,
        mesh=mesh,
        in_specs=(
            P(None, "seq", "chan"),
            P(None, None, "chan"),
            P(None, "chan"),
            P("chan"),
            P("chan", "seq"),
        ),
        out_specs=P("seq", "chan"),
        check_vma=False,
    )
```

```python
import jax
import jax.numpy as jnp
from jax import lax
from jax.experimental import pallas as pl
from jax.experimental.pallas import tpu as pltpu
from jax.sharding import PartitionSpec as P

MESH = pl.DeviceIdType.MESH
F32 = jnp.float32
BF16 = jnp.bfloat16

RING = 8
GROUP = 16
SPAN = 128
FTAPS = 7
ROWS = 384
WIDTH = 1024
BLOCKS = ROWS // SPAN
LANES = 128
STRIPS = WIDTH // LANES
PIECE = 32
HALO = 16
PAD = 8
PITCH = 49
SUBS = 8
TALL = PITCH * SUBS

OFF = (0, 1, -1, 2, -2, 3, -3, 4)
SLOT = {off: slot for slot, off in enumerate(OFF)}
OWN = SLOT[0]
GROUPS = ((0,), (1, 2), (3, 4), (5, 6), (7,))
NEAR, CROSS, NEAR_EXT, CROSS_EXT = (pl.ds(2 * PIECE * i, 2 * PIECE) for i in range(4))
PARTS = (NEAR, pl.ds(4 * PIECE, PIECE), CROSS, pl.ds(6 * PIECE, PIECE))
HALF = 4 * PIECE
BATCH = 8
JOBS = 8
CHIPS = 4


def origin(direction, step):
    return SLOT[4 if step == 4 else -direction * step]


def kernel(
    qkv_ref, taps_hbm, filt_hbm, skip_hbm, w_ref, out_ref,
    taps_ref, filt_ref, skip_ref,
    w_all, qkv_v, halo, ext_v, ub, qb, ut, qt, skt, hf, mats, y2,
    ta, sa, qa, rb, oa,
    load_sem, own_sem, halo_sem, tail_sem,
    xs, es, er, s2, r2, ys, yr, as1, ar1, bs, br, cs, cr,
):
    s = lax.axis_index("seq")
    c = lax.axis_index("chan")
    y = lax.div(s, RING)
    z = lax.rem(s, RING)
    x = lax.div(c, 2)
    p = lax.rem(c, 2)

    def y_at(d):
        return {"seq": lax.rem(y + d + RING, RING) * RING + z}

    def z_at(d):
        return {"seq": y * RING + lax.rem(z + d + 2 * RING, RING)}

    def seq_at(d):
        return {"seq": lax.rem(s + d + RING * RING, RING * RING)}

    sibling = {"chan": c + 1 - 2 * p}
    outer = 2 * lax.rem(z, 2) - 1
    inner = -outer
    started = []

    def remote(src, dst, send, recv, to):
        return pltpu.make_async_remote_copy(
            src_ref=src, dst_ref=dst, send_sem=send, recv_sem=recv, device_id=to, device_id_type=MESH
        )

    def go(make, *args):
        make(*args).start()
        if (make, args) not in started:
            started.append((make, args))

    loads = [
        pltpu.make_async_copy(qkv_ref.at[i], qkv_v.at[i], load_sem.at[i]) for i in (1, 2, 0)
    ]
    loads += [
        pltpu.make_async_copy(taps_hbm, taps_ref, load_sem.at[3]),
        pltpu.make_async_copy(skip_hbm, skip_ref, load_sem.at[5]),
        pltpu.make_async_copy(filt_hbm, filt_ref, load_sem.at[4]),
    ]
    own = pltpu.make_async_copy(w_ref, w_all.at[OWN, NEAR], own_sem)
    for copy in loads[::-1] + [own]:
        copy.start()

    barrier = pltpu.get_barrier_semaphore()
    greeted = [{"chan": lax.rem(c + d, 8)} for d in range(1, 8)]
    greeted += [z_at(outer), z_at(3 * inner), y_at(1), y_at(-1), seq_at(1), seq_at(-1)]
    greeted += [{**z_at(inner), "chan": lax.rem(c + d, 8)} for d in range(8)]
    for to in greeted:
        pl.semaphore_signal(barrier, inc=1, device_id=to, device_id_type=MESH)

    def toeplitz():
        loads[5].wait()
        hf[...] = filt_ref[...].astype(F32)

        def body(step, carry):
            row = lax.broadcasted_iota(jnp.int32, (SPAN, SPAN), 0)
            col = lax.broadcasted_iota(jnp.int32, (SPAN, SPAN), 1)
            for i in range(4):
                g = step * 4 + i
                taps = jnp.broadcast_to(hf[pl.ds(g, 1), :], (SPAN, SPAN))
                turned = pltpu.roll(taps, 0, 1, stride=1, stride_axis=0)
                mats[g, :SPAN] = jnp.where(row > col, turned, 0.0).astype(BF16)
                mats[g, SPAN:] = jnp.where(row <= col, turned, 0.0).astype(BF16)
            return carry

        lax.fori_loop(0, 16, body, 0)

    def widen():
        for copy in loads[:5]:
            copy.wait()

        def body(strip, carry):
            at = pl.ds(pl.multiple_of(strip * LANES, LANES), LANES)
            for i in range(3):
                ext_v[i, strip, PAD : PAD + ROWS, :] = qkv_v[i, :, at].astype(F32)
                ext_v[i, strip, PAD + ROWS :, :] = jnp.zeros((TALL - ROWS, LANES), F32)
            skt[at, :] = jnp.broadcast_to(skip_ref[:, at], (LANES, LANES)).T
            return carry

        lax.fori_loop(0, STRIPS, body, 0)

    widen()
    pl.semaphore_wait(barrier, len(greeted))

    def cross():
        return remote(w_ref, w_all.at[OWN, CROSS], xs.at[0], xs.at[1], z_at(3 * inner))

    def ext(which, slot):
        src, dst = ((NEAR, NEAR_EXT), (CROSS, CROSS_EXT))[which]
        if slot != OWN:
            src, dst = [pl.ds(at.start + PIECE, PIECE) for at in (src, dst)]
        found = w_ref if slot == OWN and which == 0 else w_all.at[slot, src]
        return remote(found, w_all.at[slot, dst], es.at[which, slot], er.at[which, slot], z_at(outer))

    def ring(direction, step, part):
        lane = 0 if direction == 1 else 1
        rows = PARTS[part]
        into = origin(direction, step)
        came = OWN if step == 1 else origin(direction, step - 1)
        src = w_ref if step == 1 and part == 0 else w_all.at[came, rows]
        at = lane, step - 1, part
        return remote(src, w_all.at[into, rows], s2.at[at], r2.at[at], y_at(direction))

    def lanes_of(step, part):
        if step < 4:
            return (1, -1)
        return (1,) if part < 2 else (-1,)

    def start_part(part):
        for direction in (1, -1):
            go(ring, direction, 1, part)

    def near_arrives():
        ext(0, OWN).wait_recv()
        start_part(1)

    def cross_arrives():
        cross().wait_recv()
        start_part(2)
        go(ext, 1, OWN)

    def cross_ext_arrives():
        ext(1, OWN).wait_recv()
        start_part(3)

    def part_arrives(step, part):
        for direction in lanes_of(step, part):
            ring(direction, step, part).wait_recv()
            if step < 4 and direction in lanes_of(step + 1, part):
                go(ring, direction, step + 1, part)
            if part in (0, 2):
                go(ext, part // 2, origin(direction, step))

    def settle(step):
        for slot in GROUPS[step]:
            for which in range(2):
                ext(which, slot).wait_recv()

    def happen(step, table):
        for at, calls in table.items():
            @pl.when(step == at)
            def run(calls=calls):
                for fn, *args in calls:
                    fn(*args)

    def halo_copy():
        return remote(
            qkv_ref.at[:, ROWS - HALO : ROWS], halo, halo_sem.at[0], halo_sem.at[1], seq_at(1)
        )

    go(cross)
    go(ext, 0, OWN)
    start_part(0)
    go(halo_copy)
    toeplitz()
    near_arrives()

    def halo_arrives():
        halo_copy().wait_recv()

        def body(strip, carry):
            at = pl.ds(pl.multiple_of(strip * LANES, LANES), LANES)
            for i in range(3):
                before = halo[i, :, at].astype(F32)[HALO - PAD :]
                ext_v[i, strip, :PAD, :] = jnp.where(s == 0, 0.0, before)
            return carry

        lax.fori_loop(0, STRIPS, body, 0)

    def features(strip):
        at = pl.ds(pl.multiple_of(strip * LANES, LANES), LANES)
        taps = [
            [jnp.broadcast_to(taps_ref[i, j : j + 1, at], (SUBS, LANES)) for j in range(FTAPS)]
            for i in range(3)
        ]

        def load(i, r):
            return ext_v[i, strip, pl.ds(PAD + r, SUBS, stride=PITCH), :]

        def line(i, window):
            total = taps[i][0] * window[-1]
            for j in range(1, FTAPS):
                total = total + taps[i][j] * window[-1 - j]
            return total

        def some(turn, windows):
            windows = [list(w) for w in windows]
            for step in range(FTAPS):
                r = turn * FTAPS + step
                found = []
                for i in range(3):
                    windows[i] = windows[i][1 - FTAPS :] + [load(i, r)]
                    found.append(line(i, windows[i]))
                ub[strip, pl.ds(r, SUBS, stride=PITCH), :] = found[1] * found[2]
                qb[strip, pl.ds(r, SUBS, stride=PITCH), :] = found[0]
            return tuple(tuple(w[1 - FTAPS :]) for w in windows)

        start = tuple(tuple(load(i, r) for r in range(1 - FTAPS, 0)) for i in range(3))
        lax.fori_loop(0, PITCH // FTAPS, some, start)
        for b in range(BLOCKS):
            ut[b + 1, at, :] = ub[strip, SPAN * b : SPAN * (b + 1), :].T.astype(BF16)
            qt[b, at, :] = qb[strip, SPAN * b : SPAN * (b + 1), :].T

    def tail(quarter):
        at = pl.ds(pl.multiple_of(quarter * (WIDTH // 4), WIDTH // 4), WIDTH // 4)
        return remote(
            ut.at[BLOCKS, at], ut.at[0, at], tail_sem.at[0, quarter], tail_sem.at[1, quarter], seq_at(1)
        )

    def tail_arrives(quarter):
        tail(quarter).wait_recv()

        @pl.when(s == 0)
        def clear():
            at = pl.ds(pl.multiple_of(quarter * (WIDTH // 4), WIDTH // 4), WIDTH // 4)
            ut[0, at] = jnp.zeros((WIDTH // 4, SPAN), BF16)

    def conv(quarter):
        def body(step, carry):
            base = step * BATCH
            spots = [pl.ds(pl.multiple_of((base + i) * GROUP, GROUP), GROUP) for i in range(BATCH)]
            parts = [[ut[b, at, :] for b in range(BLOCKS + 1)] for at in spots]
            mixed = []
            for i in range(BATCH):
                window = jnp.concatenate(
                    [
                        jnp.concatenate(parts[i][:BLOCKS], axis=0),
                        jnp.concatenate(parts[i][1:], axis=0),
                    ],
                    axis=1,
                )
                mixed.append(jnp.dot(window, mats[base + i], preferred_element_type=F32))
            found = []
            for i, at in enumerate(spots):
                for b in range(BLOCKS):
                    field = mixed[i][GROUP * b : GROUP * (b + 1)] + skt[at, :] * parts[i][b + 1].astype(F32)
                    found.append((qt[b, at, :] * field).astype(BF16))
            for i, at in enumerate(spots):
                for b in range(BLOCKS):
                    y2[0, at, SPAN * b : SPAN * (b + 1)] = found[BLOCKS * i + b]
            return carry

        lax.fori_loop(quarter * 2, quarter * 2 + 2, body, 0)

    def swap_y(quarter):
        at = pl.ds(pl.multiple_of(quarter * (WIDTH // 4), WIDTH // 4), WIDTH // 4)
        return remote(y2.at[0, at], y2.at[1, at], ys.at[quarter], yr.at[quarter], z_at(inner))

    def project(job, half):
        pair = lax.rem(job, 4)
        rows = w_all[pl.ds(2 * pair, 2), pl.ds(pl.multiple_of(half * HALF, HALF), HALF)]
        return jnp.dot(
            rows.reshape(2 * HALF, WIDTH), y2[lax.div(job, 4)], preferred_element_type=F32
        )

    def swap(job):
        return remote(ta.at[job], sa.at[job], as1.at[job], ar1.at[job], sibling)

    def give(job):
        ta[job] = project(job, 1 - p).astype(BF16)
        swap(job).start()

    def scatter(job, step):
        to = lax.rem(x + step, CHIPS)
        return remote(
            qa.at[job, to], rb.at[job, step - 1], bs.at[job, step - 1], br.at[job, step - 1],
            {"chan": 2 * to + p},
        )

    def take(job):
        got = project(job, p)
        swap(job).wait_recv()
        got = (got + sa[job].astype(F32)).astype(BF16)
        for i in range(2):
            for chip in range(CHIPS):
                at = HALF * i + PIECE * chip
                qa[job, chip, PIECE * i : PIECE * (i + 1)] = got[at : at + PIECE]
        for step in (2, 1, 3):
            scatter(job, step).start()

    def columns(z_here, outer_here, chip, core):
        first = jnp.where(core == 0, 0, outer_here)
        second = jnp.where(core == 0, outer_here + 4, 4)
        shard = lax.rem(z_here + jnp.where(chip < 2, first, second) + 2 * RING, RING)
        at = shard * (2 * PIECE) + lax.rem(chip, 2) * PIECE
        return out_ref.at[pl.ds(pl.multiple_of(at, PIECE), PIECE)]

    def target_of(job, i):
        slot = 2 * lax.rem(job, 4) + i
        off = lax.div(slot + 1, 2) * (2 * lax.rem(slot, 2) - 1)
        return lax.rem(y + off + RING, RING)

    def delivery(job, i):
        tokens = lax.div(job, 4)
        to = {"seq": y * RING + lax.rem(z + tokens * inner + RING, RING), "chan": target_of(job, i)}
        return remote(
            oa.at[job, i], columns(z, outer, x, p), cs.at[job, i], cr.at[tokens, x, p], to
        )

    def stays(job, i):
        return (job < 4) & (target_of(job, i) == c)

    def reduce(job):
        total = qa[job, x].astype(F32)
        for step in (1, 3, 2):
            scatter(job, step).wait_recv()
            total = total + rb[job, step - 1].astype(F32)
        total = total.astype(BF16)
        for i in range(2):
            oa[job, i] = total[PIECE * i : PIECE * (i + 1)]
        for i in range(2):
            @pl.when(stays(job, i))
            def keep():
                pltpu.make_async_copy(oa.at[job, i], columns(z, outer, x, p), cr.at[0, x, p]).start()

            @pl.when(jnp.logical_not(stays(job, i)))
            def post():
                delivery(job, i).start()

    def partner_y():
        for quarter in range(4):
            swap_y(quarter).wait_recv()

    halo_arrives()
    cross_arrives()

    def quarters(n, carry):
        @pl.when(n < 4)
        def feature_quarter():
            lax.fori_loop(n * 2, n * 2 + 2, lambda strip, carry: (features(strip), carry)[1], 0)
            tail(n).start()

        happen(n, {
            0: [(part_arrives, 1, 0)],
            1: [(cross_ext_arrives,), (part_arrives, 1, 1)],
            2: [(part_arrives, 1, 2)],
            3: [(part_arrives, 1, 3)],
            4: [(part_arrives, 2, 0)],
            5: [(part_arrives, 2, 1)],
        })

        @pl.when(n >= 2)
        def conv_quarter():
            tail_arrives(n - 2)
            conv(n - 2)
            swap_y(n - 2).start()

        return carry

    lax.fori_loop(0, 6, quarters, 0)
    own.wait()

    def turn(n, carry):
        @pl.when((n >= 1) & (n < JOBS + 1))
        def second():
            take(n - 1)

        @pl.when(n >= 3)
        def third():
            reduce(n - 3)

        happen(n, {
            0: [(part_arrives, 2, 2), (settle, 1)],
            1: [(part_arrives, 2, 3), (settle, 2)],
            2: [(part_arrives, 3, part) for part in range(4)] + [(settle, 3)],
            3: [(part_arrives, 4, part) for part in range(4)] + [(settle, 4)],
            4: [(partner_y,)],
        })

        @pl.when(n < JOBS)
        def first():
            give(n)

        return carry

    lax.fori_loop(0, JOBS + 3, turn, 0)

    for core in range(2):
        for chip in range(CHIPS):
            for tokens in range(2):
                here = columns(z + tokens * inner, outer * (1 - 2 * tokens), chip, core)
                remote(oa.at[0, 0], here, cs.at[0, 0], cr.at[tokens, chip, core], sibling).wait_recv()

    for make, args in started:
        make(*args).wait_send()

    def drain_quarter(quarter, carry):
        tail(quarter).wait_send()
        swap_y(quarter).wait_send()
        return carry

    lax.fori_loop(0, 4, drain_quarter, 0)

    def drain(job, carry):
        swap(job).wait_send()
        for step in (1, 2, 3):
            scatter(job, step).wait_send()
        for i in range(2):
            @pl.when(jnp.logical_not(stays(job, i)))
            def sent():
                delivery(job, i).wait_send()

        return carry

    lax.fori_loop(0, JOBS, drain, 0)


def local(qkv, feat_taps, long_filter, skip_gain, out_weight):
    anywhere = pl.BlockSpec(memory_space=pl.ANY)
    dma = pltpu.SemaphoreType.DMA
    return pl.pallas_call(
        kernel,
        out_shape=jax.ShapeDtypeStruct((512, ROWS), BF16),
        in_specs=[anywhere] * 5,
        out_specs=anywhere,
        scratch_shapes=[
            pltpu.VMEM((3, FTAPS, WIDTH), F32),
            pltpu.VMEM((WIDTH // GROUP, SPAN), BF16),
            pltpu.VMEM((1, WIDTH), F32),
            pltpu.VMEM((RING, 8 * PIECE, WIDTH), BF16),
            pltpu.VMEM((3, ROWS, WIDTH), BF16),
            pltpu.VMEM((3, HALO, WIDTH), BF16),
            pltpu.VMEM((3, STRIPS, PAD + TALL, LANES), F32),
            pltpu.VMEM((STRIPS, TALL, LANES), F32),
            pltpu.VMEM((STRIPS, TALL, LANES), F32),
            pltpu.VMEM((BLOCKS + 1, WIDTH, SPAN), BF16),
            pltpu.VMEM((BLOCKS, WIDTH, SPAN), F32),
            pltpu.VMEM((WIDTH, SPAN), F32),
            pltpu.VMEM((WIDTH // GROUP, SPAN), F32),
            pltpu.VMEM((WIDTH // GROUP, 2 * SPAN, SPAN), BF16),
            pltpu.VMEM((2, WIDTH, ROWS), BF16),
            pltpu.VMEM((JOBS, 2 * HALF, ROWS), BF16),
            pltpu.VMEM((JOBS, 2 * HALF, ROWS), BF16),
            pltpu.VMEM((JOBS, CHIPS, 2 * PIECE, ROWS), BF16),
            pltpu.VMEM((JOBS, CHIPS - 1, 2 * PIECE, ROWS), BF16),
            pltpu.VMEM((JOBS, 2, PIECE, ROWS), BF16),
            dma((6,)), dma, dma((2,)), dma((2, 4)),
            dma((2,)), dma((2, RING)), dma((2, RING)),
            dma((2, 4, 4)), dma((2, 4, 4)), dma((4,)), dma((4,)),
            dma((JOBS,)), dma((JOBS,)), dma((JOBS, CHIPS - 1)), dma((JOBS, CHIPS - 1)),
            dma((JOBS, 2)), dma((2, CHIPS, 2)),
        ],
        compiler_params=pltpu.CompilerParams(
            collective_id=0, has_side_effects=True, vmem_limit_bytes=56 * 2**20
        ),
    )(qkv, feat_taps, long_filter.T, skip_gain.reshape(1, WIDTH), out_weight.T).T


def solution(mesh):
    return jax.shard_map(
        local,
        mesh=mesh,
        in_specs=(
            P(None, "seq", "chan"),
            P(None, None, "chan"),
            P(None, "chan"),
            P("chan"),
            P("chan", "seq"),
        ),
        out_specs=P("seq", "chan"),
        check_vma=False,
    )
```

```python
import jax
import jax.numpy as jnp
from jax import lax
from jax.experimental import pallas as pl
from jax.experimental.pallas import tpu as pltpu
from jax.sharding import PartitionSpec as P

MESH = pl.DeviceIdType.MESH
F32 = jnp.float32
BF16 = jnp.bfloat16

RING = 8
GROUP = 16
SPAN = 128
FTAPS = 7
ROWS = 384
WIDTH = 1024
BLOCKS = ROWS // SPAN
LANES = 128
STRIPS = WIDTH // LANES
PIECE = 32
HALO = 16
PAD = 8
PITCH = 49
SUBS = 8
TALL = PITCH * SUBS

OFF = (0, 1, -1, 2, -2, 3, -3, 4)
SLOT = {off: slot for slot, off in enumerate(OFF)}
OWN = SLOT[0]
GROUPS = ((0,), (1, 2), (3, 4), (5, 6), (7,))
NEAR, CROSS, NEAR_EXT, CROSS_EXT = (pl.ds(2 * PIECE * i, 2 * PIECE) for i in range(4))
PARTS = (NEAR, pl.ds(4 * PIECE, PIECE), CROSS, pl.ds(6 * PIECE, PIECE))
HALF = 4 * PIECE
BATCH = 8
JOBS = 8
CHIPS = 4


def origin(direction, step):
    return SLOT[4 if step == 4 else -direction * step]


class Place:
    def __init__(self):
        self.s = lax.axis_index("seq")
        self.c = lax.axis_index("chan")
        self.y = lax.div(self.s, RING)
        self.z = lax.rem(self.s, RING)
        self.x = lax.div(self.c, 2)
        self.p = lax.rem(self.c, 2)

    def y_at(self, d):
        return {"seq": lax.rem(self.y + d + RING, RING) * RING + self.z}

    def z_at(self, d):
        return {"seq": self.y * RING + lax.rem(self.z + d + 2 * RING, RING)}

    def seq_at(self, d):
        return {"seq": lax.rem(self.s + d + RING * RING, RING * RING)}


def remote(src, dst, send, recv, to):
    return pltpu.make_async_remote_copy(
        src_ref=src, dst_ref=dst, send_sem=send, recv_sem=recv, device_id=to, device_id_type=MESH
    )


def greet(devices):
    barrier = pltpu.get_barrier_semaphore()
    for to in devices:
        pl.semaphore_signal(barrier, inc=1, device_id=to, device_id_type=MESH)
    return barrier


def mixer(
    qkv_ref, taps_hbm, filt_hbm, skip_hbm, y_ref,
    taps_ref, filt_ref, skip_ref,
    qkv_v, halo, ext_v, ub, qb, ut, qt, skt, hf, mats,
    load_sem, halo_sem, tail_sem,
):
    place = Place()
    s, seq_at = place.s, place.seq_at
    loads = [
        pltpu.make_async_copy(qkv_ref.at[i], qkv_v.at[i], load_sem.at[i]) for i in (1, 2, 0)
    ]
    loads += [
        pltpu.make_async_copy(taps_hbm, taps_ref, load_sem.at[3]),
        pltpu.make_async_copy(skip_hbm, skip_ref, load_sem.at[5]),
        pltpu.make_async_copy(filt_hbm, filt_ref, load_sem.at[4]),
    ]
    for copy in loads[::-1]:
        copy.start()
    barrier = greet([seq_at(1), seq_at(-1)])

    def toeplitz():
        loads[5].wait()
        hf[...] = filt_ref[...].astype(F32)

        def body(step, carry):
            row = lax.broadcasted_iota(jnp.int32, (SUBS, SPAN), 0)
            col = lax.broadcasted_iota(jnp.int32, (SUBS, SPAN), 1)
            for i in range(4):
                g = step * 4 + i
                base = jnp.broadcast_to(hf[pl.ds(g, 1), :], (SUBS, SPAN))
                for bit in (1, 2, 4):
                    base = jnp.where((row & bit) != 0, pltpu.roll(base, bit, 1), base)
                for pair in range(SPAN // (2 * SUBS)):
                    above, below = [], []
                    for k in (2 * pair, 2 * pair + 1):
                        turned = pltpu.roll(base, SUBS * k, 1) if k else base
                        under = row + SUBS * k > col
                        above.append(jnp.where(under, turned, 0.0))
                        below.append(jnp.where(under, 0.0, turned))
                    at = 2 * SUBS * pair
                    mats[g, at : at + 2 * SUBS] = jnp.concatenate(above, axis=0).astype(BF16)
                    mats[g, SPAN + at : SPAN + at + 2 * SUBS] = jnp.concatenate(below, axis=0).astype(BF16)
            return carry

        lax.fori_loop(0, 16, body, 0)

    def widen():
        for copy in loads[:5]:
            copy.wait()

        def body(strip, carry):
            at = pl.ds(pl.multiple_of(strip * LANES, LANES), LANES)
            for i in range(3):
                ext_v[i, strip, PAD : PAD + ROWS, :] = qkv_v[i, :, at].astype(F32)
                ext_v[i, strip, PAD + ROWS :, :] = jnp.zeros((TALL - ROWS, LANES), F32)
            skt[at, :] = jnp.broadcast_to(skip_ref[:, at], (LANES, LANES)).T
            return carry

        lax.fori_loop(0, STRIPS, body, 0)

    widen()
    pl.semaphore_wait(barrier, 2)

    def halo_copy():
        return remote(
            qkv_ref.at[:, ROWS - HALO : ROWS], halo, halo_sem.at[0], halo_sem.at[1], seq_at(1)
        )

    halo_copy().start()
    toeplitz()

    def halo_arrives():
        halo_copy().wait_recv()

        def body(strip, carry):
            at = pl.ds(pl.multiple_of(strip * LANES, LANES), LANES)
            for i in range(3):
                before = halo[i, :, at].astype(F32)[HALO - PAD :]
                ext_v[i, strip, :PAD, :] = jnp.where(s == 0, 0.0, before)
            return carry

        lax.fori_loop(0, STRIPS, body, 0)

    def features(strip):
        at = pl.ds(pl.multiple_of(strip * LANES, LANES), LANES)
        taps = [
            [jnp.broadcast_to(taps_ref[i, j : j + 1, at], (SUBS, LANES)) for j in range(FTAPS)]
            for i in range(3)
        ]

        def load(i, r):
            return ext_v[i, strip, pl.ds(PAD + r, SUBS, stride=PITCH), :]

        def line(i, window):
            total = taps[i][0] * window[-1]
            for j in range(1, FTAPS):
                total = total + taps[i][j] * window[-1 - j]
            return total

        def some(turn, windows):
            windows = [list(w) for w in windows]
            for step in range(FTAPS):
                r = turn * FTAPS + step
                found = []
                for i in range(3):
                    windows[i] = windows[i][1 - FTAPS :] + [load(i, r)]
                    found.append(line(i, windows[i]))
                ub[strip, pl.ds(r, SUBS, stride=PITCH), :] = found[1] * found[2]
                qb[strip, pl.ds(r, SUBS, stride=PITCH), :] = found[0]
            return tuple(tuple(w[1 - FTAPS :]) for w in windows)

        start = tuple(tuple(load(i, r) for r in range(1 - FTAPS, 0)) for i in range(3))
        lax.fori_loop(0, PITCH // FTAPS, some, start)
        for b in range(BLOCKS):
            ut[b + 1, at, :] = ub[strip, SPAN * b : SPAN * (b + 1), :].T.astype(BF16)
            qt[b, at, :] = qb[strip, SPAN * b : SPAN * (b + 1), :].T

    def tail(quarter):
        at = pl.ds(pl.multiple_of(quarter * (WIDTH // 4), WIDTH // 4), WIDTH // 4)
        return remote(
            ut.at[BLOCKS, at], ut.at[0, at], tail_sem.at[0, quarter], tail_sem.at[1, quarter], seq_at(1)
        )

    def tail_arrives(quarter):
        tail(quarter).wait_recv()

        @pl.when(s == 0)
        def clear():
            at = pl.ds(pl.multiple_of(quarter * (WIDTH // 4), WIDTH // 4), WIDTH // 4)
            ut[0, at] = jnp.zeros((WIDTH // 4, SPAN), BF16)

    def conv(quarter):
        def body(step, carry):
            base = step * BATCH
            spots = [pl.ds(pl.multiple_of((base + i) * GROUP, GROUP), GROUP) for i in range(BATCH)]
            parts = [[ut[b, at, :] for b in range(BLOCKS + 1)] for at in spots]
            mixed = []
            for i in range(BATCH):
                window = jnp.concatenate(
                    [
                        jnp.concatenate(parts[i][:BLOCKS], axis=0),
                        jnp.concatenate(parts[i][1:], axis=0),
                    ],
                    axis=1,
                )
                mixed.append(jnp.dot(window, mats[base + i], preferred_element_type=F32))
            found = []
            for i, at in enumerate(spots):
                for b in range(BLOCKS):
                    field = mixed[i][GROUP * b : GROUP * (b + 1)] + skt[at, :] * parts[i][b + 1].astype(F32)
                    found.append((qt[b, at, :] * field).astype(BF16))
            for i, at in enumerate(spots):
                for b in range(BLOCKS):
                    y_ref[at, SPAN * b : SPAN * (b + 1)] = found[BLOCKS * i + b]
            return carry

        lax.fori_loop(quarter * 2, quarter * 2 + 2, body, 0)

    halo_arrives()

    def quarters(n, carry):
        @pl.when(n < 4)
        def feature_quarter():
            lax.fori_loop(n * 2, n * 2 + 2, lambda strip, carry: (features(strip), carry)[1], 0)
            tail(n).start()

        @pl.when(n >= 2)
        def conv_quarter():
            tail_arrives(n - 2)
            conv(n - 2)

        return carry

    lax.fori_loop(0, 6, quarters, 0)
    halo_copy().wait_send()

    def drain(quarter, carry):
        tail(quarter).wait_send()
        return carry

    lax.fori_loop(0, 4, drain, 0)


def projector(
    y_ref, w_ref, out_ref,
    w_all, y2, ta, sa, qa, rb, oa,
    own_sem, xs, es, er, s2, r2, ys, as1, ar1, bs, br, cs, cr,
):
    place = Place()
    c, y, z, x, p = place.c, place.y, place.z, place.x, place.p
    y_at, z_at, seq_at = place.y_at, place.z_at, place.seq_at
    sibling = {"chan": c + 1 - 2 * p}
    outer = 2 * lax.rem(z, 2) - 1
    inner = -outer
    started = []

    def go(make, *args):
        make(*args).start()
        if (make, args) not in started:
            started.append((make, args))

    own = pltpu.make_async_copy(w_ref, w_all.at[OWN, NEAR], own_sem.at[0])
    mine = pltpu.make_async_copy(y_ref, y2.at[0], own_sem.at[1])
    own.start()
    mine.start()
    greeted = [{"chan": lax.rem(c + d, 8)} for d in range(1, 8)]
    greeted += [z_at(outer), z_at(3 * inner), y_at(1), y_at(-1)]
    greeted += [{**z_at(inner), "chan": lax.rem(c + d, 8)} for d in range(8)]
    pl.semaphore_wait(greet(greeted), len(greeted))

    def cross():
        return remote(w_ref, w_all.at[OWN, CROSS], xs.at[0], xs.at[1], z_at(3 * inner))

    def ext(which, slot):
        src, dst = ((NEAR, NEAR_EXT), (CROSS, CROSS_EXT))[which]
        if slot != OWN:
            src, dst = [pl.ds(at.start + PIECE, PIECE) for at in (src, dst)]
        found = w_ref if slot == OWN and which == 0 else w_all.at[slot, src]
        return remote(found, w_all.at[slot, dst], es.at[which, slot], er.at[which, slot], z_at(outer))

    def ring(direction, step, part):
        lane = 0 if direction == 1 else 1
        rows = PARTS[part]
        into = origin(direction, step)
        came = OWN if step == 1 else origin(direction, step - 1)
        src = w_ref if step == 1 and part == 0 else w_all.at[came, rows]
        at = lane, step - 1, part
        return remote(src, w_all.at[into, rows], s2.at[at], r2.at[at], y_at(direction))

    def lanes_of(step, part):
        if step < 4:
            return (1, -1)
        return (1,) if part < 2 else (-1,)

    def start_part(part):
        for direction in (1, -1):
            go(ring, direction, 1, part)

    def near_arrives():
        ext(0, OWN).wait_recv()
        start_part(1)

    def cross_arrives():
        cross().wait_recv()
        start_part(2)
        go(ext, 1, OWN)

    def cross_ext_arrives():
        ext(1, OWN).wait_recv()
        start_part(3)

    def part_arrives(step, part):
        for direction in lanes_of(step, part):
            ring(direction, step, part).wait_recv()
            if step < 4 and direction in lanes_of(step + 1, part):
                go(ring, direction, step + 1, part)
            if part in (0, 2):
                go(ext, part // 2, origin(direction, step))

    def settle(step):
        for slot in GROUPS[step]:
            for which in range(2):
                ext(which, slot).wait_recv()

    def happen(step, table):
        for at, calls in table.items():
            @pl.when(step == at)
            def run(calls=calls):
                for fn, *args in calls:
                    fn(*args)

    def swap_y():
        return remote(y_ref, y2.at[1], ys.at[0], ys.at[1], z_at(inner))

    go(cross)
    go(ext, 0, OWN)
    start_part(0)
    go(swap_y)

    def project(job, half):
        pair = lax.rem(job, 4)
        rows = w_all[pl.ds(2 * pair, 2), pl.ds(pl.multiple_of(half * HALF, HALF), HALF)]
        return jnp.dot(
            rows.reshape(2 * HALF, WIDTH), y2[lax.div(job, 4)], preferred_element_type=F32
        )

    def swap(job):
        return remote(ta.at[job], sa.at[job], as1.at[job], ar1.at[job], sibling)

    def give(job):
        ta[job] = project(job, 1 - p).astype(BF16)
        swap(job).start()

    def scatter(job, step):
        to = lax.rem(x + step, CHIPS)
        return remote(
            qa.at[job, to], rb.at[job, step - 1], bs.at[job, step - 1], br.at[job, step - 1],
            {"chan": 2 * to + p},
        )

    def take(job):
        got = project(job, p)
        swap(job).wait_recv()
        got = (got + sa[job].astype(F32)).astype(BF16)
        for i in range(2):
            for chip in range(CHIPS):
                at = HALF * i + PIECE * chip
                qa[job, chip, PIECE * i : PIECE * (i + 1)] = got[at : at + PIECE]
        for step in (2, 1, 3):
            scatter(job, step).start()

    def columns(z_here, outer_here, chip, core):
        first = jnp.where(core == 0, 0, outer_here)
        second = jnp.where(core == 0, outer_here + 4, 4)
        shard = lax.rem(z_here + jnp.where(chip < 2, first, second) + 2 * RING, RING)
        at = shard * (2 * PIECE) + lax.rem(chip, 2) * PIECE
        return out_ref.at[pl.ds(pl.multiple_of(at, PIECE), PIECE)]

    def target_of(job, i):
        slot = 2 * lax.rem(job, 4) + i
        off = lax.div(slot + 1, 2) * (2 * lax.rem(slot, 2) - 1)
        return lax.rem(y + off + RING, RING)

    def delivery(job, i):
        tokens = lax.div(job, 4)
        to = {"seq": y * RING + lax.rem(z + tokens * inner + RING, RING), "chan": target_of(job, i)}
        return remote(
            oa.at[job, i], columns(z, outer, x, p), cs.at[job, i], cr.at[tokens, x, p], to
        )

    def stays(job, i):
        return (job < 4) & (target_of(job, i) == c)

    def reduce(job):
        total = qa[job, x].astype(F32)
        for step in (1, 3, 2):
            scatter(job, step).wait_recv()
            total = total + rb[job, step - 1].astype(F32)
        total = total.astype(BF16)
        for i in range(2):
            oa[job, i] = total[PIECE * i : PIECE * (i + 1)]
        for i in range(2):
            @pl.when(stays(job, i))
            def keep():
                pltpu.make_async_copy(oa.at[job, i], columns(z, outer, x, p), cr.at[0, x, p]).start()

            @pl.when(jnp.logical_not(stays(job, i)))
            def post():
                delivery(job, i).start()

    near_arrives()
    cross_arrives()
    cross_ext_arrives()
    for part in range(4):
        part_arrives(1, part)
    part_arrives(2, 0)
    own.wait()
    mine.wait()

    def turn(n, carry):
        happen(n, {
            1: [(part_arrives, 2, 1)],
            2: [(part_arrives, 3, 1)],
            3: [(part_arrives, 4, 1)],
        })

        @pl.when((n >= 1) & (n < JOBS + 1))
        def second():
            take(n - 1)

        @pl.when(n >= 3)
        def third():
            reduce(n - 3)

        happen(n, {
            0: [(settle, 1)],
            1: [(part_arrives, 2, 2), (part_arrives, 2, 3), (part_arrives, 3, 0), (settle, 2)],
            2: [(part_arrives, 3, 2), (part_arrives, 3, 3), (part_arrives, 4, 0), (settle, 3)],
            3: [(part_arrives, 4, 2), (part_arrives, 4, 3), (settle, 4)],
            4: [(lambda: swap_y().wait_recv(),)],
        })

        @pl.when(n < JOBS)
        def first():
            give(n)

        return carry

    lax.fori_loop(0, JOBS + 3, turn, 0)

    for core in range(2):
        for chip in range(CHIPS):
            for tokens in range(2):
                here = columns(z + tokens * inner, outer * (1 - 2 * tokens), chip, core)
                remote(oa.at[0, 0], here, cs.at[0, 0], cr.at[tokens, chip, core], sibling).wait_recv()

    for make, args in started:
        make(*args).wait_send()

    def drain(job, carry):
        swap(job).wait_send()
        for step in (1, 2, 3):
            scatter(job, step).wait_send()
        for i in range(2):
            @pl.when(jnp.logical_not(stays(job, i)))
            def sent():
                delivery(job, i).wait_send()

        return carry

    lax.fori_loop(0, JOBS, drain, 0)


def local(qkv, feat_taps, long_filter, skip_gain, out_weight):
    anywhere = pl.BlockSpec(memory_space=pl.ANY)
    dma = pltpu.SemaphoreType.DMA
    grant = 56 * 2**20
    y = pl.pallas_call(
        mixer,
        out_shape=jax.ShapeDtypeStruct((WIDTH, ROWS), BF16),
        in_specs=[anywhere] * 4,
        out_specs=pl.BlockSpec(memory_space=pltpu.VMEM),
        scratch_shapes=[
            pltpu.VMEM((3, FTAPS, WIDTH), F32),
            pltpu.VMEM((WIDTH // GROUP, SPAN), BF16),
            pltpu.VMEM((1, WIDTH), F32),
            pltpu.VMEM((3, ROWS, WIDTH), BF16),
            pltpu.VMEM((3, HALO, WIDTH), BF16),
            pltpu.VMEM((3, STRIPS, PAD + TALL, LANES), F32),
            pltpu.VMEM((STRIPS, TALL, LANES), F32),
            pltpu.VMEM((STRIPS, TALL, LANES), F32),
            pltpu.VMEM((BLOCKS + 1, WIDTH, SPAN), BF16),
            pltpu.VMEM((BLOCKS, WIDTH, SPAN), F32),
            pltpu.VMEM((WIDTH, SPAN), F32),
            pltpu.VMEM((WIDTH // GROUP, SPAN), F32),
            pltpu.VMEM((WIDTH // GROUP, 2 * SPAN, SPAN), BF16),
            dma((6,)), dma((2,)), dma((2, 4)),
        ],
        compiler_params=pltpu.CompilerParams(
            collective_id=1, has_side_effects=True, vmem_limit_bytes=grant
        ),
    )(qkv, feat_taps, long_filter.T, skip_gain.reshape(1, WIDTH))
    return pl.pallas_call(
        projector,
        out_shape=jax.ShapeDtypeStruct((512, ROWS), BF16),
        in_specs=[anywhere] * 2,
        out_specs=anywhere,
        scratch_shapes=[
            pltpu.VMEM((RING, 8 * PIECE, WIDTH), BF16),
            pltpu.VMEM((2, WIDTH, ROWS), BF16),
            pltpu.VMEM((JOBS, 2 * HALF, ROWS), BF16),
            pltpu.VMEM((JOBS, 2 * HALF, ROWS), BF16),
            pltpu.VMEM((JOBS, CHIPS, 2 * PIECE, ROWS), BF16),
            pltpu.VMEM((JOBS, CHIPS - 1, 2 * PIECE, ROWS), BF16),
            pltpu.VMEM((JOBS, 2, PIECE, ROWS), BF16),
            dma((2,)), dma((2,)), dma((2, RING)), dma((2, RING)),
            dma((2, 4, 4)), dma((2, 4, 4)), dma((2,)),
            dma((JOBS,)), dma((JOBS,)), dma((JOBS, CHIPS - 1)), dma((JOBS, CHIPS - 1)),
            dma((JOBS, 2)), dma((2, CHIPS, 2)),
        ],
        compiler_params=pltpu.CompilerParams(
            collective_id=0, has_side_effects=True, vmem_limit_bytes=grant
        ),
    )(y, out_weight.T).T


def solution(mesh):
    return jax.shard_map(
        local,
        mesh=mesh,
        in_specs=(
            P(None, "seq", "chan"),
            P(None, None, "chan"),
            P(None, "chan"),
            P("chan"),
            P("chan", "seq"),
        ),
        out_specs=P("seq", "chan"),
        check_vma=False,
    )
```

```python
import jax
import jax.numpy as jnp
from jax import lax
from jax.experimental import pallas as pl
from jax.experimental.pallas import tpu as pltpu
from jax.sharding import PartitionSpec as P

MESH = pl.DeviceIdType.MESH
F32 = jnp.float32
BF16 = jnp.bfloat16

RING = 8
GROUP = 16
SPAN = 128
FTAPS = 7
ROWS = 384
WIDTH = 1024
BLOCKS = ROWS // SPAN
LANES = 128
STRIPS = WIDTH // LANES
PIECE = 32
HALO = 16
PAD = 8
PITCH = 49
SUBS = 8
TALL = PITCH * SUBS
BATCH = 8

OFF = (1, -1, 2, -2, 3, -3, 4, 0)
SLOT = {off: slot for slot, off in enumerate(OFF)}
PACKS = ((7, 8), (0, 2), (2, 4), (4, 6), (6, 7))
FAR_UP = (0, 1, 4)
OWN = SLOT[0]
FAR = SLOT[4]
PAIRS = 3


def origin(direction, step):
    return SLOT[4 if step == 4 else -direction * step]


def kernel(
    qkv_ref, taps_hbm, filt_hbm, skip_hbm, w_ref, out_ref,
    taps_ref, filt_ref, skip_ref,
    w_all, qkv_v, halo, ext_v, ub, qs, ut, qt, skt, hf, mats, yt,
    ta, sa, qa, tb, sb, qb, tc, sc, qc, ra, rb, rc,
    load_sem, own_sem, halo_sem, tail_sem,
    s1, r1, s2, r2, as1, ar1, as2, ar2, bs1, br1, bs2, br2, cs1, cr1, cs2, cr2,
):
    s = lax.axis_index("seq")
    c = lax.axis_index("chan")
    y = lax.div(s, RING)
    z = lax.rem(s, RING)
    x = lax.div(c, 2)
    p = lax.rem(c, 2)

    def y_at(d):
        return {"seq": lax.rem(y + d + RING, RING) * RING + z}

    def z_at(d):
        return {"seq": y * RING + lax.rem(z + d + RING, RING)}

    def seq_at(d):
        return {"seq": lax.rem(s + d + RING * RING, RING * RING)}

    sibling = {"chan": c + 1 - 2 * p}
    minor_at = (z_at, y_at)
    major_at = (y_at, z_at)
    started = []

    def remote(src, dst, send, recv, to):
        return pltpu.make_async_remote_copy(
            src_ref=src, dst_ref=dst, send_sem=send, recv_sem=recv, device_id=to, device_id_type=MESH
        )

    def go(make, *args):
        make(*args).start()
        if (make, args) not in started:
            started.append((make, args))

    loads = [
        pltpu.make_async_copy(qkv_ref.at[i], qkv_v.at[i], load_sem.at[i]) for i in (1, 2, 0)
    ]
    loads += [
        pltpu.make_async_copy(taps_hbm, taps_ref, load_sem.at[3]),
        pltpu.make_async_copy(skip_hbm, skip_ref, load_sem.at[5]),
        pltpu.make_async_copy(filt_hbm, filt_ref, load_sem.at[4]),
    ]
    own = [
        pltpu.make_async_copy(
            w_ref.at[PIECE * kind : PIECE * (kind + 1)], w_all.at[kind, OWN, OWN], own_sem.at[kind]
        )
        for kind in range(2)
    ]
    for copy in loads[::-1] + own:
        copy.start()

    barrier = pltpu.get_barrier_semaphore()
    greeted = [{"chan": lax.rem(c + d, 8)} for d in range(1, 8)]
    greeted += [z_at(1), z_at(-1), y_at(1), y_at(-1), seq_at(1), seq_at(-1)]
    for to in greeted:
        pl.semaphore_signal(barrier, inc=1, device_id=to, device_id_type=MESH)
    def toeplitz():
        loads[5].wait()
        hf[...] = filt_ref[...].astype(F32)

        def body(step, carry):
            row = lax.broadcasted_iota(jnp.int32, (SUBS, SPAN), 0)
            col = lax.broadcasted_iota(jnp.int32, (SUBS, SPAN), 1)
            for i in range(4):
                g = step * 4 + i
                base = jnp.broadcast_to(hf[pl.ds(g, 1), :], (SUBS, SPAN))
                for bit in (1, 2, 4):
                    base = jnp.where((row & bit) != 0, pltpu.roll(base, bit, 1), base)
                for pair in range(SPAN // (2 * SUBS)):
                    above, below = [], []
                    for k in (2 * pair, 2 * pair + 1):
                        turned = pltpu.roll(base, SUBS * k, 1) if k else base
                        under = row + SUBS * k > col
                        above.append(jnp.where(under, turned, 0.0))
                        below.append(jnp.where(under, 0.0, turned))
                    at = 2 * SUBS * pair
                    mats[g, at : at + 2 * SUBS] = jnp.concatenate(above, axis=0).astype(BF16)
                    mats[g, SPAN + at : SPAN + at + 2 * SUBS] = jnp.concatenate(below, axis=0).astype(BF16)
            return carry

        lax.fori_loop(0, 16, body, 0)

    def widen():
        for copy in loads[:5]:
            copy.wait()

        def body(strip, carry):
            at = pl.ds(pl.multiple_of(strip * LANES, LANES), LANES)
            for i in range(3):
                ext_v[i, strip, PAD : PAD + ROWS, :] = qkv_v[i, :, at].astype(F32)
                ext_v[i, strip, PAD + ROWS :, :] = jnp.zeros((TALL - ROWS, LANES), F32)
            skt[at, :] = jnp.broadcast_to(skip_ref[:, at], (LANES, LANES)).T
            return carry

        lax.fori_loop(0, STRIPS, body, 0)

    widen()
    pl.semaphore_wait(barrier, len(greeted))

    def first(kind, direction, step):
        lane = 0 if direction == 1 else 1
        into = origin(direction, step)
        if step == 1:
            src, dst = w_ref.at[PIECE * kind : PIECE * (kind + 1)], w_all.at[kind, OWN, into]
        elif step < 4:
            src, dst = w_all.at[kind, OWN, origin(direction, step - 1)], w_all.at[kind, OWN, into]
        else:
            half = pl.ds(lane * (PIECE // 2), PIECE // 2)
            src = w_all.at[kind, OWN, origin(direction, 3), half]
            dst = w_all.at[kind, OWN, into, half]
        at = kind, lane, step - 1
        return remote(src, dst, s1.at[at], r1.at[at], minor_at[kind](direction))

    def second(kind, direction, step, pack):
        lane = 0 if direction == 1 else 1
        lo, hi = PACKS[pack]
        into = origin(direction, step)
        if step == 1 and pack == 0:
            src, dst = w_ref.at[PIECE * kind : PIECE * (kind + 1)], w_all.at[kind, into, OWN]
        else:
            came = OWN if step == 1 else origin(direction, step - 1)
            src = w_all.at[kind, came, pl.ds(lo, hi - lo)]
            dst = w_all.at[kind, into, pl.ds(lo, hi - lo)]
        at = kind, lane, step - 1, pack
        return remote(src, dst, s2.at[at], r2.at[at], major_at[kind](direction))

    def lanes_of(step, pack):
        if step < 4:
            return (1, -1)
        return (1,) if pack in FAR_UP else (-1,)

    def first_arrives(step):
        for kind in range(2):
            for direction in (1, -1):
                first(kind, direction, step).wait_recv()
                if step < 4:
                    go(first, kind, direction, step + 1)
        for kind in range(2):
            for direction in (1, -1):
                go(second, kind, direction, 1, step)

    def second_arrives(step, pack):
        for kind in range(2):
            for direction in lanes_of(step, pack):
                second(kind, direction, step, pack).wait_recv()
                if step < 4 and direction in lanes_of(step + 1, pack):
                    go(second, kind, direction, step + 1, pack)

    events = [(2.9 + 11.7 * (k - 1) + 3.5 * (g + 1), second_arrives, (k, g)) for k in range(1, 5) for g in range(5)]
    events.sort(key=lambda e: e[0])

    def happen(step, table):
        for at, calls in table.items():
            @pl.when(step == at)
            def run(calls=calls):
                for fn, *args in calls:
                    fn(*args)

    def early(number):
        at, fn, args = events[number]
        seen.add(args)
        return fn, *args

    clock = [0.0]
    seen = set()

    def take_event():
        at, fn, args = events.pop(0)
        fn(*args)
        seen.add(args)
        clock[0] = max(clock[0], at)

    def work(cost, fn, *args):
        while events and events[0][0] <= clock[0]:
            take_event()
        fn(*args)
        clock[0] += cost

    def need(step):
        wanted = {(step, g) for g in range(5)}
        while not wanted <= seen:
            take_event()

    def halo_copy():
        return remote(
            qkv_ref.at[:, ROWS - HALO : ROWS], halo, halo_sem.at[0], halo_sem.at[1], seq_at(1)
        )

    go(halo_copy)
    for kind in range(2):
        for direction in (1, -1):
            go(first, kind, direction, 1)
    for kind in range(2):
        for direction in (1, -1):
            go(second, kind, direction, 1, 0)

    def halo_arrives():
        halo_copy().wait_recv()

        def body(strip, carry):
            at = pl.ds(pl.multiple_of(strip * LANES, LANES), LANES)
            for i in range(3):
                before = halo[i, :, at].astype(F32)[HALO - PAD :]
                ext_v[i, strip, :PAD, :] = jnp.where(s == 0, 0.0, before)
            return carry

        lax.fori_loop(0, STRIPS, body, 0)

    def features(strip):
        at = pl.ds(pl.multiple_of(strip * LANES, LANES), LANES)
        taps = [
            [jnp.broadcast_to(taps_ref[i, j : j + 1, at], (SUBS, LANES)) for j in range(FTAPS)]
            for i in range(3)
        ]

        def load(i, r):
            return ext_v[i, strip, pl.ds(PAD + r, SUBS, stride=PITCH), :]

        def line(i, window):
            total = taps[i][0] * window[-1]
            for j in range(1, FTAPS):
                total = total + taps[i][j] * window[-1 - j]
            return total

        def some(turn, windows):
            windows = [list(w) for w in windows]
            for step in range(FTAPS):
                r = turn * FTAPS + step
                found = []
                for i in range(3):
                    windows[i] = windows[i][1 - FTAPS :] + [load(i, r)]
                    found.append(line(i, windows[i]))
                ub[strip, pl.ds(r, SUBS, stride=PITCH), :] = found[1] * found[2]
                qs[strip, pl.ds(r, SUBS, stride=PITCH), :] = found[0]
            return tuple(tuple(w[1 - FTAPS :]) for w in windows)

        start = tuple(tuple(load(i, r) for r in range(1 - FTAPS, 0)) for i in range(3))
        lax.fori_loop(0, PITCH // FTAPS, some, start)
        for b in range(BLOCKS):
            ut[b + 1, at, :] = ub[strip, SPAN * b : SPAN * (b + 1), :].T.astype(BF16)
            qt[b, at, :] = qs[strip, SPAN * b : SPAN * (b + 1), :].T

    def tail(quarter):
        at = pl.ds(pl.multiple_of(quarter * (WIDTH // 4), WIDTH // 4), WIDTH // 4)
        return remote(
            ut.at[BLOCKS, at], ut.at[0, at], tail_sem.at[0, quarter], tail_sem.at[1, quarter], seq_at(1)
        )

    def tail_arrives(quarter):
        tail(quarter).wait_recv()

        @pl.when(s == 0)
        def clear():
            at = pl.ds(pl.multiple_of(quarter * (WIDTH // 4), WIDTH // 4), WIDTH // 4)
            ut[0, at] = jnp.zeros((WIDTH // 4, SPAN), BF16)

    def conv(step):
        base = step * BATCH
        spots = [pl.ds(pl.multiple_of((base + i) * GROUP, GROUP), GROUP) for i in range(BATCH)]
        parts = [[ut[b, at, :] for b in range(BLOCKS + 1)] for at in spots]
        mixed = []
        for i in range(BATCH):
            window = [jnp.concatenate(parts[i][b : b + 2], axis=1) for b in range(BLOCKS)]
            mixed.append(
                jnp.dot(jnp.concatenate(window, axis=0), mats[base + i], preferred_element_type=F32)
            )
        found = []
        for i, at in enumerate(spots):
            for b in range(BLOCKS):
                field = mixed[i][GROUP * b : GROUP * (b + 1)] + skt[at, :] * parts[i][b + 1].astype(F32)
                found.append((qt[b, at, :] * field).astype(BF16))
        for i, at in enumerate(spots):
            for b in range(BLOCKS):
                yt[at, SPAN * b : SPAN * (b + 1)] = found[BLOCKS * i + b]

    def project(pieces):
        rows = jnp.concatenate(pieces, axis=0) if len(pieces) > 1 else pieces[0]
        return jnp.dot(rows, yt[...], preferred_element_type=F32)

    def two(kind, major, batch, half):
        return w_all[kind, major, pl.ds(4 * batch + 2 * half, 2)].reshape(2 * PIECE, WIDTH)

    def four(kind, major, half):
        return [two(kind, major, batch, half) for batch in range(2)]

    def target(slot):
        return lax.rem(y + OFF[slot] + RING, RING)

    delivered = []

    def deliver(src, dst, send, recv, to):
        copy = remote(src, dst, send, recv, {"chan": to})

        @pl.when(to == c)
        def keep():
            pltpu.make_async_copy(src, dst, recv).start()

        @pl.when(to != c)
        def post():
            copy.start()

        delivered.append((to, copy))

    def a_swap(slot):
        return remote(ta.at[slot], sa.at[slot], as1.at[slot], ar1.at[slot], sibling)

    def a_first(slots):
        got = project(sum([four(0, m, 1 - p) for m in slots], [])).astype(BF16)
        for i, m in enumerate(slots):
            ta[m] = got[4 * PIECE * i : 4 * PIECE * (i + 1)]
            go(a_swap, m)

    def a_second(slots):
        got = project(sum([four(0, m, p) for m in slots], []))
        for i, m in enumerate(slots):
            a_swap(m).wait_recv()
            qa[m] = (got[4 * PIECE * i : 4 * PIECE * (i + 1)] + sa[m].astype(F32)).astype(BF16)
            deliver(qa.at[m], ra.at[x, p], as2.at[m, 0], ar2.at[x, p], target(m))

    def b_swap(turn):
        return remote(tb.at[turn], sb.at[turn], bs1.at[turn], br1.at[turn], sibling)

    def b_rows(turn, half):
        return w_all[1, 2 * turn + half].reshape(RING * PIECE, WIDTH)

    def b_first(turn):
        tb[turn] = project([b_rows(turn, 1 - p)]).astype(BF16)
        go(b_swap, turn)

    def b_second(turn):
        got = project([b_rows(turn, p)])
        b_swap(turn).wait_recv()
        qb[turn] = (got + sb[turn].astype(F32)).astype(BF16)
        for m in range(RING):
            deliver(
                qb.at[turn, PIECE * m : PIECE * (m + 1)], rb.at[turn, x, p],
                bs2.at[turn, m], br2.at[turn, x, p], target(m),
            )

    def o_swap(part):
        at = pl.ds(4 * PIECE * part, 4 * PIECE)
        return remote(tc.at[at], sc.at[at], cs1.at[part], cr1.at[part], sibling)

    def o_post(single, batch, at):
        for i in range(2):
            to = lax.rem(y + jnp.where(p == 0, OFF[4 * batch + i], OFF[4 * batch + 2 + i]) + RING, RING)
            deliver(
                qc.at[pl.ds(at + PIECE * i, PIECE)], rc.at[single, x],
                cs2.at[single, batch, i], cr2.at[single, x], to,
            )

    def o_first():
        tc[: 4 * PIECE] = project(four(1, OWN, 1 - p)).astype(BF16)
        go(o_swap, 0)

    def o_second():
        got = project(four(1, OWN, p))
        o_swap(0).wait_recv()
        qc[: 4 * PIECE] = (got + sc[: 4 * PIECE].astype(F32)).astype(BF16)
        for batch in range(2):
            o_post(0, batch, 2 * PIECE * batch)

    def far_first(batch):
        at = pl.ds(4 * PIECE * (batch + 1), 4 * PIECE)
        tc[at] = project([two(0, FAR, batch, 1 - p), two(1, FAR, batch, 1 - p)]).astype(BF16)
        go(o_swap, batch + 1)

    def far_second(batch):
        base = 4 * PIECE * (batch + 1)
        got = project([two(0, FAR, batch, p), two(1, FAR, batch, p)])
        o_swap(batch + 1).wait_recv()
        qc[base : base + 4 * PIECE] = (got + sc[base : base + 4 * PIECE].astype(F32)).astype(BF16)
        deliver(
            qc.at[base : base + 2 * PIECE], ra.at[x, p, pl.ds(2 * PIECE * batch, 2 * PIECE)],
            as2.at[FAR, batch], ar2.at[x, p], target(FAR),
        )
        o_post(1, batch, base + 2 * PIECE)

    def own_wait():
        for copy in own:
            copy.wait()

    def place(kind, slot, rows):
        at = lax.rem(z + OFF[slot] + RING, RING) * (2 * PIECE) + kind * PIECE
        out_ref[pl.ds(pl.multiple_of(at, PIECE), PIECE), :] = rows.astype(BF16)

    def total(refs):
        found = None
        for ref in refs:
            term = ref[...].astype(F32)
            found = term if found is None else found + term
        return found

    def arrived(ref, sem):
        remote(ref, ref, cs2.at[0, 0, 0], sem, sibling).wait_recv()

    def pair_sums(turn):
        for half in range(2):
            for chip in range(4):
                arrived(rb.at[turn, chip, half], br2.at[turn, chip, half])
            place(1, 2 * turn + half, total([rb.at[turn, chip, half] for chip in range(4)]))

    def single_sums(single, slot):
        for chip in range(4):
            arrived(rc.at[single, chip], cr2.at[single, chip])
        place(1, slot, total([rc.at[single, chip] for chip in range(4)]))

    def row_sums():
        for half in range(2):
            for chip in range(4):
                arrived(ra.at[chip, half], ar2.at[chip, half])
            found = total([ra.at[chip, half] for chip in range(4)])
            for i in range(4):
                slot = 4 * (i // 2) + 2 * half + i % 2
                place(0, slot, found[PIECE * i : PIECE * (i + 1)])

    toeplitz()
    first_arrives(1)
    halo_arrives()

    def feature_strip(strip, carry):
        features(strip)

        @pl.when(lax.rem(strip, 2) == 1)
        def send():
            tail(lax.div(strip, 2)).start()

        happen(strip, {1: [(first_arrives, 2)], 4: [(first_arrives, 3)], 6: [early(0)]})
        return carry

    lax.fori_loop(0, STRIPS, feature_strip, 0)
    first_arrives(4)

    def conv_step(step, carry):
        @pl.when(lax.rem(step, 2) == 0)
        def wait():
            tail_arrives(lax.div(step, 2))

        conv(step)
        happen(step, {1: [early(1)], 5: [early(2)]})
        return carry

    lax.fori_loop(0, 64 // BATCH, conv_step, 0)
    del events[:3]
    clock[0] = 15.0
    work(0.1, own_wait)
    work(0.6, a_first, (OWN,))
    work(0.6, o_first)
    work(0.6, a_second, (OWN,))
    work(0.6, o_second)
    for k in (1, 2, 3):
        low, high = SLOT[k], SLOT[-k]
        need(k)
        work(1.0, a_first, (low, high))
        work(1.0, b_first, k - 1)
        work(1.0, a_second, (low, high))
        work(1.2, b_second, k - 1)
    while not {(4, g) for g in (0, 1, 2)} <= seen:
        take_event()
    far_first(0)
    far_second(0)
    need(4)
    far_first(1)
    pair_sums(0)
    pair_sums(1)
    single_sums(0, OWN)
    far_second(1)
    pair_sums(2)
    single_sums(1, FAR)
    row_sums()

    for make, args in started:
        make(*args).wait_send()

    def drain_tail(quarter, carry):
        tail(quarter).wait_send()
        return carry

    lax.fori_loop(0, 4, drain_tail, 0)
    for to, copy in delivered:
        @pl.when(to != c)
        def drain(copy=copy):
            copy.wait_send()


def local(qkv, feat_taps, long_filter, skip_gain, out_weight):
    vmem = pl.BlockSpec(memory_space=pltpu.VMEM)
    anywhere = pl.BlockSpec(memory_space=pl.ANY)
    dma = pltpu.SemaphoreType.DMA
    half_piece = (4 * PIECE, ROWS)
    return pl.pallas_call(
        kernel,
        out_shape=jax.ShapeDtypeStruct((512, ROWS), BF16),
        in_specs=[anywhere] * 5,
        out_specs=vmem,
        scratch_shapes=[
            pltpu.VMEM((3, FTAPS, WIDTH), F32),
            pltpu.VMEM((WIDTH // GROUP, SPAN), BF16),
            pltpu.VMEM((1, WIDTH), F32),
            pltpu.VMEM((2, RING, RING, PIECE, WIDTH), BF16),
            pltpu.VMEM((3, ROWS, WIDTH), BF16),
            pltpu.VMEM((3, HALO, WIDTH), BF16),
            pltpu.VMEM((3, STRIPS, PAD + TALL, LANES), F32),
            pltpu.VMEM((STRIPS, TALL, LANES), F32),
            pltpu.VMEM((STRIPS, TALL, LANES), F32),
            pltpu.VMEM((BLOCKS + 1, WIDTH, SPAN), BF16),
            pltpu.VMEM((BLOCKS, WIDTH, SPAN), F32),
            pltpu.VMEM((WIDTH, SPAN), F32),
            pltpu.VMEM((WIDTH // GROUP, SPAN), F32),
            pltpu.VMEM((WIDTH // GROUP, 2 * SPAN, SPAN), BF16),
            pltpu.VMEM((WIDTH, ROWS), BF16),
            pltpu.VMEM((RING,) + half_piece, BF16),
            pltpu.VMEM((RING,) + half_piece, BF16),
            pltpu.VMEM((RING,) + half_piece, BF16),
            pltpu.VMEM((PAIRS, RING * PIECE, ROWS), BF16),
            pltpu.VMEM((PAIRS, RING * PIECE, ROWS), BF16),
            pltpu.VMEM((PAIRS, RING * PIECE, ROWS), BF16),
            pltpu.VMEM((12 * PIECE, ROWS), BF16),
            pltpu.VMEM((12 * PIECE, ROWS), BF16),
            pltpu.VMEM((12 * PIECE, ROWS), BF16),
            pltpu.VMEM((4, 2) + half_piece, BF16),
            pltpu.VMEM((PAIRS, 4, 2, PIECE, ROWS), BF16),
            pltpu.VMEM((2, 4, PIECE, ROWS), BF16),
            dma((6,)), dma((2,)), dma((2,)), dma((2, 4)),
            dma((2, 2, 4)), dma((2, 2, 4)),
            dma((2, 2, 4, 5)), dma((2, 2, 4, 5)),
            dma((RING,)), dma((RING,)), dma((RING, 2)), dma((4, 2)),
            dma((PAIRS,)), dma((PAIRS,)), dma((PAIRS, RING)), dma((PAIRS, 4, 2)),
            dma((3,)), dma((3,)), dma((2, 2, 2)), dma((2, 4)),
        ],
        compiler_params=pltpu.CompilerParams(
            collective_id=0, has_side_effects=True, vmem_limit_bytes=56 * 2**20
        ),
    )(qkv, feat_taps, long_filter.T, skip_gain.reshape(1, WIDTH), out_weight.T).T


def solution(mesh):
    return jax.shard_map(
        local,
        mesh=mesh,
        in_specs=(
            P(None, "seq", "chan"),
            P(None, None, "chan"),
            P(None, "chan"),
            P("chan"),
            P("chan", "seq"),
        ),
        out_specs=P("seq", "chan"),
        check_vma=False,
    )
```

```python
import jax
import jax.numpy as jnp
from jax import lax
from jax.experimental import pallas as pl
from jax.experimental.pallas import tpu as pltpu
from jax.sharding import PartitionSpec as P

MESH = pl.DeviceIdType.MESH
F32 = jnp.float32
BF16 = jnp.bfloat16

RING = 8
GROUP = 16
SPAN = 128
FTAPS = 7
ROWS = 384
WIDTH = 1024
BLOCKS = ROWS // SPAN
LANES = 128
STRIPS = WIDTH // LANES
PIECE = 32
HALO = 16
PAD = 8
PITCH = 49
SUBS = 8
TALL = PITCH * SUBS
BATCH = 8

OFF = (1, -1, 2, -2, 3, -3, 4, 0)
SLOT = {off: slot for slot, off in enumerate(OFF)}
PACKS = ((7, 8), (0, 2), (2, 4), (4, 6), (6, 7))
FAR_UP = (0, 1, 4)
OWN = SLOT[0]
FAR = SLOT[4]
PAIRS = 3


def origin(direction, step):
    return SLOT[4 if step == 4 else -direction * step]


def kernel(
    qkv_ref, taps_hbm, filt_hbm, skip_hbm, w_ref, out_ref,
    taps_ref, filt_ref, skip_ref,
    w_all, qkv_v, halo, ext_v, ub, qs, ut, qt, skt, hf, mats, yt,
    ta, sa, qa, tb, sb, qb, tc, sc, qc, ra, rb, rc,
    load_sem, own_sem, halo_sem, tail_sem,
    s1, r1, s2, r2, as1, ar1, as2, ar2, bs1, br1, bs2, br2, cs1, cr1, cs2, cr2,
):
    s = lax.axis_index("seq")
    c = lax.axis_index("chan")
    y = lax.div(s, RING)
    z = lax.rem(s, RING)
    x = lax.div(c, 2)
    p = lax.rem(c, 2)

    def y_at(d):
        return {"seq": lax.rem(y + d + RING, RING) * RING + z}

    def z_at(d):
        return {"seq": y * RING + lax.rem(z + d + RING, RING)}

    def seq_at(d):
        return {"seq": lax.rem(s + d + RING * RING, RING * RING)}

    sibling = {"chan": c + 1 - 2 * p}
    minor_at = (z_at, y_at)
    major_at = (y_at, z_at)
    started = []

    def remote(src, dst, send, recv, to):
        return pltpu.make_async_remote_copy(
            src_ref=src, dst_ref=dst, send_sem=send, recv_sem=recv, device_id=to, device_id_type=MESH
        )

    def go(make, *args):
        make(*args).start()
        if (make, args) not in started:
            started.append((make, args))

    loads = [
        pltpu.make_async_copy(qkv_ref.at[i], qkv_v.at[i], load_sem.at[i]) for i in (1, 2, 0)
    ]
    loads += [
        pltpu.make_async_copy(taps_hbm, taps_ref, load_sem.at[3]),
        pltpu.make_async_copy(skip_hbm, skip_ref, load_sem.at[5]),
        pltpu.make_async_copy(filt_hbm, filt_ref, load_sem.at[4]),
    ]
    own = [
        pltpu.make_async_copy(
            w_ref.at[PIECE * kind : PIECE * (kind + 1)], w_all.at[kind, OWN, OWN], own_sem.at[kind]
        )
        for kind in range(2)
    ]
    for copy in loads[::-1] + own:
        copy.start()

    barrier = pltpu.get_barrier_semaphore()
    greeted = [{"chan": lax.rem(c + d, 8)} for d in range(1, 8)]
    greeted += [z_at(1), z_at(-1), y_at(1), y_at(-1), seq_at(1), seq_at(-1)]
    for to in greeted:
        pl.semaphore_signal(barrier, inc=1, device_id=to, device_id_type=MESH)
    def toeplitz(low, high):
        def body(step, carry):
            row = lax.broadcasted_iota(jnp.int32, (SUBS, SPAN), 0)
            col = lax.broadcasted_iota(jnp.int32, (SUBS, SPAN), 1)
            for i in range(4):
                g = step * 4 + i
                base = jnp.broadcast_to(hf[pl.ds(g, 1), :], (SUBS, SPAN))
                for bit in (1, 2, 4):
                    base = jnp.where((row & bit) != 0, pltpu.roll(base, bit, 1), base)
                for pair in range(SPAN // (2 * SUBS)):
                    above, below = [], []
                    for k in (2 * pair, 2 * pair + 1):
                        turned = pltpu.roll(base, SUBS * k, 1) if k else base
                        under = row + SUBS * k > col
                        above.append(jnp.where(under, turned, 0.0))
                        below.append(jnp.where(under, 0.0, turned))
                    at = 2 * SUBS * pair
                    mats[g, at : at + 2 * SUBS] = jnp.concatenate(above, axis=0).astype(BF16)
                    mats[g, SPAN + at : SPAN + at + 2 * SUBS] = jnp.concatenate(below, axis=0).astype(BF16)
            return carry

        lax.fori_loop(low, high, body, 0)

    def widen():
        for copy in loads[:5]:
            copy.wait()

        def body(strip, carry):
            at = pl.ds(pl.multiple_of(strip * LANES, LANES), LANES)
            for i in range(3):
                ext_v[i, strip, PAD : PAD + ROWS, :] = qkv_v[i, :, at].astype(F32)
                ext_v[i, strip, PAD + ROWS :, :] = jnp.zeros((TALL - ROWS, LANES), F32)
            skt[at, :] = jnp.broadcast_to(skip_ref[:, at], (LANES, LANES)).T
            return carry

        lax.fori_loop(0, STRIPS, body, 0)

    pl.semaphore_wait(barrier, len(greeted))

    def first(kind, direction, step):
        lane = 0 if direction == 1 else 1
        into = origin(direction, step)
        if step == 1:
            src, dst = w_ref.at[PIECE * kind : PIECE * (kind + 1)], w_all.at[kind, OWN, into]
        elif step < 4:
            src, dst = w_all.at[kind, OWN, origin(direction, step - 1)], w_all.at[kind, OWN, into]
        else:
            half = pl.ds(lane * (PIECE // 2), PIECE // 2)
            src = w_all.at[kind, OWN, origin(direction, 3), half]
            dst = w_all.at[kind, OWN, into, half]
        at = kind, lane, step - 1
        return remote(src, dst, s1.at[at], r1.at[at], minor_at[kind](direction))

    def second(kind, direction, step, pack):
        lane = 0 if direction == 1 else 1
        lo, hi = PACKS[pack]
        into = origin(direction, step)
        if step == 1 and pack == 0:
            src, dst = w_ref.at[PIECE * kind : PIECE * (kind + 1)], w_all.at[kind, into, OWN]
        else:
            came = OWN if step == 1 else origin(direction, step - 1)
            src = w_all.at[kind, came, pl.ds(lo, hi - lo)]
            dst = w_all.at[kind, into, pl.ds(lo, hi - lo)]
        at = kind, lane, step - 1, pack
        return remote(src, dst, s2.at[at], r2.at[at], major_at[kind](direction))

    def lanes_of(step, pack):
        if step < 4:
            return (1, -1)
        return (1,) if pack in FAR_UP else (-1,)

    def first_arrives(step):
        for kind in range(2):
            for direction in (1, -1):
                first(kind, direction, step).wait_recv()
                if step < 4:
                    go(first, kind, direction, step + 1)
        for kind in range(2):
            for direction in (1, -1):
                go(second, kind, direction, 1, step)

    def second_arrives(step, pack):
        for kind in range(2):
            for direction in lanes_of(step, pack):
                second(kind, direction, step, pack).wait_recv()
                if step < 4 and direction in lanes_of(step + 1, pack):
                    go(second, kind, direction, step + 1, pack)

    events = [(2.9 + 11.7 * (k - 1) + 3.5 * (g + 1), second_arrives, (k, g)) for k in range(1, 5) for g in range(5)]
    events.sort(key=lambda e: e[0])

    def happen(step, table):
        for at, calls in table.items():
            @pl.when(step == at)
            def run(calls=calls):
                for fn, *args in calls:
                    fn(*args)

    def early(number):
        at, fn, args = events[number]
        seen.add(args)
        return fn, *args

    clock = [0.0]
    seen = set()

    def take_event():
        at, fn, args = events.pop(0)
        fn(*args)
        seen.add(args)
        clock[0] = max(clock[0], at)

    def work(cost, fn, *args):
        while events and events[0][0] <= clock[0]:
            take_event()
        fn(*args)
        clock[0] += cost

    def need(step):
        wanted = {(step, g) for g in range(5)}
        while not wanted <= seen:
            take_event()

    def halo_copy():
        return remote(
            qkv_ref.at[:, ROWS - HALO : ROWS], halo, halo_sem.at[0], halo_sem.at[1], seq_at(1)
        )

    go(halo_copy)
    for kind in range(2):
        for direction in (1, -1):
            go(first, kind, direction, 1)
    for kind in range(2):
        for direction in (1, -1):
            go(second, kind, direction, 1, 0)

    def halo_arrives():
        halo_copy().wait_recv()

        def body(strip, carry):
            at = pl.ds(pl.multiple_of(strip * LANES, LANES), LANES)
            for i in range(3):
                before = halo[i, :, at].astype(F32)[HALO - PAD :]
                ext_v[i, strip, :PAD, :] = jnp.where(s == 0, 0.0, before)
            return carry

        lax.fori_loop(0, STRIPS, body, 0)

    def features(strip):
        at = pl.ds(pl.multiple_of(strip * LANES, LANES), LANES)
        taps = [
            [jnp.broadcast_to(taps_ref[i, j : j + 1, at], (SUBS, LANES)) for j in range(FTAPS)]
            for i in range(3)
        ]

        def load(i, r):
            return ext_v[i, strip, pl.ds(PAD + r, SUBS, stride=PITCH), :]

        def line(i, window):
            total = taps[i][0] * window[-1]
            for j in range(1, FTAPS):
                total = total + taps[i][j] * window[-1 - j]
            return total

        def some(turn, windows):
            windows = [list(w) for w in windows]
            for step in range(FTAPS):
                r = turn * FTAPS + step
                found = []
                for i in range(3):
                    windows[i] = windows[i][1 - FTAPS :] + [load(i, r)]
                    found.append(line(i, windows[i]))
                ub[strip, pl.ds(r, SUBS, stride=PITCH), :] = found[1] * found[2]
                qs[strip, pl.ds(r, SUBS, stride=PITCH), :] = found[0]
            return tuple(tuple(w[1 - FTAPS :]) for w in windows)

        start = tuple(tuple(load(i, r) for r in range(1 - FTAPS, 0)) for i in range(3))
        lax.fori_loop(0, PITCH // FTAPS, some, start)
        for b in range(BLOCKS):
            ut[b + 1, at, :] = ub[strip, SPAN * b : SPAN * (b + 1), :].T.astype(BF16)
            qt[b, at, :] = qs[strip, SPAN * b : SPAN * (b + 1), :].T

    def tail(quarter):
        at = pl.ds(pl.multiple_of(quarter * (WIDTH // 4), WIDTH // 4), WIDTH // 4)
        return remote(
            ut.at[BLOCKS, at], ut.at[0, at], tail_sem.at[0, quarter], tail_sem.at[1, quarter], seq_at(1)
        )

    def tail_arrives(quarter):
        tail(quarter).wait_recv()

        @pl.when(s == 0)
        def clear():
            at = pl.ds(pl.multiple_of(quarter * (WIDTH // 4), WIDTH // 4), WIDTH // 4)
            ut[0, at] = jnp.zeros((WIDTH // 4, SPAN), BF16)

    def conv(step):
        base = step * BATCH
        spots = [pl.ds(pl.multiple_of((base + i) * GROUP, GROUP), GROUP) for i in range(BATCH)]
        parts = [[ut[b, at, :] for b in range(BLOCKS + 1)] for at in spots]
        mixed = []
        for i in range(BATCH):
            window = [jnp.concatenate(parts[i][b : b + 2], axis=1) for b in range(BLOCKS)]
            mixed.append(
                jnp.dot(jnp.concatenate(window, axis=0), mats[base + i], preferred_element_type=F32)
            )
        found = []
        for i, at in enumerate(spots):
            for b in range(BLOCKS):
                field = mixed[i][GROUP * b : GROUP * (b + 1)] + skt[at, :] * parts[i][b + 1].astype(F32)
                found.append((qt[b, at, :] * field).astype(BF16))
        for i, at in enumerate(spots):
            for b in range(BLOCKS):
                yt[at, SPAN * b : SPAN * (b + 1)] = found[BLOCKS * i + b]

    def project(pieces):
        rows = jnp.concatenate(pieces, axis=0) if len(pieces) > 1 else pieces[0]
        return jnp.dot(rows, yt[...], preferred_element_type=F32)

    def two(kind, major, batch, half):
        return w_all[kind, major, pl.ds(4 * batch + 2 * half, 2)].reshape(2 * PIECE, WIDTH)

    def four(kind, major, half):
        return [two(kind, major, batch, half) for batch in range(2)]

    def target(slot):
        return lax.rem(y + OFF[slot] + RING, RING)

    delivered = []

    def deliver(src, dst, send, recv, to):
        copy = remote(src, dst, send, recv, {"chan": to})

        @pl.when(to == c)
        def keep():
            pltpu.make_async_copy(src, dst, recv).start()

        @pl.when(to != c)
        def post():
            copy.start()

        delivered.append((to, copy))

    def a_swap(slot):
        return remote(ta.at[slot], sa.at[slot], as1.at[slot], ar1.at[slot], sibling)

    def a_first(slots):
        got = project(sum([four(0, m, 1 - p) for m in slots], [])).astype(BF16)
        for i, m in enumerate(slots):
            ta[m] = got[4 * PIECE * i : 4 * PIECE * (i + 1)]
            go(a_swap, m)

    def a_second(slots):
        got = project(sum([four(0, m, p) for m in slots], []))
        for i, m in enumerate(slots):
            a_swap(m).wait_recv()
            qa[m] = (got[4 * PIECE * i : 4 * PIECE * (i + 1)] + sa[m].astype(F32)).astype(BF16)
            deliver(qa.at[m], ra.at[x, p], as2.at[m, 0], ar2.at[x, p], target(m))

    def b_swap(turn):
        return remote(tb.at[turn], sb.at[turn], bs1.at[turn], br1.at[turn], sibling)

    def b_rows(turn, half):
        return w_all[1, 2 * turn + half].reshape(RING * PIECE, WIDTH)

    def b_first(turn):
        tb[turn] = project([b_rows(turn, 1 - p)]).astype(BF16)
        go(b_swap, turn)

    def b_second(turn):
        got = project([b_rows(turn, p)])
        b_swap(turn).wait_recv()
        qb[turn] = (got + sb[turn].astype(F32)).astype(BF16)
        for m in range(RING):
            deliver(
                qb.at[turn, PIECE * m : PIECE * (m + 1)], rb.at[turn, x, p],
                bs2.at[turn, m], br2.at[turn, x, p], target(m),
            )

    def o_swap(part):
        at = pl.ds(4 * PIECE * part, 4 * PIECE)
        return remote(tc.at[at], sc.at[at], cs1.at[part], cr1.at[part], sibling)

    def o_post(single, batch, at):
        for i in range(2):
            to = lax.rem(y + jnp.where(p == 0, OFF[4 * batch + i], OFF[4 * batch + 2 + i]) + RING, RING)
            deliver(
                qc.at[pl.ds(at + PIECE * i, PIECE)], rc.at[single, x],
                cs2.at[single, batch, i], cr2.at[single, x], to,
            )

    def o_first():
        tc[: 4 * PIECE] = project(four(1, OWN, 1 - p)).astype(BF16)
        go(o_swap, 0)

    def o_second():
        got = project(four(1, OWN, p))
        o_swap(0).wait_recv()
        qc[: 4 * PIECE] = (got + sc[: 4 * PIECE].astype(F32)).astype(BF16)
        for batch in range(2):
            o_post(0, batch, 2 * PIECE * batch)

    def far_first(batch):
        at = pl.ds(4 * PIECE * (batch + 1), 4 * PIECE)
        tc[at] = project([two(0, FAR, batch, 1 - p), two(1, FAR, batch, 1 - p)]).astype(BF16)
        go(o_swap, batch + 1)

    def far_second(batch):
        base = 4 * PIECE * (batch + 1)
        got = project([two(0, FAR, batch, p), two(1, FAR, batch, p)])
        o_swap(batch + 1).wait_recv()
        qc[base : base + 4 * PIECE] = (got + sc[base : base + 4 * PIECE].astype(F32)).astype(BF16)
        deliver(
            qc.at[base : base + 2 * PIECE], ra.at[x, p, pl.ds(2 * PIECE * batch, 2 * PIECE)],
            as2.at[FAR, batch], ar2.at[x, p], target(FAR),
        )
        o_post(1, batch, base + 2 * PIECE)

    def own_wait():
        for copy in own:
            copy.wait()

    def place(kind, slot, rows):
        at = lax.rem(z + OFF[slot] + RING, RING) * (2 * PIECE) + kind * PIECE
        out_ref[pl.ds(pl.multiple_of(at, PIECE), PIECE), :] = rows.astype(BF16)

    def total(refs):
        found = None
        for ref in refs:
            term = ref[...].astype(F32)
            found = term if found is None else found + term
        return found

    def arrived(ref, sem):
        remote(ref, ref, cs2.at[0, 0, 0], sem, sibling).wait_recv()

    def pair_sums(turn):
        for half in range(2):
            for chip in range(4):
                arrived(rb.at[turn, chip, half], br2.at[turn, chip, half])
            place(1, 2 * turn + half, total([rb.at[turn, chip, half] for chip in range(4)]))

    def single_sums(single, slot):
        for chip in range(4):
            arrived(rc.at[single, chip], cr2.at[single, chip])
        place(1, slot, total([rc.at[single, chip] for chip in range(4)]))

    def row_sums():
        for half in range(2):
            for chip in range(4):
                arrived(ra.at[chip, half], ar2.at[chip, half])
            found = total([ra.at[chip, half] for chip in range(4)])
            for i in range(4):
                slot = 4 * (i // 2) + 2 * half + i % 2
                place(0, slot, found[PIECE * i : PIECE * (i + 1)])

    loads[5].wait()
    hf[...] = filt_ref[...].astype(F32)

    def filters(n, carry):
        toeplitz(n * 6, jnp.minimum(n * 6 + 6, 16))
        happen(n, {0: [(first_arrives, 1)], 2: [(first_arrives, 2)]})
        return carry

    lax.fori_loop(0, 3, filters, 0)
    widen()
    first_arrives(3)
    halo_arrives()

    def feature_strip(strip, carry):
        features(strip)

        @pl.when(lax.rem(strip, 2) == 1)
        def send():
            tail(lax.div(strip, 2)).start()

        happen(strip, {0: [(first_arrives, 4)], 2: [early(0)], 4: [early(1)], 7: [early(2)]})
        return carry

    lax.fori_loop(0, STRIPS, feature_strip, 0)

    def conv_step(step, carry):
        @pl.when(lax.rem(step, 2) == 0)
        def wait():
            tail_arrives(lax.div(step, 2))

        conv(step)
        happen(step, {3: [early(3)], 7: [early(4)]})
        return carry

    lax.fori_loop(0, 64 // BATCH, conv_step, 0)
    del events[:5]
    clock[0] = 18.0
    work(0.1, own_wait)
    work(0.6, a_first, (OWN,))
    work(0.6, o_first)
    work(0.6, a_second, (OWN,))
    work(0.6, o_second)
    for k in (1, 2, 3):
        low, high = SLOT[k], SLOT[-k]
        need(k)
        work(1.2, a_first, (low, high))
        work(1.2, b_first, k - 1)
        work(1.2, a_second, (low, high))
        work(1.2, b_second, k - 1)
    while not {(4, g) for g in (0, 1, 2)} <= seen:
        take_event()
    far_first(0)
    far_second(0)
    need(4)
    far_first(1)
    pair_sums(0)
    pair_sums(1)
    single_sums(0, OWN)
    far_second(1)
    pair_sums(2)
    single_sums(1, FAR)
    row_sums()

    for make, args in started:
        make(*args).wait_send()

    def drain_tail(quarter, carry):
        tail(quarter).wait_send()
        return carry

    lax.fori_loop(0, 4, drain_tail, 0)
    for to, copy in delivered:
        @pl.when(to != c)
        def drain(copy=copy):
            copy.wait_send()


def local(qkv, feat_taps, long_filter, skip_gain, out_weight):
    vmem = pl.BlockSpec(memory_space=pltpu.VMEM)
    anywhere = pl.BlockSpec(memory_space=pl.ANY)
    dma = pltpu.SemaphoreType.DMA
    half_piece = (4 * PIECE, ROWS)
    return pl.pallas_call(
        kernel,
        out_shape=jax.ShapeDtypeStruct((512, ROWS), BF16),
        in_specs=[anywhere] * 5,
        out_specs=vmem,
        scratch_shapes=[
            pltpu.VMEM((3, FTAPS, WIDTH), F32),
            pltpu.VMEM((WIDTH // GROUP, SPAN), BF16),
            pltpu.VMEM((1, WIDTH), F32),
            pltpu.VMEM((2, RING, RING, PIECE, WIDTH), BF16),
            pltpu.VMEM((3, ROWS, WIDTH), BF16),
            pltpu.VMEM((3, HALO, WIDTH), BF16),
            pltpu.VMEM((3, STRIPS, PAD + TALL, LANES), F32),
            pltpu.VMEM((STRIPS, TALL, LANES), F32),
            pltpu.VMEM((STRIPS, TALL, LANES), F32),
            pltpu.VMEM((BLOCKS + 1, WIDTH, SPAN), BF16),
            pltpu.VMEM((BLOCKS, WIDTH, SPAN), F32),
            pltpu.VMEM((WIDTH, SPAN), F32),
            pltpu.VMEM((WIDTH // GROUP, SPAN), F32),
            pltpu.VMEM((WIDTH // GROUP, 2 * SPAN, SPAN), BF16),
            pltpu.VMEM((WIDTH, ROWS), BF16),
            pltpu.VMEM((RING,) + half_piece, BF16),
            pltpu.VMEM((RING,) + half_piece, BF16),
            pltpu.VMEM((RING,) + half_piece, BF16),
            pltpu.VMEM((PAIRS, RING * PIECE, ROWS), BF16),
            pltpu.VMEM((PAIRS, RING * PIECE, ROWS), BF16),
            pltpu.VMEM((PAIRS, RING * PIECE, ROWS), BF16),
            pltpu.VMEM((12 * PIECE, ROWS), BF16),
            pltpu.VMEM((12 * PIECE, ROWS), BF16),
            pltpu.VMEM((12 * PIECE, ROWS), BF16),
            pltpu.VMEM((4, 2) + half_piece, BF16),
            pltpu.VMEM((PAIRS, 4, 2, PIECE, ROWS), BF16),
            pltpu.VMEM((2, 4, PIECE, ROWS), BF16),
            dma((6,)), dma((2,)), dma((2,)), dma((2, 4)),
            dma((2, 2, 4)), dma((2, 2, 4)),
            dma((2, 2, 4, 5)), dma((2, 2, 4, 5)),
            dma((RING,)), dma((RING,)), dma((RING, 2)), dma((4, 2)),
            dma((PAIRS,)), dma((PAIRS,)), dma((PAIRS, RING)), dma((PAIRS, 4, 2)),
            dma((3,)), dma((3,)), dma((2, 2, 2)), dma((2, 4)),
        ],
        compiler_params=pltpu.CompilerParams(
            collective_id=0, has_side_effects=True, vmem_limit_bytes=56 * 2**20
        ),
    )(qkv, feat_taps, long_filter.T, skip_gain.reshape(1, WIDTH), out_weight.T).T


def solution(mesh):
    return jax.shard_map(
        local,
        mesh=mesh,
        in_specs=(
            P(None, "seq", "chan"),
            P(None, None, "chan"),
            P(None, "chan"),
            P("chan"),
            P("chan", "seq"),
        ),
        out_specs=P("seq", "chan"),
        check_vma=False,
    )
```

```python
import jax
import jax.numpy as jnp
from jax import lax
from jax.experimental import pallas as pl
from jax.experimental.pallas import tpu as pltpu
from jax.sharding import PartitionSpec as P

MESH = pl.DeviceIdType.MESH
F32 = jnp.float32
BF16 = jnp.bfloat16

RING = 8
GROUP = 16
SPAN = 128
FTAPS = 7
ROWS = 384
WIDTH = 1024
BLOCKS = ROWS // SPAN
LANES = 128
STRIPS = WIDTH // LANES
PIECE = 32
HALO = 16
PAD = 8
PITCH = 49
SUBS = 8
TALL = PITCH * SUBS
BATCH = 8

OFF = (1, -1, 2, -2, 3, -3, 4, 0)
SLOT = {off: slot for slot, off in enumerate(OFF)}
PACKS = ((7, 8), (0, 2), (2, 4), (4, 6), (6, 7))
FAR_UP = (0, 1, 4)
OWN = SLOT[0]
FAR = SLOT[4]
PAIRS = 3


def origin(direction, step):
    return SLOT[4 if step == 4 else -direction * step]


def kernel(
    qkv_ref, taps_hbm, filt_hbm, skip_hbm, w_ref, out_ref,
    taps_ref, filt_ref, skip_ref,
    w_all, qkv_v, halo, ext_v, ub, qs, ut, qt, skt, hf, mats, yt,
    ta, sa, qa, tb, sb, qb, tc, sc, qc, ra, rb, rc,
    load_sem, own_sem, halo_sem, tail_sem,
    s1, r1, s2, r2, as1, ar1, as2, ar2, bs1, br1, bs2, br2, cs1, cr1, cs2, cr2,
):
    s = lax.axis_index("seq")
    c = lax.axis_index("chan")
    y = lax.div(s, RING)
    z = lax.rem(s, RING)
    x = lax.div(c, 2)
    p = lax.rem(c, 2)

    def y_at(d):
        return {"seq": lax.rem(y + d + RING, RING) * RING + z}

    def z_at(d):
        return {"seq": y * RING + lax.rem(z + d + RING, RING)}

    def seq_at(d):
        return {"seq": lax.rem(s + d + RING * RING, RING * RING)}

    sibling = {"chan": c + 1 - 2 * p}
    minor_at = (z_at, y_at)
    major_at = (y_at, z_at)
    started = []

    def remote(src, dst, send, recv, to):
        return pltpu.make_async_remote_copy(
            src_ref=src, dst_ref=dst, send_sem=send, recv_sem=recv, device_id=to, device_id_type=MESH
        )

    def go(make, *args):
        make(*args).start()
        if (make, args) not in started:
            started.append((make, args))

    loads = [
        pltpu.make_async_copy(qkv_ref.at[i], qkv_v.at[i], load_sem.at[i]) for i in (1, 2, 0)
    ]
    loads += [
        pltpu.make_async_copy(taps_hbm, taps_ref, load_sem.at[3]),
        pltpu.make_async_copy(skip_hbm, skip_ref, load_sem.at[5]),
        pltpu.make_async_copy(filt_hbm, filt_ref, load_sem.at[4]),
    ]
    own = [
        pltpu.make_async_copy(
            w_ref.at[PIECE * kind : PIECE * (kind + 1)], w_all.at[kind, OWN, OWN], own_sem.at[kind]
        )
        for kind in range(2)
    ]
    for copy in loads[::-1] + own:
        copy.start()

    barrier = pltpu.get_barrier_semaphore()
    greeted = [{"chan": lax.rem(c + d, 8)} for d in range(1, 8)]
    greeted += [z_at(1), z_at(-1), y_at(1), y_at(-1), seq_at(1), seq_at(-1)]
    for to in greeted:
        pl.semaphore_signal(barrier, inc=1, device_id=to, device_id_type=MESH)
    def toeplitz(low, high):
        def body(step, carry):
            row = lax.broadcasted_iota(jnp.int32, (SUBS, SPAN), 0)
            col = lax.broadcasted_iota(jnp.int32, (SUBS, SPAN), 1)
            for i in range(4):
                g = step * 4 + i
                base = jnp.broadcast_to(hf[pl.ds(g, 1), :], (SUBS, SPAN))
                for bit in (1, 2, 4):
                    base = jnp.where((row & bit) != 0, pltpu.roll(base, bit, 1), base)
                for pair in range(SPAN // (2 * SUBS)):
                    above, below = [], []
                    for k in (2 * pair, 2 * pair + 1):
                        turned = pltpu.roll(base, SUBS * k, 1) if k else base
                        under = row + SUBS * k > col
                        above.append(jnp.where(under, turned, 0.0))
                        below.append(jnp.where(under, 0.0, turned))
                    at = 2 * SUBS * pair
                    mats[g, at : at + 2 * SUBS] = jnp.concatenate(above, axis=0).astype(BF16)
                    mats[g, SPAN + at : SPAN + at + 2 * SUBS] = jnp.concatenate(below, axis=0).astype(BF16)
            return carry

        lax.fori_loop(low, high, body, 0)

    def widen():
        for copy in loads[:5]:
            copy.wait()

        def body(strip, carry):
            at = pl.ds(pl.multiple_of(strip * LANES, LANES), LANES)
            for i in range(3):
                ext_v[i, strip, PAD : PAD + ROWS, :] = qkv_v[i, :, at].astype(F32)
                ext_v[i, strip, PAD + ROWS :, :] = jnp.zeros((TALL - ROWS, LANES), F32)
            skt[at, :] = jnp.broadcast_to(skip_ref[:, at], (LANES, LANES)).T
            return carry

        lax.fori_loop(0, STRIPS, body, 0)

    pl.semaphore_wait(barrier, len(greeted))

    def first(kind, direction, step):
        lane = 0 if direction == 1 else 1
        into = origin(direction, step)
        if step == 1:
            src, dst = w_ref.at[PIECE * kind : PIECE * (kind + 1)], w_all.at[kind, OWN, into]
        elif step < 4:
            src, dst = w_all.at[kind, OWN, origin(direction, step - 1)], w_all.at[kind, OWN, into]
        else:
            half = pl.ds(lane * (PIECE // 2), PIECE // 2)
            src = w_all.at[kind, OWN, origin(direction, 3), half]
            dst = w_all.at[kind, OWN, into, half]
        at = kind, lane, step - 1
        return remote(src, dst, s1.at[at], r1.at[at], minor_at[kind](direction))

    def second(kind, direction, step, pack):
        lane = 0 if direction == 1 else 1
        lo, hi = PACKS[pack]
        into = origin(direction, step)
        if step == 1 and pack == 0:
            src, dst = w_ref.at[PIECE * kind : PIECE * (kind + 1)], w_all.at[kind, into, OWN]
        else:
            came = OWN if step == 1 else origin(direction, step - 1)
            src = w_all.at[kind, came, pl.ds(lo, hi - lo)]
            dst = w_all.at[kind, into, pl.ds(lo, hi - lo)]
        at = kind, lane, step - 1, pack
        return remote(src, dst, s2.at[at], r2.at[at], major_at[kind](direction))

    def lanes_of(step, pack):
        if step < 4:
            return (1, -1)
        return (1,) if pack in FAR_UP else (-1,)

    def first_arrives(step):
        for kind in range(2):
            for direction in (1, -1):
                first(kind, direction, step).wait_recv()
                if step < 4:
                    go(first, kind, direction, step + 1)
        for kind in range(2):
            for direction in (1, -1):
                go(second, kind, direction, 1, step)

    def second_arrives(step, pack):
        for kind in range(2):
            for direction in lanes_of(step, pack):
                second(kind, direction, step, pack).wait_recv()
                if step < 4 and direction in lanes_of(step + 1, pack):
                    go(second, kind, direction, step + 1, pack)

    events = [(2.6 + 10.5 * (k - 1) + 2.4 * g, second_arrives, (k, g)) for k in range(1, 5) for g in range(5)]
    events.sort(key=lambda e: e[0])

    def happen(step, table):
        for at, calls in table.items():
            @pl.when(step == at)
            def run(calls=calls):
                for fn, *args in calls:
                    fn(*args)

    def early(number):
        at, fn, args = events[number]
        seen.add(args)
        return fn, *args

    def run_early(number):
        fn, *args = early(number)
        fn(*args)

    clock = [0.0]
    seen = set()

    def take_event():
        at, fn, args = events.pop(0)
        fn(*args)
        seen.add(args)
        clock[0] = max(clock[0], at)

    def work(cost, fn, *args):
        while events and events[0][0] <= clock[0]:
            take_event()
        fn(*args)
        clock[0] += cost

    def need(step):
        wanted = {(step, g) for g in range(5)}
        while not wanted <= seen:
            take_event()

    def halo_copy():
        return remote(
            qkv_ref.at[:, ROWS - HALO : ROWS], halo, halo_sem.at[0], halo_sem.at[1], seq_at(1)
        )

    go(halo_copy)
    for kind in range(2):
        for direction in (1, -1):
            go(first, kind, direction, 1)
    for kind in range(2):
        for direction in (1, -1):
            go(second, kind, direction, 1, 0)

    def halo_arrives():
        halo_copy().wait_recv()

        def body(strip, carry):
            at = pl.ds(pl.multiple_of(strip * LANES, LANES), LANES)
            for i in range(3):
                before = halo[i, :, at].astype(F32)[HALO - PAD :]
                ext_v[i, strip, :PAD, :] = jnp.where(s == 0, 0.0, before)
            return carry

        lax.fori_loop(0, STRIPS, body, 0)

    def features(strip):
        at = pl.ds(pl.multiple_of(strip * LANES, LANES), LANES)
        taps = [
            [jnp.broadcast_to(taps_ref[i, j : j + 1, at], (SUBS, LANES)) for j in range(FTAPS)]
            for i in range(3)
        ]

        def load(i, r):
            return ext_v[i, strip, pl.ds(PAD + r, SUBS, stride=PITCH), :]

        def line(i, window):
            total = taps[i][0] * window[-1]
            for j in range(1, FTAPS):
                total = total + taps[i][j] * window[-1 - j]
            return total

        def some(turn, windows):
            windows = [list(w) for w in windows]
            for step in range(FTAPS):
                r = turn * FTAPS + step
                found = []
                for i in range(3):
                    windows[i] = windows[i][1 - FTAPS :] + [load(i, r)]
                    found.append(line(i, windows[i]))
                ub[strip, pl.ds(r, SUBS, stride=PITCH), :] = found[1] * found[2]
                qs[strip, pl.ds(r, SUBS, stride=PITCH), :] = found[0]
            return tuple(tuple(w[1 - FTAPS :]) for w in windows)

        start = tuple(tuple(load(i, r) for r in range(1 - FTAPS, 0)) for i in range(3))
        lax.fori_loop(0, PITCH // FTAPS, some, start)
        for b in range(BLOCKS):
            ut[b + 1, at, :] = ub[strip, SPAN * b : SPAN * (b + 1), :].T.astype(BF16)
            qt[b, at, :] = qs[strip, SPAN * b : SPAN * (b + 1), :].T

    def tail(quarter):
        at = pl.ds(pl.multiple_of(quarter * (WIDTH // 4), WIDTH // 4), WIDTH // 4)
        return remote(
            ut.at[BLOCKS, at], ut.at[0, at], tail_sem.at[0, quarter], tail_sem.at[1, quarter], seq_at(1)
        )

    def tail_arrives(quarter):
        tail(quarter).wait_recv()

        @pl.when(s == 0)
        def clear():
            at = pl.ds(pl.multiple_of(quarter * (WIDTH // 4), WIDTH // 4), WIDTH // 4)
            ut[0, at] = jnp.zeros((WIDTH // 4, SPAN), BF16)

    def conv(step):
        base = step * BATCH
        spots = [pl.ds(pl.multiple_of((base + i) * GROUP, GROUP), GROUP) for i in range(BATCH)]
        parts = [[ut[b, at, :] for b in range(BLOCKS + 1)] for at in spots]
        mixed = []
        for i in range(BATCH):
            window = [jnp.concatenate(parts[i][b : b + 2], axis=1) for b in range(BLOCKS)]
            mixed.append(
                jnp.dot(jnp.concatenate(window, axis=0), mats[base + i], preferred_element_type=F32)
            )
        found = []
        for i, at in enumerate(spots):
            for b in range(BLOCKS):
                field = mixed[i][GROUP * b : GROUP * (b + 1)] + skt[at, :] * parts[i][b + 1].astype(F32)
                found.append((qt[b, at, :] * field).astype(BF16))
        for i, at in enumerate(spots):
            for b in range(BLOCKS):
                yt[at, SPAN * b : SPAN * (b + 1)] = found[BLOCKS * i + b]

    def project(pieces):
        rows = jnp.concatenate(pieces, axis=0) if len(pieces) > 1 else pieces[0]
        return jnp.dot(rows, yt[...], preferred_element_type=F32)

    def two(kind, major, batch, half):
        return w_all[kind, major, pl.ds(4 * batch + 2 * half, 2)].reshape(2 * PIECE, WIDTH)

    def four(kind, major, half):
        return [two(kind, major, batch, half) for batch in range(2)]

    def target(slot):
        return lax.rem(y + OFF[slot] + RING, RING)

    delivered = []

    def deliver(src, dst, send, recv, to):
        copy = remote(src, dst, send, recv, {"chan": to})

        @pl.when(to == c)
        def keep():
            pltpu.make_async_copy(src, dst, recv).start()

        @pl.when(to != c)
        def post():
            copy.start()

        delivered.append((to, copy))

    def a_swap(slot):
        return remote(ta.at[slot], sa.at[slot], as1.at[slot], ar1.at[slot], sibling)

    def a_first(slots):
        got = project(sum([four(0, m, 1 - p) for m in slots], [])).astype(BF16)
        for i, m in enumerate(slots):
            ta[m] = got[4 * PIECE * i : 4 * PIECE * (i + 1)]
            go(a_swap, m)

    def a_second(slots):
        got = project(sum([four(0, m, p) for m in slots], []))
        for i, m in enumerate(slots):
            a_swap(m).wait_recv()
            qa[m] = (got[4 * PIECE * i : 4 * PIECE * (i + 1)] + sa[m].astype(F32)).astype(BF16)
            deliver(qa.at[m], ra.at[x, p], as2.at[m, 0], ar2.at[x, p], target(m))

    def b_swap(turn):
        return remote(tb.at[turn], sb.at[turn], bs1.at[turn], br1.at[turn], sibling)

    def b_rows(turn, half):
        return w_all[1, 2 * turn + half].reshape(RING * PIECE, WIDTH)

    def b_first(turn):
        tb[turn] = project([b_rows(turn, 1 - p)]).astype(BF16)
        go(b_swap, turn)

    def b_second(turn):
        got = project([b_rows(turn, p)])
        b_swap(turn).wait_recv()
        qb[turn] = (got + sb[turn].astype(F32)).astype(BF16)
        for m in range(RING):
            deliver(
                qb.at[turn, PIECE * m : PIECE * (m + 1)], rb.at[turn, x, p],
                bs2.at[turn, m], br2.at[turn, x, p], target(m),
            )

    def o_swap(part):
        at = pl.ds(4 * PIECE * part, 4 * PIECE)
        return remote(tc.at[at], sc.at[at], cs1.at[part], cr1.at[part], sibling)

    def o_post(single, batch, at):
        for i in range(2):
            to = lax.rem(y + jnp.where(p == 0, OFF[4 * batch + i], OFF[4 * batch + 2 + i]) + RING, RING)
            deliver(
                qc.at[pl.ds(at + PIECE * i, PIECE)], rc.at[single, x],
                cs2.at[single, batch, i], cr2.at[single, x], to,
            )

    def o_first():
        tc[: 4 * PIECE] = project(four(1, OWN, 1 - p)).astype(BF16)
        go(o_swap, 0)

    def o_second():
        got = project(four(1, OWN, p))
        o_swap(0).wait_recv()
        qc[: 4 * PIECE] = (got + sc[: 4 * PIECE].astype(F32)).astype(BF16)
        for batch in range(2):
            o_post(0, batch, 2 * PIECE * batch)

    def far_first(batch):
        at = pl.ds(4 * PIECE * (batch + 1), 4 * PIECE)
        tc[at] = project([two(0, FAR, batch, 1 - p), two(1, FAR, batch, 1 - p)]).astype(BF16)
        go(o_swap, batch + 1)

    def far_second(batch):
        base = 4 * PIECE * (batch + 1)
        got = project([two(0, FAR, batch, p), two(1, FAR, batch, p)])
        o_swap(batch + 1).wait_recv()
        qc[base : base + 4 * PIECE] = (got + sc[base : base + 4 * PIECE].astype(F32)).astype(BF16)
        deliver(
            qc.at[base : base + 2 * PIECE], ra.at[x, p, pl.ds(2 * PIECE * batch, 2 * PIECE)],
            as2.at[FAR, batch], ar2.at[x, p], target(FAR),
        )
        o_post(1, batch, base + 2 * PIECE)

    def own_wait():
        for copy in own:
            copy.wait()

    def place(kind, slot, rows):
        at = lax.rem(z + OFF[slot] + RING, RING) * (2 * PIECE) + kind * PIECE
        out_ref[pl.ds(pl.multiple_of(at, PIECE), PIECE), :] = rows.astype(BF16)

    def total(refs):
        found = None
        for ref in refs:
            term = ref[...].astype(F32)
            found = term if found is None else found + term
        return found

    def arrived(ref, sem):
        remote(ref, ref, cs2.at[0, 0, 0], sem, sibling).wait_recv()

    def pair_sums(turn):
        for half in range(2):
            for chip in range(4):
                arrived(rb.at[turn, chip, half], br2.at[turn, chip, half])
            place(1, 2 * turn + half, total([rb.at[turn, chip, half] for chip in range(4)]))

    def single_sums(single, slot):
        for chip in range(4):
            arrived(rc.at[single, chip], cr2.at[single, chip])
        place(1, slot, total([rc.at[single, chip] for chip in range(4)]))

    def row_sums():
        for half in range(2):
            for chip in range(4):
                arrived(ra.at[chip, half], ar2.at[chip, half])
            found = total([ra.at[chip, half] for chip in range(4)])
            for i in range(4):
                slot = 4 * (i // 2) + 2 * half + i % 2
                place(0, slot, found[PIECE * i : PIECE * (i + 1)])

    loads[5].wait()
    hf[...] = filt_ref[...].astype(F32)

    def filters(n, carry):
        toeplitz(n * 6, jnp.minimum(n * 6 + 6, 16))
        happen(n, {0: [(first_arrives, 1)], 1: [early(0)], 2: [(first_arrives, 2)]})
        return carry

    lax.fori_loop(0, 3, filters, 0)
    widen()
    run_early(1)
    halo_arrives()

    def feature_strip(strip, carry):
        features(strip)

        @pl.when(lax.rem(strip, 2) == 1)
        def send():
            tail(lax.div(strip, 2)).start()

        happen(strip, {
            0: [(first_arrives, 3)], 2: [early(2)], 3: [(first_arrives, 4)], 5: [early(3)], 7: [early(4)],
        })
        return carry

    lax.fori_loop(0, STRIPS, feature_strip, 0)

    def conv_step(step, carry):
        @pl.when(lax.rem(step, 2) == 0)
        def wait():
            tail_arrives(lax.div(step, 2))

        conv(step)
        happen(step, {1: [early(5)], 4: [early(6)], 7: [early(7)]})
        return carry

    lax.fori_loop(0, 64 // BATCH, conv_step, 0)
    del events[:8]
    clock[0] = 18.0
    work(0.1, own_wait)
    work(0.6, a_first, (OWN,))
    work(0.6, o_first)
    work(0.6, a_second, (OWN,))
    work(0.6, o_second)
    for k in (1, 2, 3):
        low, high = SLOT[k], SLOT[-k]
        need(k)
        work(1.0, a_first, (low, high))
        work(1.0, b_first, k - 1)
        work(1.0, a_second, (low, high))
        work(1.0, b_second, k - 1)
    while not {(4, g) for g in (0, 1, 2)} <= seen:
        take_event()
    far_first(0)
    far_second(0)
    need(4)
    far_first(1)
    pair_sums(0)
    pair_sums(1)
    single_sums(0, OWN)
    far_second(1)
    pair_sums(2)
    single_sums(1, FAR)
    row_sums()

    for make, args in started:
        make(*args).wait_send()

    def drain_tail(quarter, carry):
        tail(quarter).wait_send()
        return carry

    lax.fori_loop(0, 4, drain_tail, 0)
    for to, copy in delivered:
        @pl.when(to != c)
        def drain(copy=copy):
            copy.wait_send()


def local(qkv, feat_taps, long_filter, skip_gain, out_weight):
    vmem = pl.BlockSpec(memory_space=pltpu.VMEM)
    anywhere = pl.BlockSpec(memory_space=pl.ANY)
    dma = pltpu.SemaphoreType.DMA
    half_piece = (4 * PIECE, ROWS)
    return pl.pallas_call(
        kernel,
        out_shape=jax.ShapeDtypeStruct((512, ROWS), BF16),
        in_specs=[anywhere] * 5,
        out_specs=vmem,
        scratch_shapes=[
            pltpu.VMEM((3, FTAPS, WIDTH), F32),
            pltpu.VMEM((WIDTH // GROUP, SPAN), BF16),
            pltpu.VMEM((1, WIDTH), F32),
            pltpu.VMEM((2, RING, RING, PIECE, WIDTH), BF16),
            pltpu.VMEM((3, ROWS, WIDTH), BF16),
            pltpu.VMEM((3, HALO, WIDTH), BF16),
            pltpu.VMEM((3, STRIPS, PAD + TALL, LANES), F32),
            pltpu.VMEM((STRIPS, TALL, LANES), F32),
            pltpu.VMEM((STRIPS, TALL, LANES), F32),
            pltpu.VMEM((BLOCKS + 1, WIDTH, SPAN), BF16),
            pltpu.VMEM((BLOCKS, WIDTH, SPAN), F32),
            pltpu.VMEM((WIDTH, SPAN), F32),
            pltpu.VMEM((WIDTH // GROUP, SPAN), F32),
            pltpu.VMEM((WIDTH // GROUP, 2 * SPAN, SPAN), BF16),
            pltpu.VMEM((WIDTH, ROWS), BF16),
            pltpu.VMEM((RING,) + half_piece, BF16),
            pltpu.VMEM((RING,) + half_piece, BF16),
            pltpu.VMEM((RING,) + half_piece, BF16),
            pltpu.VMEM((PAIRS, RING * PIECE, ROWS), BF16),
            pltpu.VMEM((PAIRS, RING * PIECE, ROWS), BF16),
            pltpu.VMEM((PAIRS, RING * PIECE, ROWS), BF16),
            pltpu.VMEM((12 * PIECE, ROWS), BF16),
            pltpu.VMEM((12 * PIECE, ROWS), BF16),
            pltpu.VMEM((12 * PIECE, ROWS), BF16),
            pltpu.VMEM((4, 2) + half_piece, BF16),
            pltpu.VMEM((PAIRS, 4, 2, PIECE, ROWS), BF16),
            pltpu.VMEM((2, 4, PIECE, ROWS), BF16),
            dma((6,)), dma((2,)), dma((2,)), dma((2, 4)),
            dma((2, 2, 4)), dma((2, 2, 4)),
            dma((2, 2, 4, 5)), dma((2, 2, 4, 5)),
            dma((RING,)), dma((RING,)), dma((RING, 2)), dma((4, 2)),
            dma((PAIRS,)), dma((PAIRS,)), dma((PAIRS, RING)), dma((PAIRS, 4, 2)),
            dma((3,)), dma((3,)), dma((2, 2, 2)), dma((2, 4)),
        ],
        compiler_params=pltpu.CompilerParams(
            collective_id=0, has_side_effects=True, vmem_limit_bytes=56 * 2**20
        ),
    )(qkv, feat_taps, long_filter.T, skip_gain.reshape(1, WIDTH), out_weight.T).T


def solution(mesh):
    return jax.shard_map(
        local,
        mesh=mesh,
        in_specs=(
            P(None, "seq", "chan"),
            P(None, None, "chan"),
            P(None, "chan"),
            P("chan"),
            P("chan", "seq"),
        ),
        out_specs=P("seq", "chan"),
        check_vma=False,
    )
```

```python
import jax
import jax.numpy as jnp
from jax import lax
from jax.experimental import pallas as pl
from jax.experimental.pallas import tpu as pltpu
from jax.sharding import PartitionSpec as P

MESH = pl.DeviceIdType.MESH
F32 = jnp.float32
BF16 = jnp.bfloat16

RING = 8
GROUP = 16
SPAN = 128
FTAPS = 7
ROWS = 384
WIDTH = 1024
BLOCKS = ROWS // SPAN
LANES = 128
STRIPS = WIDTH // LANES
PIECE = 32
HALO = 16
PAD = 8

OFF = (1, -1, 2, -2, 3, -3, 4, 0)
SLOT = {off: slot for slot, off in enumerate(OFF)}
PACKS = ((7, 8), (0, 2), (2, 4), (4, 6), (6, 7))
FAR_UP = (0, 1, 4)
OWN = SLOT[0]
FAR = SLOT[4]
PAIRS = 3


def origin(direction, step):
    return SLOT[4 if step == 4 else -direction * step]


def kernel(
    qkv_ref, taps_hbm, filt_hbm, skip_hbm, w_ref, out_ref,
    taps_ref, filt_ref, skip_ref,
    w_all, qkv_v, halo, ext, ut, qt, skt, hf, yt,
    ta, sa, qa, ra, rb, rc,
    load_sem, own_sem, halo_sem, tail_sem,
    s1, r1, s2, r2, as1, ar1, as2, ar2, bs2, br2, cs2, cr2,
):
    s = lax.axis_index("seq")
    c = lax.axis_index("chan")
    y = lax.div(s, RING)
    z = lax.rem(s, RING)
    x = lax.div(c, 2)
    p = lax.rem(c, 2)

    def y_at(d):
        return {"seq": lax.rem(y + d + RING, RING) * RING + z}

    def z_at(d):
        return {"seq": y * RING + lax.rem(z + d + RING, RING)}

    def seq_at(d):
        return {"seq": lax.rem(s + d + RING * RING, RING * RING)}

    sibling = {"chan": c + 1 - 2 * p}
    minor_at = (z_at, y_at)
    major_at = (y_at, z_at)
    started = []

    def remote(src, dst, send, recv, to):
        return pltpu.make_async_remote_copy(
            src_ref=src, dst_ref=dst, send_sem=send, recv_sem=recv, device_id=to, device_id_type=MESH
        )

    def go(copy):
        copy.start()
        started.append(copy)

    loads = [
        pltpu.make_async_copy(qkv_ref.at[i], qkv_v.at[i], load_sem.at[i]) for i in (1, 2, 0)
    ]
    loads += [
        pltpu.make_async_copy(taps_hbm, taps_ref, load_sem.at[3]),
        pltpu.make_async_copy(filt_hbm, filt_ref, load_sem.at[4]),
        pltpu.make_async_copy(skip_hbm, skip_ref, load_sem.at[5]),
    ]
    own = [
        pltpu.make_async_copy(
            w_ref.at[PIECE * kind : PIECE * (kind + 1)], w_all.at[kind, OWN, OWN], own_sem.at[kind]
        )
        for kind in range(2)
    ]
    for copy in loads + own:
        copy.start()

    barrier = pltpu.get_barrier_semaphore()
    greeted = [{"chan": lax.rem(c + d, 8)} for d in range(1, 8)]
    greeted += [z_at(1), z_at(-1), y_at(1), y_at(-1), seq_at(1), seq_at(-1)]
    for to in greeted:
        pl.semaphore_signal(barrier, inc=1, device_id=to, device_id_type=MESH)
    pl.semaphore_wait(barrier, len(greeted))

    def first(kind, direction, step):
        lane = 0 if direction == 1 else 1
        into = origin(direction, step)
        if step == 1:
            src, dst = w_ref.at[PIECE * kind : PIECE * (kind + 1)], w_all.at[kind, OWN, into]
        elif step < 4:
            src, dst = w_all.at[kind, OWN, origin(direction, step - 1)], w_all.at[kind, OWN, into]
        else:
            half = pl.ds(lane * (PIECE // 2), PIECE // 2)
            src = w_all.at[kind, OWN, origin(direction, 3), half]
            dst = w_all.at[kind, OWN, into, half]
        at = kind, lane, step - 1
        return remote(src, dst, s1.at[at], r1.at[at], minor_at[kind](direction))

    def second(kind, direction, step, pack):
        lane = 0 if direction == 1 else 1
        lo, hi = PACKS[pack]
        into = origin(direction, step)
        if step == 1 and pack == 0:
            src, dst = w_ref.at[PIECE * kind : PIECE * (kind + 1)], w_all.at[kind, into, OWN]
        else:
            came = OWN if step == 1 else origin(direction, step - 1)
            src = w_all.at[kind, came, pl.ds(lo, hi - lo)]
            dst = w_all.at[kind, into, pl.ds(lo, hi - lo)]
        at = kind, lane, step - 1, pack
        return remote(src, dst, s2.at[at], r2.at[at], major_at[kind](direction))

    def lanes_of(step, pack):
        if step < 4:
            return (1, -1)
        return (1,) if pack in FAR_UP else (-1,)

    def first_arrives(step):
        for kind in range(2):
            for direction in (1, -1):
                first(kind, direction, step).wait_recv()
                if step < 4:
                    go(first(kind, direction, step + 1))
        for kind in range(2):
            for direction in (1, -1):
                go(second(kind, direction, 1, step))

    def second_arrives(step, pack):
        for kind in range(2):
            for direction in lanes_of(step, pack):
                second(kind, direction, step, pack).wait_recv()
                if step < 4 and direction in lanes_of(step + 1, pack):
                    go(second(kind, direction, step + 1, pack))

    events = [(2.2 * k, first_arrives, (k,)) for k in range(1, 5)]
    events += [
        (2.6 + 10.5 * (k - 1) + 2.4 * g, second_arrives, (k, g)) for k in range(1, 5) for g in range(5)
    ]
    events.sort(key=lambda e: e[0])
    events = [(at, fn, args) for at, fn, args in events]
    clock = [0.0]
    seen = set()

    def take_event():
        at, fn, args = events.pop(0)
        fn(*args)
        if fn is second_arrives:
            seen.add(args)
        else:
            seen.add(args[0])
        clock[0] = max(clock[0], at)

    def work(cost, fn, *args):
        while events and events[0][0] <= clock[0]:
            take_event()
        fn(*args)
        clock[0] += cost

    def need(step):
        wanted = {(step, g) for g in range(5)}
        while not wanted <= seen:
            take_event()

    halo_copy = remote(
        qkv_ref.at[:, ROWS - HALO : ROWS], halo, halo_sem.at[0], halo_sem.at[1], seq_at(1)
    )
    go(halo_copy)
    for kind in range(2):
        for direction in (1, -1):
            go(first(kind, direction, 1))
    for kind in range(2):
        for direction in (1, -1):
            go(second(kind, direction, 1, 0))

    def widen(strip):
        at = pl.ds(pl.multiple_of(strip * LANES, LANES), LANES)
        for i in range(3):
            ext[i, strip, PAD:, :] = qkv_v[i, :, at].astype(F32)

    def widen_halo(strip):
        at = pl.ds(pl.multiple_of(strip * LANES, LANES), LANES)
        for i in range(3):
            before = halo[i, :, at].astype(F32)[HALO - PAD :]
            ext[i, strip, :PAD, :] = jnp.where(s == 0, 0.0, before)

    def feature(i, block, strip, at):
        total = None
        for j in range(FTAPS):
            term = taps_ref[i, j : j + 1, at] * ext[i, strip, pl.ds(PAD + SPAN * block - j, SPAN), :]
            total = term if total is None else total + term
        return total

    def features(block, strips):
        def body(strip, carry):
            at = pl.ds(pl.multiple_of(strip * LANES, LANES), LANES)
            u = (feature(1, block, strip, at) * feature(2, block, strip, at)).astype(BF16).astype(F32)
            ut[block + 1, at, :] = u.T.astype(BF16)
            qt[block, at, :] = feature(0, block, strip, at).T
            return carry

        lax.fori_loop(strips[0], strips[1], body, 0)

    def widen_all():
        for copy in loads:
            copy.wait()

        def body(strip, carry):
            widen(strip)
            return carry

        lax.fori_loop(0, STRIPS, body, 0)
        hf[...] = filt_ref[...].astype(F32)

    def halo_arrives():
        halo_copy.wait_recv()

        def body(strip, carry):
            widen_halo(strip)
            at = pl.ds(pl.multiple_of(strip * LANES, LANES), LANES)
            skt[at, :] = jnp.broadcast_to(skip_ref[:, at], (LANES, LANES)).T
            return carry

        lax.fori_loop(0, STRIPS, body, 0)

    tail_copy = remote(ut.at[BLOCKS], ut.at[0], tail_sem.at[0], tail_sem.at[1], seq_at(1))

    def send_tail():
        go(tail_copy)

    def tail_arrives():
        tail_copy.wait_recv()

        @pl.when(s == 0)
        def clear():
            ut[0] = jnp.zeros((WIDTH, SPAN), BF16)

    def conv(lo, hi):
        def body(g, carry):
            row = lax.broadcasted_iota(jnp.int32, (SPAN, SPAN), 0)
            col = lax.broadcasted_iota(jnp.int32, (SPAN, SPAN), 1)
            taps = jnp.broadcast_to(hf[pl.ds(g, 1), :], (SPAN, SPAN))
            ring = pltpu.roll(taps, 0, 1, stride=1, stride_axis=0)
            here = jnp.where(row <= col, ring, 0.0)
            before = jnp.where(row > col, ring, 0.0)
            matrix = jnp.concatenate([before, here], axis=0).astype(BF16)
            at = pl.ds(pl.multiple_of(g * GROUP, GROUP), GROUP)
            parts = [ut[b, at, :] for b in range(BLOCKS + 1)]
            window = jnp.concatenate(
                [jnp.concatenate(parts[:BLOCKS], axis=0), jnp.concatenate(parts[1:], axis=0)], axis=1
            )
            mixed = jnp.dot(window, matrix, preferred_element_type=F32)
            for b in range(BLOCKS):
                field = mixed[GROUP * b : GROUP * (b + 1)] + skt[at, :] * parts[b + 1].astype(F32)
                yt[at, SPAN * b : SPAN * (b + 1)] = (qt[b, at, :] * field).astype(BF16)
            return carry

        lax.fori_loop(lo, hi, body, 0, unroll=4)

    def project(pieces):
        rows = jnp.concatenate(pieces, axis=0) if len(pieces) > 1 else pieces[0]
        return jnp.dot(rows, yt[...], preferred_element_type=F32)

    def two(kind, major, batch, half):
        return w_all[kind, major, pl.ds(4 * batch + 2 * half, 2)].reshape(2 * PIECE, WIDTH)

    def four(kind, major, half):
        return [two(kind, major, batch, half) for batch in range(2)]

    def target(slot):
        return lax.rem(y + OFF[slot] + RING, RING)

    delivered = []

    def deliver(src, dst, send, recv, to):
        copy = remote(src, dst, send, recv, {"chan": to})

        @pl.when(to == c)
        def keep():
            pltpu.make_async_copy(src, dst, recv).start()

        @pl.when(to != c)
        def post():
            copy.start()

        delivered.append((to, copy))

    STARTS = (0, 256, 768, 1280, 1792, 1920)
    COUNTS = (256, 512, 512, 512, 128, 128)

    def b_rows(turn, half):
        return w_all[1, 2 * turn + half].reshape(RING * PIECE, WIDTH)

    def pieces(bundle, half):
        if bundle == 0:
            return four(0, OWN, half) + four(1, OWN, half)
        if bundle < 4:
            low = 2 * (bundle - 1)
            return four(0, low, half) + four(0, low + 1, half) + [b_rows(bundle - 1, half)]
        return [two(kind, FAR, bundle - 4, half) for kind in range(2)]

    def rows_of(bundle):
        return slice(STARTS[bundle], STARTS[bundle] + COUNTS[bundle])

    def swap(bundle):
        at = pl.ds(STARTS[bundle], COUNTS[bundle])
        return remote(ta.at[at], sa.at[at], as1.at[bundle], ar1.at[bundle], sibling)

    def give(bundle):
        ta[rows_of(bundle)] = project(pieces(bundle, 1 - p)).astype(BF16)
        copy = swap(bundle)
        go(copy)

    def post_row(slot, at, many, batch):
        deliver(
            qa.at[at : at + many], ra.at[x, p, pl.ds(2 * PIECE * batch, many)],
            as2.at[slot, batch], ar2.at[x, p], target(slot),
        )

    def post_single(single, batch, at):
        for i in range(2):
            to = lax.rem(y + jnp.where(p == 0, OFF[4 * batch + i], OFF[4 * batch + 2 + i]) + RING, RING)
            deliver(
                qa.at[at + PIECE * i : at + PIECE * (i + 1)], rc.at[single, x],
                cs2.at[single, batch, i], cr2.at[single, x], to,
            )

    def take(bundle):
        got = project(pieces(bundle, p))
        swap(bundle).wait_recv()
        at = rows_of(bundle)
        qa[at] = (got + sa[at].astype(F32)).astype(BF16)
        start = STARTS[bundle]
        if bundle == 0:
            post_row(OWN, start, 4 * PIECE, 0)
            for batch in range(2):
                post_single(0, batch, start + 4 * PIECE + 2 * PIECE * batch)
        elif bundle < 4:
            turn = bundle - 1
            for i in range(2):
                post_row(2 * turn + i, start + 4 * PIECE * i, 4 * PIECE, 0)
            for m in range(RING):
                from_row = start + 8 * PIECE + PIECE * m
                deliver(
                    qa.at[from_row : from_row + PIECE], rb.at[turn, x, p],
                    bs2.at[turn, m], br2.at[turn, x, p], target(m),
                )
        else:
            post_row(FAR, start, 2 * PIECE, bundle - 4)
            post_single(1, bundle - 4, start + 2 * PIECE)

    def own_wait():
        for copy in own:
            copy.wait()

    def place(kind, slot, rows):
        at = lax.rem(z + OFF[slot] + RING, RING) * (2 * PIECE) + kind * PIECE
        out_ref[pl.ds(pl.multiple_of(at, PIECE), PIECE), :] = rows.astype(BF16)

    def total(refs):
        found = None
        for ref in refs:
            term = ref[...].astype(F32)
            found = term if found is None else found + term
        return found

    def arrived(ref, sem):
        remote(ref, ref, cs2.at[0, 0, 0], sem, sibling).wait_recv()

    def pair_sums(turn):
        for half in range(2):
            for chip in range(4):
                arrived(rb.at[turn, chip, half], br2.at[turn, chip, half])
            place(1, 2 * turn + half, total([rb.at[turn, chip, half] for chip in range(4)]))

    def single_sums(single, slot):
        for chip in range(4):
            arrived(rc.at[single, chip], cr2.at[single, chip])
        place(1, slot, total([rc.at[single, chip] for chip in range(4)]))

    def row_sums():
        for half in range(2):
            for chip in range(4):
                arrived(ra.at[chip, half], ar2.at[chip, half])
            found = total([ra.at[chip, half] for chip in range(4)])
            for i in range(4):
                slot = 4 * (i // 2) + 2 * half + i % 2
                place(0, slot, found[PIECE * i : PIECE * (i + 1)])

    work(1.0, widen_all)
    for lo in (0, 4):
        work(1.4, features, BLOCKS - 1, (lo, lo + 4))
    work(0.1, send_tail)
    for lo in (0, 4):
        work(1.4, features, 1, (lo, lo + 4))
    work(0.3, halo_arrives)
    for lo in (0, 4):
        work(1.4, features, 0, (lo, lo + 4))
    work(0.1, tail_arrives)
    for lo in range(0, 64, 16):
        work(1.5, conv, lo, lo + 16)
    work(0.1, own_wait)
    work(1.0, give, 0)
    work(1.0, take, 0)
    for k in (1, 2, 3):
        need(k)
        work(1.8, give, k)
        work(2.2, take, k)
    while not {(4, g) for g in (0, 1, 2)} <= seen:
        take_event()
    give(4)
    take(4)
    need(4)
    give(5)
    pair_sums(0)
    pair_sums(1)
    single_sums(0, OWN)
    take(5)
    pair_sums(2)
    single_sums(1, FAR)
    row_sums()

    for copy in started:
        copy.wait_send()
    for to, copy in delivered:
        @pl.when(to != c)
        def drain(copy=copy):
            copy.wait_send()


def local(qkv, feat_taps, long_filter, skip_gain, out_weight):
    vmem = pl.BlockSpec(memory_space=pltpu.VMEM)
    anywhere = pl.BlockSpec(memory_space=pl.ANY)
    dma = pltpu.SemaphoreType.DMA
    half_piece = (4 * PIECE, ROWS)
    return pl.pallas_call(
        kernel,
        out_shape=jax.ShapeDtypeStruct((512, ROWS), BF16),
        in_specs=[anywhere] * 5,
        out_specs=vmem,
        scratch_shapes=[
            pltpu.VMEM((3, FTAPS, WIDTH), F32),
            pltpu.VMEM((WIDTH // GROUP, SPAN), BF16),
            pltpu.VMEM((1, WIDTH), F32),
            pltpu.VMEM((2, RING, RING, PIECE, WIDTH), BF16),
            pltpu.VMEM((3, ROWS, WIDTH), BF16),
            pltpu.VMEM((3, HALO, WIDTH), BF16),
            pltpu.VMEM((3, STRIPS, PAD + ROWS, LANES), F32),
            pltpu.VMEM((BLOCKS + 1, WIDTH, SPAN), BF16),
            pltpu.VMEM((BLOCKS, WIDTH, SPAN), F32),
            pltpu.VMEM((WIDTH, SPAN), F32),
            pltpu.VMEM((WIDTH // GROUP, SPAN), F32),
            pltpu.VMEM((WIDTH, ROWS), BF16),
            pltpu.VMEM((2048, ROWS), BF16),
            pltpu.VMEM((2048, ROWS), BF16),
            pltpu.VMEM((2048, ROWS), BF16),
            pltpu.VMEM((4, 2) + half_piece, BF16),
            pltpu.VMEM((PAIRS, 4, 2, PIECE, ROWS), BF16),
            pltpu.VMEM((2, 4, PIECE, ROWS), BF16),
            dma((6,)), dma((2,)), dma((2,)), dma((2,)),
            dma((2, 2, 4)), dma((2, 2, 4)),
            dma((2, 2, 4, 5)), dma((2, 2, 4, 5)),
            dma((6,)), dma((6,)), dma((RING, 2)), dma((4, 2)),
            dma((PAIRS, RING)), dma((PAIRS, 4, 2)), dma((2, 2, 2)), dma((2, 4)),
        ],
        compiler_params=pltpu.CompilerParams(
            collective_id=0, has_side_effects=True, vmem_limit_bytes=56 * 2**20
        ),
    )(qkv, feat_taps, long_filter.T, skip_gain.reshape(1, WIDTH), out_weight.T).T


def solution(mesh):
    return jax.shard_map(
        local,
        mesh=mesh,
        in_specs=(
            P(None, "seq", "chan"),
            P(None, None, "chan"),
            P(None, "chan"),
            P("chan"),
            P("chan", "seq"),
        ),
        out_specs=P("seq", "chan"),
        check_vma=False,
    )
```

```python
import jax
import jax.numpy as jnp
from jax import lax
from jax.experimental import pallas as pl
from jax.experimental.pallas import tpu as pltpu
from jax.sharding import PartitionSpec as P

MESH = pl.DeviceIdType.MESH
F32 = jnp.float32
BF16 = jnp.bfloat16

RING = 8
GROUP = 16
SPAN = 128
FTAPS = 7
ROWS = 384
WIDTH = 1024
BLOCKS = ROWS // SPAN
LANES = 128
STRIPS = WIDTH // LANES
PIECE = 32
HALO = 16
PAD = 8
PITCH = 49
SUBS = 8
TALL = PITCH * SUBS

OFF = (0, 1, -1, 2, -2, 3, -3, 4)
SLOT = {off: slot for slot, off in enumerate(OFF)}
OWN = SLOT[0]
GROUPS = ((0,), (1, 2), (3, 4), (5, 6), (7,))
NEAR, CROSS, NEAR_EXT, CROSS_EXT = (pl.ds(2 * PIECE * i, 2 * PIECE) for i in range(4))
PARTS = (NEAR, pl.ds(4 * PIECE, PIECE), CROSS, pl.ds(6 * PIECE, PIECE))
HALF = 4 * PIECE
BATCH = 8
JOBS = 16
CHIPS = 4


def origin(direction, step):
    return SLOT[4 if step == 4 else -direction * step]


def kernel(
    qkv_ref, taps_hbm, filt_hbm, skip_hbm, w_ref, out_ref,
    taps_ref, filt_ref, skip_ref,
    w_all, qkv_v, halo, ext_v, ub, qb, ut, qt, skt, hf, mats, y2,
    ta, sa, qa, ra, qp, rp,
    load_sem, own_sem, halo_sem, tail_sem,
    xs, es, er, s2, r2, ys, yr, as1, ar1, as2, ar2, ps,
):
    s = lax.axis_index("seq")
    c = lax.axis_index("chan")
    y = lax.div(s, RING)
    z = lax.rem(s, RING)
    x = lax.div(c, 2)
    p = lax.rem(c, 2)

    def y_at(d):
        return {"seq": lax.rem(y + d + RING, RING) * RING + z}

    def z_at(d):
        return {"seq": y * RING + lax.rem(z + d + 2 * RING, RING)}

    def seq_at(d):
        return {"seq": lax.rem(s + d + RING * RING, RING * RING)}

    sibling = {"chan": c + 1 - 2 * p}
    outer = 2 * lax.rem(z, 2) - 1
    inner = -outer
    started = []

    def remote(src, dst, send, recv, to):
        return pltpu.make_async_remote_copy(
            src_ref=src, dst_ref=dst, send_sem=send, recv_sem=recv, device_id=to, device_id_type=MESH
        )

    def go(make, *args):
        make(*args).start()
        if (make, args) not in started:
            started.append((make, args))

    loads = [
        pltpu.make_async_copy(qkv_ref.at[i], qkv_v.at[i], load_sem.at[i]) for i in (1, 2, 0)
    ]
    loads += [
        pltpu.make_async_copy(taps_hbm, taps_ref, load_sem.at[3]),
        pltpu.make_async_copy(skip_hbm, skip_ref, load_sem.at[5]),
        pltpu.make_async_copy(filt_hbm, filt_ref, load_sem.at[4]),
    ]
    own = pltpu.make_async_copy(w_ref, w_all.at[OWN, NEAR], own_sem)
    for copy in loads[::-1] + [own]:
        copy.start()

    barrier = pltpu.get_barrier_semaphore()
    greeted = [{"chan": lax.rem(c + d, 8)} for d in range(1, 8)]
    greeted += [z_at(outer), z_at(inner), z_at(3 * inner), y_at(1), y_at(-1), seq_at(1), seq_at(-1)]
    for to in greeted:
        pl.semaphore_signal(barrier, inc=1, device_id=to, device_id_type=MESH)

    def toeplitz():
        loads[5].wait()
        hf[...] = filt_ref[...].astype(F32)

        def body(step, carry):
            row = lax.broadcasted_iota(jnp.int32, (SUBS, SPAN), 0)
            col = lax.broadcasted_iota(jnp.int32, (SUBS, SPAN), 1)
            for i in range(4):
                g = step * 4 + i
                base = jnp.broadcast_to(hf[pl.ds(g, 1), :], (SUBS, SPAN))
                for bit in (1, 2, 4):
                    base = jnp.where((row & bit) != 0, pltpu.roll(base, bit, 1), base)
                for pair in range(SPAN // (2 * SUBS)):
                    above, below = [], []
                    for k in (2 * pair, 2 * pair + 1):
                        turned = pltpu.roll(base, SUBS * k, 1) if k else base
                        under = row + SUBS * k > col
                        above.append(jnp.where(under, turned, 0.0))
                        below.append(jnp.where(under, 0.0, turned))
                    at = 2 * SUBS * pair
                    mats[g, at : at + 2 * SUBS] = jnp.concatenate(above, axis=0).astype(BF16)
                    mats[g, SPAN + at : SPAN + at + 2 * SUBS] = jnp.concatenate(below, axis=0).astype(BF16)
            return carry

        lax.fori_loop(0, 16, body, 0)

    def widen():
        for copy in loads[:5]:
            copy.wait()

        def body(strip, carry):
            at = pl.ds(pl.multiple_of(strip * LANES, LANES), LANES)
            for i in range(3):
                ext_v[i, strip, PAD : PAD + ROWS, :] = qkv_v[i, :, at].astype(F32)
                ext_v[i, strip, PAD + ROWS :, :] = jnp.zeros((TALL - ROWS, LANES), F32)
            skt[at, :] = jnp.broadcast_to(skip_ref[:, at], (LANES, LANES)).T
            return carry

        lax.fori_loop(0, STRIPS, body, 0)

    widen()
    pl.semaphore_wait(barrier, len(greeted))

    def cross():
        return remote(w_ref, w_all.at[OWN, CROSS], xs.at[0], xs.at[1], z_at(3 * inner))

    def ext(which, slot):
        src, dst = ((NEAR, NEAR_EXT), (CROSS, CROSS_EXT))[which]
        if slot != OWN:
            src, dst = [pl.ds(at.start + PIECE, PIECE) for at in (src, dst)]
        found = w_ref if slot == OWN and which == 0 else w_all.at[slot, src]
        return remote(found, w_all.at[slot, dst], es.at[which, slot], er.at[which, slot], z_at(outer))

    def ring(direction, step, part):
        lane = 0 if direction == 1 else 1
        rows = PARTS[part]
        into = origin(direction, step)
        came = OWN if step == 1 else origin(direction, step - 1)
        src = w_ref if step == 1 and part == 0 else w_all.at[came, rows]
        at = lane, step - 1, part
        return remote(src, w_all.at[into, rows], s2.at[at], r2.at[at], y_at(direction))

    def lanes_of(step, part):
        if step < 4:
            return (1, -1)
        return (1,) if part < 2 else (-1,)

    def start_part(part):
        for direction in (1, -1):
            go(ring, direction, 1, part)

    def near_arrives():
        ext(0, OWN).wait_recv()
        start_part(1)

    def cross_arrives():
        cross().wait_recv()
        start_part(2)
        go(ext, 1, OWN)

    def cross_ext_arrives():
        ext(1, OWN).wait_recv()
        start_part(3)

    def part_arrives(step, part):
        for direction in lanes_of(step, part):
            ring(direction, step, part).wait_recv()
            if step < 4 and direction in lanes_of(step + 1, part):
                go(ring, direction, step + 1, part)
            if part in (0, 2):
                go(ext, part // 2, origin(direction, step))

    def settle(step):
        for slot in GROUPS[step]:
            for which in range(2):
                ext(which, slot).wait_recv()

    def happen(step, table):
        for at, calls in table.items():
            @pl.when(step == at)
            def run(calls=calls):
                for fn, *args in calls:
                    fn(*args)

    def halo_copy():
        return remote(
            qkv_ref.at[:, ROWS - HALO : ROWS], halo, halo_sem.at[0], halo_sem.at[1], seq_at(1)
        )

    go(cross)
    go(ext, 0, OWN)
    start_part(0)
    go(halo_copy)
    toeplitz()

    def halo_arrives():
        halo_copy().wait_recv()

        def body(strip, carry):
            at = pl.ds(pl.multiple_of(strip * LANES, LANES), LANES)
            for i in range(3):
                before = halo[i, :, at].astype(F32)[HALO - PAD :]
                ext_v[i, strip, :PAD, :] = jnp.where(s == 0, 0.0, before)
            return carry

        lax.fori_loop(0, STRIPS, body, 0)

    def features(strip):
        at = pl.ds(pl.multiple_of(strip * LANES, LANES), LANES)
        taps = [
            [jnp.broadcast_to(taps_ref[i, j : j + 1, at], (SUBS, LANES)) for j in range(FTAPS)]
            for i in range(3)
        ]

        def load(i, r):
            return ext_v[i, strip, pl.ds(PAD + r, SUBS, stride=PITCH), :]

        def line(i, window):
            total = taps[i][0] * window[-1]
            for j in range(1, FTAPS):
                total = total + taps[i][j] * window[-1 - j]
            return total

        def some(turn, windows):
            windows = [list(w) for w in windows]
            for step in range(FTAPS):
                r = turn * FTAPS + step
                found = []
                for i in range(3):
                    windows[i] = windows[i][1 - FTAPS :] + [load(i, r)]
                    found.append(line(i, windows[i]))
                ub[strip, pl.ds(r, SUBS, stride=PITCH), :] = found[1] * found[2]
                qb[strip, pl.ds(r, SUBS, stride=PITCH), :] = found[0]
            return tuple(tuple(w[1 - FTAPS :]) for w in windows)

        start = tuple(tuple(load(i, r) for r in range(1 - FTAPS, 0)) for i in range(3))
        lax.fori_loop(0, PITCH // FTAPS, some, start)
        for b in range(BLOCKS):
            ut[b + 1, at, :] = ub[strip, SPAN * b : SPAN * (b + 1), :].T.astype(BF16)
            qt[b, at, :] = qb[strip, SPAN * b : SPAN * (b + 1), :].T

    def tail(quarter):
        at = pl.ds(pl.multiple_of(quarter * (WIDTH // 4), WIDTH // 4), WIDTH // 4)
        return remote(
            ut.at[BLOCKS, at], ut.at[0, at], tail_sem.at[0, quarter], tail_sem.at[1, quarter], seq_at(1)
        )

    def tail_arrives(quarter):
        tail(quarter).wait_recv()

        @pl.when(s == 0)
        def clear():
            at = pl.ds(pl.multiple_of(quarter * (WIDTH // 4), WIDTH // 4), WIDTH // 4)
            ut[0, at] = jnp.zeros((WIDTH // 4, SPAN), BF16)

    def conv(quarter):
        def body(step, carry):
            base = step * BATCH
            spots = [pl.ds(pl.multiple_of((base + i) * GROUP, GROUP), GROUP) for i in range(BATCH)]
            parts = [[ut[b, at, :] for b in range(BLOCKS + 1)] for at in spots]
            mixed = []
            for i in range(BATCH):
                window = jnp.concatenate(
                    [
                        jnp.concatenate(parts[i][:BLOCKS], axis=0),
                        jnp.concatenate(parts[i][1:], axis=0),
                    ],
                    axis=1,
                )
                mixed.append(jnp.dot(window, mats[base + i], preferred_element_type=F32))
            found = []
            for i, at in enumerate(spots):
                for b in range(BLOCKS):
                    field = mixed[i][GROUP * b : GROUP * (b + 1)] + skt[at, :] * parts[i][b + 1].astype(F32)
                    found.append((qt[b, at, :] * field).astype(BF16))
            for i, at in enumerate(spots):
                for b in range(BLOCKS):
                    y2[0, at, SPAN * b : SPAN * (b + 1)] = found[BLOCKS * i + b]
            happen(step, {
                2: [(cross_ext_arrives,)],
                3: [(part_arrives, 1, 2)],
                4: [(part_arrives, 2, 1)],
                5: [(part_arrives, 1, 3)],
            })
            return carry

        lax.fori_loop(quarter * 2, quarter * 2 + 2, body, 0)

    def swap_y(quarter):
        at = pl.ds(pl.multiple_of(quarter * (WIDTH // 4), WIDTH // 4), WIDTH // 4)
        return remote(y2.at[0, at], y2.at[1, at], ys.at[quarter], yr.at[quarter], z_at(inner))

    def pick(n, table):
        found = -1
        for at, value in table.items():
            found = jnp.where(n == at, value, found)
        return found

    def slot_of(job):
        return jnp.where(job < RING, job, pick(job - RING, {0: 0, 1: 3, 2: 4, 3: 7, 4: 1, 5: 5, 6: 6, 7: 2}))

    def tokens_of(job):
        return lax.div(job, RING)

    def target_of(job):
        slot = slot_of(job)
        off = lax.div(slot + 1, 2) * (2 * lax.rem(slot, 2) - 1)
        return lax.rem(y + off + RING, RING)

    def project(job, half):
        rows = w_all[slot_of(job), pl.ds(pl.multiple_of(half * HALF, HALF), HALF)]
        return jnp.dot(rows, y2[tokens_of(job)], preferred_element_type=F32)

    def swap(job):
        return remote(ta.at[job], sa.at[job], as1.at[job], ar1.at[job], sibling)

    def give(job):
        ta[job] = project(job, 1 - p).astype(BF16)
        swap(job).start()

    def delivery(job):
        tokens = tokens_of(job)
        return remote(
            qa.at[job], ra.at[tokens, x, p], as2.at[job], ar2.at[tokens, x, p], {"chan": target_of(job)}
        )

    def take(job):
        got = project(job, p)
        swap(job).wait_recv()
        qa[job] = (got + sa[job].astype(F32)).astype(BF16)
        to, tokens = target_of(job), tokens_of(job)

        @pl.when(to == c)
        def keep():
            pltpu.make_async_copy(qa.at[job], ra.at[tokens, x, p], ar2.at[tokens, x, p]).start()

        @pl.when(to != c)
        def post():
            delivery(job).start()

    def gathered(tokens, half):
        found = None
        for chip in range(4):
            here = ra.at[tokens, chip, half]
            remote(here, here, as2.at[0], ar2.at[tokens, chip, half], sibling).wait_recv()
        for chip in range(4):
            term = ra[tokens, chip, half].astype(F32)
            found = term if found is None else found + term
        return found

    def hand():
        return remote(qp, rp, ps.at[0], ps.at[1], z_at(inner))

    ahead = lax.rem(c - y + RING, RING)
    ready = jnp.minimum(13 + pick(ahead, {0: 0, 2: 1, 6: 2, 4: 3, 1: 4, 3: 5, 5: 6, 7: 7}), 19)

    def finish():
        for half in range(2):
            qp[half * HALF : (half + 1) * HALF] = gathered(1, half).astype(BF16)
        hand().start()

    def partner_y():
        for quarter in range(4):
            swap_y(quarter).wait_recv()

    halo_arrives()

    def quarters(n, carry):
        @pl.when(n < 4)
        def feature_quarter():
            def body(strip, carry):
                features(strip)
                happen(strip, {
                    1: [(near_arrives,)],
                    2: [(part_arrives, 1, 0)],
                    4: [(cross_arrives,)],
                    5: [(part_arrives, 1, 1)],
                    7: [(part_arrives, 2, 0)],
                })
                return carry

            lax.fori_loop(n * 2, n * 2 + 2, body, 0)
            tail(n).start()

        @pl.when(n >= 2)
        def conv_quarter():
            tail_arrives(n - 2)
            conv(n - 2)
            swap_y(n - 2).start()

        return carry

    lax.fori_loop(0, 6, quarters, 0)
    own.wait()

    def turn(n, carry):
        @pl.when((n >= 2) & (n < JOBS + 2))
        def second():
            take(n - 2)

        @pl.when(n == ready)
        def partner_sum():
            finish()

        happen(n, {
            0: [(part_arrives, 2, 2)],
            1: [(settle, 1)],
            2: [(part_arrives, 2, 3), (part_arrives, 3, 0)],
            3: [(settle, 2), (part_arrives, 3, 1)],
            4: [(part_arrives, 3, 2)],
            5: [(part_arrives, 3, 3), (part_arrives, 4, 0), (settle, 3)],
            6: [(part_arrives, 4, 1), (part_arrives, 4, 2)],
            7: [(part_arrives, 4, 3), (settle, 4)],
            8: [(partner_y,)],
        })

        @pl.when(n < JOBS)
        def first():
            give(n)

        return carry

    lax.fori_loop(0, JOBS + 4, turn, 0)

    def place(z_from, rows):
        at = lax.rem(z + z_from + 2 * RING, RING) * (2 * PIECE)
        out_ref[pl.ds(pl.multiple_of(at, 2 * PIECE), 2 * PIECE), :] = rows

    for half in range(2):
        found = gathered(0, half).astype(BF16)
        for i, z_from in enumerate(((0, outer + 4), (outer, 4))[half]):
            place(z_from, found[2 * PIECE * i : 2 * PIECE * (i + 1)])
    hand().wait_recv()
    for i, z_from in enumerate((inner, 2 * inner + 4, 2 * inner, inner + 4)):
        place(z_from, rp[2 * PIECE * i : 2 * PIECE * (i + 1)])

    for make, args in started:
        make(*args).wait_send()
    hand().wait_send()

    def drain_quarter(quarter, carry):
        tail(quarter).wait_send()
        swap_y(quarter).wait_send()
        return carry

    lax.fori_loop(0, 4, drain_quarter, 0)

    def drain(job, carry):
        swap(job).wait_send()

        @pl.when(target_of(job) != c)
        def sent():
            delivery(job).wait_send()

        return carry

    lax.fori_loop(0, JOBS, drain, 0)


def local(qkv, feat_taps, long_filter, skip_gain, out_weight):
    anywhere = pl.BlockSpec(memory_space=pl.ANY)
    dma = pltpu.SemaphoreType.DMA
    return pl.pallas_call(
        kernel,
        out_shape=jax.ShapeDtypeStruct((512, ROWS), BF16),
        in_specs=[anywhere] * 5,
        out_specs=pl.BlockSpec(memory_space=pltpu.VMEM),
        scratch_shapes=[
            pltpu.VMEM((3, FTAPS, WIDTH), F32),
            pltpu.VMEM((WIDTH // GROUP, SPAN), BF16),
            pltpu.VMEM((1, WIDTH), F32),
            pltpu.VMEM((RING, 8 * PIECE, WIDTH), BF16),
            pltpu.VMEM((3, ROWS, WIDTH), BF16),
            pltpu.VMEM((3, HALO, WIDTH), BF16),
            pltpu.VMEM((3, STRIPS, PAD + TALL, LANES), F32),
            pltpu.VMEM((STRIPS, TALL, LANES), F32),
            pltpu.VMEM((STRIPS, TALL, LANES), F32),
            pltpu.VMEM((BLOCKS + 1, WIDTH, SPAN), BF16),
            pltpu.VMEM((BLOCKS, WIDTH, SPAN), F32),
            pltpu.VMEM((WIDTH, SPAN), F32),
            pltpu.VMEM((WIDTH // GROUP, SPAN), F32),
            pltpu.VMEM((WIDTH // GROUP, 2 * SPAN, SPAN), BF16),
            pltpu.VMEM((2, WIDTH, ROWS), BF16),
            pltpu.VMEM((JOBS, HALF, ROWS), BF16),
            pltpu.VMEM((JOBS, HALF, ROWS), BF16),
            pltpu.VMEM((JOBS, HALF, ROWS), BF16),
            pltpu.VMEM((2, 4, 2, HALF, ROWS), BF16),
            pltpu.VMEM((2 * HALF, ROWS), BF16),
            pltpu.VMEM((2 * HALF, ROWS), BF16),
            dma((6,)), dma, dma((2,)), dma((2, 4)),
            dma((2,)), dma((2, RING)), dma((2, RING)),
            dma((2, 4, 4)), dma((2, 4, 4)), dma((4,)), dma((4,)),
            dma((JOBS,)), dma((JOBS,)), dma((JOBS,)), dma((2, 4, 2)), dma((2,)),
        ],
        compiler_params=pltpu.CompilerParams(
            collective_id=0, has_side_effects=True, vmem_limit_bytes=56 * 2**20
        ),
    )(qkv, feat_taps, long_filter.T, skip_gain.reshape(1, WIDTH), out_weight.T).T


def solution(mesh):
    return jax.shard_map(
        local,
        mesh=mesh,
        in_specs=(
            P(None, "seq", "chan"),
            P(None, None, "chan"),
            P(None, "chan"),
            P("chan"),
            P("chan", "seq"),
        ),
        out_specs=P("seq", "chan"),
        check_vma=False,
    )
```

```python
import jax
import jax.numpy as jnp
from jax import lax
from jax.experimental import pallas as pl
from jax.experimental.pallas import tpu as pltpu
from jax.sharding import PartitionSpec as P

MESH = pl.DeviceIdType.MESH
F32 = jnp.float32
BF16 = jnp.bfloat16

RING = 8
GROUP = 16
SPAN = 128
FTAPS = 7
ROWS = 384
WIDTH = 1024
BLOCKS = ROWS // SPAN
LANES = 128
STRIPS = WIDTH // LANES
PIECE = 32
HALO = 16
PAD = 8

OFF = (1, -1, 2, -2, 3, -3, 4, 0)
SLOT = {off: slot for slot, off in enumerate(OFF)}
PACKS = ((7, 8), (0, 2), (2, 4), (4, 6), (6, 7))
FAR_UP = ((0, 4), (0,))
OWN = SLOT[0]
FAR = SLOT[4]
PAIRS = 3


def origin(direction, step):
    return SLOT[4 if step == 4 else -direction * step]


def kernel(
    qkv_ref, taps_hbm, filt_hbm, skip_hbm, w_ref, out_ref,
    taps_ref, filt_ref, skip_ref,
    w_all, qkv_v, halo, ext, ut, qt, skt, hf, yt,
    ta, sa, qa, ra, rb, rc,
    load_sem, own_sem, halo_sem, tail_sem,
    s1, r1, s2, r2, as1, ar1, as2, ar2, bs2, br2, cs2, cr2,
):
    s = lax.axis_index("seq")
    c = lax.axis_index("chan")
    y = lax.div(s, RING)
    z = lax.rem(s, RING)
    x = lax.div(c, 2)
    p = lax.rem(c, 2)

    def y_at(d):
        return {"seq": lax.rem(y + d + RING, RING) * RING + z}

    def z_at(d):
        return {"seq": y * RING + lax.rem(z + d + RING, RING)}

    def seq_at(d):
        return {"seq": lax.rem(s + d + RING * RING, RING * RING)}

    sibling = {"chan": c + 1 - 2 * p}
    minor_at = (z_at, y_at)
    major_at = (y_at, z_at)
    started = []

    def remote(src, dst, send, recv, to):
        return pltpu.make_async_remote_copy(
            src_ref=src, dst_ref=dst, send_sem=send, recv_sem=recv, device_id=to, device_id_type=MESH
        )

    def go(copy):
        copy.start()
        started.append(copy)

    barrier = pltpu.get_barrier_semaphore()
    greeted = [{"chan": lax.rem(c + d, 8)} for d in range(1, 8)]
    greeted += [z_at(1), z_at(-1), y_at(1), y_at(-1), seq_at(1), seq_at(-1)]
    for to in greeted:
        pl.semaphore_signal(barrier, inc=1, device_id=to, device_id_type=MESH)

    loads = [
        pltpu.make_async_copy(qkv_ref.at[i], qkv_v.at[i], load_sem.at[i]) for i in (1, 2, 0)
    ]
    loads += [
        pltpu.make_async_copy(taps_hbm, taps_ref, load_sem.at[3]),
        pltpu.make_async_copy(filt_hbm, filt_ref, load_sem.at[4]),
        pltpu.make_async_copy(skip_hbm, skip_ref, load_sem.at[5]),
    ]
    own = [
        pltpu.make_async_copy(
            w_ref.at[PIECE * kind : PIECE * (kind + 1)], w_all.at[kind, OWN, OWN], own_sem.at[kind]
        )
        for kind in range(2)
    ]
    for copy in loads + own:
        copy.start()

    pl.semaphore_wait(barrier, len(greeted))

    def first(kind, direction, step):
        lane = 0 if direction == 1 else 1
        into = origin(direction, step)
        if step == 1:
            src, dst = w_ref.at[PIECE * kind : PIECE * (kind + 1)], w_all.at[kind, OWN, into]
        elif step < 4:
            src, dst = w_all.at[kind, OWN, origin(direction, step - 1)], w_all.at[kind, OWN, into]
        else:
            half = pl.ds(lane * (PIECE // 2), PIECE // 2)
            src = w_all.at[kind, OWN, origin(direction, 3), half]
            dst = w_all.at[kind, OWN, into, half]
        at = kind, lane, step - 1
        return remote(src, dst, s1.at[at], r1.at[at], minor_at[kind](direction))

    def second(kind, direction, step, pack):
        lane = 0 if direction == 1 else 1
        lo, hi = PACKS[pack]
        into = origin(direction, step)
        if step == 1 and pack == 0:
            src, dst = w_ref.at[PIECE * kind : PIECE * (kind + 1)], w_all.at[kind, into, OWN]
        else:
            came = OWN if step == 1 else origin(direction, step - 1)
            src = w_all.at[kind, came, pl.ds(lo, hi - lo)]
            dst = w_all.at[kind, into, pl.ds(lo, hi - lo)]
        at = kind, lane, step - 1, pack
        return remote(src, dst, s2.at[at], r2.at[at], major_at[kind](direction))

    def lanes_of(kind, step, pack):
        if step < 4:
            return (1, -1)
        return (1,) if pack in FAR_UP[kind] else (-1,)

    def first_arrives(step):
        for kind in range(2):
            for direction in (1, -1):
                first(kind, direction, step).wait_recv()
                if step < 4:
                    go(first(kind, direction, step + 1))
        for kind in range(2):
            for direction in (1, -1):
                go(second(kind, direction, 1, step))

    def second_arrives(step, pack):
        for kind in range(2):
            for direction in lanes_of(kind, step, pack):
                second(kind, direction, step, pack).wait_recv()
                if step < 4 and direction in lanes_of(kind, step + 1, pack):
                    go(second(kind, direction, step + 1, pack))

    events = [(2.2 * k, first_arrives, (k,)) for k in range(1, 5)]
    events += [
        (2.6 + 10.5 * (k - 1) + 2.4 * g, second_arrives, (k, g)) for k in range(1, 5) for g in range(5)
    ]
    events.sort(key=lambda e: e[0])
    events = [(at, fn, args) for at, fn, args in events]
    clock = [0.0]
    seen = set()

    def take_event():
        at, fn, args = events.pop(0)
        fn(*args)
        if fn is second_arrives:
            seen.add(args)
        else:
            seen.add(args[0])
        clock[0] = max(clock[0], at)

    def work(cost, fn, *args):
        while events and events[0][0] <= clock[0]:
            take_event()
        fn(*args)
        clock[0] += cost

    def need(step):
        wanted = {(step, g) for g in range(5)}
        while not wanted <= seen:
            take_event()

    halo_copy = remote(
        qkv_ref.at[:, ROWS - HALO : ROWS], halo, halo_sem.at[0], halo_sem.at[1], seq_at(1)
    )
    for kind in range(2):
        for direction in (1, -1):
            go(first(kind, direction, 1))
    for kind in range(2):
        for direction in (1, -1):
            go(second(kind, direction, 1, 0))
    go(halo_copy)

    def widen(strip):
        at = pl.ds(pl.multiple_of(strip * LANES, LANES), LANES)
        for i in range(3):
            ext[i, strip, PAD:, :] = qkv_v[i, :, at].astype(F32)

    def widen_halo(strip):
        at = pl.ds(pl.multiple_of(strip * LANES, LANES), LANES)
        for i in range(3):
            before = halo[i, :, at].astype(F32)[HALO - PAD :]
            ext[i, strip, :PAD, :] = jnp.where(s == 0, 0.0, before)

    def feature(i, block, strip, at):
        total = None
        for j in range(FTAPS):
            term = taps_ref[i, j : j + 1, at] * ext[i, strip, pl.ds(PAD + SPAN * block - j, SPAN), :]
            total = term if total is None else total + term
        return total

    def features(block, strips):
        def body(strip, carry):
            at = pl.ds(pl.multiple_of(strip * LANES, LANES), LANES)
            u = (feature(1, block, strip, at) * feature(2, block, strip, at)).astype(BF16).astype(F32)
            ut[block + 1, at, :] = u.T.astype(BF16)
            qt[block, at, :] = feature(0, block, strip, at).T
            return carry

        lax.fori_loop(strips[0], strips[1], body, 0)

    def widen_all():
        for copy in loads:
            copy.wait()

        def body(strip, carry):
            widen(strip)
            return carry

        lax.fori_loop(0, STRIPS, body, 0)
        hf[...] = filt_ref[...].astype(F32)

    def halo_arrives():
        halo_copy.wait_recv()

        def body(strip, carry):
            widen_halo(strip)
            at = pl.ds(pl.multiple_of(strip * LANES, LANES), LANES)
            skt[at, :] = jnp.broadcast_to(skip_ref[:, at], (LANES, LANES)).T
            return carry

        lax.fori_loop(0, STRIPS, body, 0)

    tail_copy = remote(ut.at[BLOCKS], ut.at[0], tail_sem.at[0], tail_sem.at[1], seq_at(1))

    def send_tail():
        go(tail_copy)

    def tail_arrives():
        tail_copy.wait_recv()

        @pl.when(s == 0)
        def clear():
            ut[0] = jnp.zeros((WIDTH, SPAN), BF16)

    def conv(lo, hi):
        def body(g, carry):
            row = lax.broadcasted_iota(jnp.int32, (SPAN, SPAN), 0)
            col = lax.broadcasted_iota(jnp.int32, (SPAN, SPAN), 1)
            taps = jnp.broadcast_to(hf[pl.ds(g, 1), :], (SPAN, SPAN))
            ring = pltpu.roll(taps, 0, 1, stride=1, stride_axis=0)
            here = jnp.where(row <= col, ring, 0.0)
            before = jnp.where(row > col, ring, 0.0)
            matrix = jnp.concatenate([before, here], axis=0).astype(BF16)
            at = pl.ds(pl.multiple_of(g * GROUP, GROUP), GROUP)
            parts = [ut[b, at, :] for b in range(BLOCKS + 1)]
            window = jnp.concatenate(
                [jnp.concatenate(parts[:BLOCKS], axis=0), jnp.concatenate(parts[1:], axis=0)], axis=1
            )
            mixed = jnp.dot(window, matrix, preferred_element_type=F32)
            for b in range(BLOCKS):
                field = mixed[GROUP * b : GROUP * (b + 1)] + skt[at, :] * parts[b + 1].astype(F32)
                yt[at, SPAN * b : SPAN * (b + 1)] = (qt[b, at, :] * field).astype(BF16)
            return carry

        lax.fori_loop(lo, hi, body, 0, unroll=4)

    def project(pieces):
        rows = jnp.concatenate(pieces, axis=0) if len(pieces) > 1 else pieces[0]
        return jnp.dot(rows, yt[...], preferred_element_type=F32)

    def two(kind, major, batch, half):
        return w_all[kind, major, pl.ds(4 * batch + 2 * half, 2)].reshape(2 * PIECE, WIDTH)

    def four(kind, major, half):
        return [two(kind, major, batch, half) for batch in range(2)]

    def target(slot):
        return lax.rem(y + OFF[slot] + RING, RING)

    delivered = []

    def deliver(src, dst, send, recv, to):
        copy = remote(src, dst, send, recv, {"chan": to})

        @pl.when(to == c)
        def keep():
            pltpu.make_async_copy(src, dst, recv).start()

        @pl.when(to != c)
        def post():
            copy.start()

        delivered.append((to, copy))

    STARTS = (0, 256, 768, 1280, 1792, 1920)
    COUNTS = (256, 512, 512, 512, 128, 128)

    def b_rows(turn, half):
        return w_all[1, 2 * turn + half].reshape(RING * PIECE, WIDTH)

    def pieces(bundle, half):
        if bundle == 0:
            return four(0, OWN, half) + four(1, OWN, half)
        if bundle < 4:
            low = 2 * (bundle - 1)
            return four(0, low, half) + four(0, low + 1, half) + [b_rows(bundle - 1, half)]
        return [two(kind, FAR, bundle - 4, half) for kind in range(2)]

    def rows_of(bundle):
        return slice(STARTS[bundle], STARTS[bundle] + COUNTS[bundle])

    def swap(bundle):
        at = pl.ds(STARTS[bundle], COUNTS[bundle])
        return remote(ta.at[at], sa.at[at], as1.at[bundle], ar1.at[bundle], sibling)

    def give(bundle):
        ta[rows_of(bundle)] = project(pieces(bundle, 1 - p)).astype(BF16)
        copy = swap(bundle)
        go(copy)

    def post_row(slot, at, many, batch):
        deliver(
            qa.at[at : at + many], ra.at[x, p, pl.ds(2 * PIECE * batch, many)],
            as2.at[slot, batch], ar2.at[x, p], target(slot),
        )

    def post_single(single, batch, at):
        for i in range(2):
            to = lax.rem(y + jnp.where(p == 0, OFF[4 * batch + i], OFF[4 * batch + 2 + i]) + RING, RING)
            deliver(
                qa.at[at + PIECE * i : at + PIECE * (i + 1)], rc.at[single, x],
                cs2.at[single, batch, i], cr2.at[single, x], to,
            )

    def take(bundle):
        got = project(pieces(bundle, p))
        swap(bundle).wait_recv()
        at = rows_of(bundle)
        qa[at] = (got + sa[at].astype(F32)).astype(BF16)
        start = STARTS[bundle]
        if bundle == 0:
            post_row(OWN, start, 4 * PIECE, 0)
            for batch in range(2):
                post_single(0, batch, start + 4 * PIECE + 2 * PIECE * batch)
        elif bundle < 4:
            turn = bundle - 1
            for i in range(2):
                post_row(2 * turn + i, start + 4 * PIECE * i, 4 * PIECE, 0)
            for m in range(RING):
                from_row = start + 8 * PIECE + PIECE * m
                deliver(
                    qa.at[from_row : from_row + PIECE], rb.at[turn, x, p],
                    bs2.at[turn, m], br2.at[turn, x, p], target(m),
                )
        else:
            post_row(FAR, start, 2 * PIECE, bundle - 4)
            post_single(1, bundle - 4, start + 2 * PIECE)

    def own_wait():
        for copy in own:
            copy.wait()

    def place(kind, slot, rows):
        at = lax.rem(z + OFF[slot] + RING, RING) * (2 * PIECE) + kind * PIECE
        out_ref[pl.ds(pl.multiple_of(at, PIECE), PIECE), :] = rows.astype(BF16)

    def total(refs):
        found = None
        for ref in refs:
            term = ref[...].astype(F32)
            found = term if found is None else found + term
        return found

    def arrived(ref, sem):
        remote(ref, ref, cs2.at[0, 0, 0], sem, sibling).wait_recv()

    def pair_sums(turn):
        for half in range(2):
            for chip in range(4):
                arrived(rb.at[turn, chip, half], br2.at[turn, chip, half])
            place(1, 2 * turn + half, total([rb.at[turn, chip, half] for chip in range(4)]))

    def single_sums(single, slot):
        for chip in range(4):
            arrived(rc.at[single, chip], cr2.at[single, chip])
        place(1, slot, total([rc.at[single, chip] for chip in range(4)]))

    def row_sums():
        for half in range(2):
            for chip in range(4):
                arrived(ra.at[chip, half], ar2.at[chip, half])
            found = total([ra.at[chip, half] for chip in range(4)])
            for i in range(4):
                slot = 4 * (i // 2) + 2 * half + i % 2
                place(0, slot, found[PIECE * i : PIECE * (i + 1)])

    work(1.0, widen_all)
    for lo in (0, 4):
        work(1.4, features, BLOCKS - 1, (lo, lo + 4))
    work(0.1, send_tail)
    for lo in (0, 4):
        work(1.4, features, 1, (lo, lo + 4))
    work(0.3, halo_arrives)
    for lo in (0, 4):
        work(1.4, features, 0, (lo, lo + 4))
    work(0.1, tail_arrives)
    for lo in range(0, 64, 16):
        work(1.5, conv, lo, lo + 16)
    work(0.1, own_wait)
    work(1.0, give, 0)
    work(1.0, take, 0)
    for k in (1, 2, 3):
        need(k)
        work(1.8, give, k)
        work(2.2, take, k)
    while not {(4, g) for g in (0, 1, 2)} <= seen:
        take_event()
    give(4)
    take(4)
    need(4)
    give(5)
    pair_sums(0)
    pair_sums(1)
    single_sums(0, OWN)
    take(5)
    pair_sums(2)
    single_sums(1, FAR)
    row_sums()

    for copy in started:
        copy.wait_send()
    for to, copy in delivered:
        @pl.when(to != c)
        def drain(copy=copy):
            copy.wait_send()


def local(qkv, feat_taps, long_filter, skip_gain, out_weight):
    vmem = pl.BlockSpec(memory_space=pltpu.VMEM)
    anywhere = pl.BlockSpec(memory_space=pl.ANY)
    dma = pltpu.SemaphoreType.DMA
    half_piece = (4 * PIECE, ROWS)
    return pl.pallas_call(
        kernel,
        out_shape=jax.ShapeDtypeStruct((512, ROWS), BF16),
        in_specs=[anywhere] * 5,
        out_specs=vmem,
        scratch_shapes=[
            pltpu.VMEM((3, FTAPS, WIDTH), F32),
            pltpu.VMEM((WIDTH // GROUP, SPAN), BF16),
            pltpu.VMEM((1, WIDTH), F32),
            pltpu.VMEM((2, RING, RING, PIECE, WIDTH), BF16),
            pltpu.VMEM((3, ROWS, WIDTH), BF16),
            pltpu.VMEM((3, HALO, WIDTH), BF16),
            pltpu.VMEM((3, STRIPS, PAD + ROWS, LANES), F32),
            pltpu.VMEM((BLOCKS + 1, WIDTH, SPAN), BF16),
            pltpu.VMEM((BLOCKS, WIDTH, SPAN), F32),
            pltpu.VMEM((WIDTH, SPAN), F32),
            pltpu.VMEM((WIDTH // GROUP, SPAN), F32),
            pltpu.VMEM((WIDTH, ROWS), BF16),
            pltpu.VMEM((2048, ROWS), BF16),
            pltpu.VMEM((2048, ROWS), BF16),
            pltpu.VMEM((2048, ROWS), BF16),
            pltpu.VMEM((4, 2) + half_piece, BF16),
            pltpu.VMEM((PAIRS, 4, 2, PIECE, ROWS), BF16),
            pltpu.VMEM((2, 4, PIECE, ROWS), BF16),
            dma((6,)), dma((2,)), dma((2,)), dma((2,)),
            dma((2, 2, 4)), dma((2, 2, 4)),
            dma((2, 2, 4, 5)), dma((2, 2, 4, 5)),
            dma((6,)), dma((6,)), dma((RING, 2)), dma((4, 2)),
            dma((PAIRS, RING)), dma((PAIRS, 4, 2)), dma((2, 2, 2)), dma((2, 4)),
        ],
        compiler_params=pltpu.CompilerParams(
            collective_id=0, has_side_effects=True, vmem_limit_bytes=56 * 2**20
        ),
    )(qkv, feat_taps, long_filter.T, skip_gain.reshape(1, WIDTH), out_weight.T).T


def solution(mesh):
    return jax.shard_map(
        local,
        mesh=mesh,
        in_specs=(
            P(None, "seq", "chan"),
            P(None, None, "chan"),
            P(None, "chan"),
            P("chan"),
            P("chan", "seq"),
        ),
        out_specs=P("seq", "chan"),
        check_vma=False,
    )
```

```python
import jax
import jax.numpy as jnp
from jax import lax
from jax.experimental import pallas as pl
from jax.experimental.pallas import tpu as pltpu
from jax.sharding import PartitionSpec as P

MESH = pl.DeviceIdType.MESH
F32 = jnp.float32
BF16 = jnp.bfloat16

RING = 8
GROUP = 16
SPAN = 128
FTAPS = 7
ROWS = 384
WIDTH = 1024
BLOCKS = ROWS // SPAN
LANES = 128
STRIPS = WIDTH // LANES
PIECE = 32
HALO = 16
PAD = 8

OFF = (1, -1, 2, -2, 3, -3, 4, 0)
SLOT = {off: slot for slot, off in enumerate(OFF)}
PACKS = ((7, 8), (0, 2), (2, 4), (4, 6), (6, 7))
FAR_UP = ((0, 4), (0,))
OWN = SLOT[0]
FAR = SLOT[4]
PAIRS = 3


def origin(direction, step):
    return SLOT[4 if step == 4 else -direction * step]


def kernel(
    qkv_ref, taps_hbm, filt_hbm, skip_hbm, w_ref, out_ref,
    taps_ref, filt_ref, skip_ref,
    w_all, qkv_v, halo, ext, ut, qt, skt, hf, yt,
    ta, sa, qa, ra, rb, rc,
    load_sem, own_sem, halo_sem, tail_sem,
    s1, r1, s2, r2, as1, ar1, as2, ar2, bs2, br2, cs2, cr2,
):
    s = lax.axis_index("seq")
    c = lax.axis_index("chan")
    y = lax.div(s, RING)
    z = lax.rem(s, RING)
    x = lax.div(c, 2)
    p = lax.rem(c, 2)

    def y_at(d):
        return {"seq": lax.rem(y + d + RING, RING) * RING + z}

    def z_at(d):
        return {"seq": y * RING + lax.rem(z + d + RING, RING)}

    def seq_at(d):
        return {"seq": lax.rem(s + d + RING * RING, RING * RING)}

    sibling = {"chan": c + 1 - 2 * p}
    minor_at = (z_at, y_at)
    major_at = (y_at, z_at)
    started = []

    def remote(src, dst, send, recv, to):
        return pltpu.make_async_remote_copy(
            src_ref=src, dst_ref=dst, send_sem=send, recv_sem=recv, device_id=to, device_id_type=MESH
        )

    def go(copy):
        copy.start()
        started.append(copy)

    barrier = pltpu.get_barrier_semaphore()
    greeted = [{"chan": lax.rem(c + d, 8)} for d in range(1, 8)]
    greeted += [z_at(1), z_at(-1), y_at(1), y_at(-1), seq_at(1), seq_at(-1)]
    for to in greeted:
        pl.semaphore_signal(barrier, inc=1, device_id=to, device_id_type=MESH)

    loads = [
        pltpu.make_async_copy(qkv_ref.at[i], qkv_v.at[i], load_sem.at[i]) for i in (1, 2, 0)
    ]
    loads += [
        pltpu.make_async_copy(taps_hbm, taps_ref, load_sem.at[3]),
        pltpu.make_async_copy(filt_hbm, filt_ref, load_sem.at[4]),
        pltpu.make_async_copy(skip_hbm, skip_ref, load_sem.at[5]),
    ]
    own = [
        pltpu.make_async_copy(
            w_ref.at[PIECE * kind : PIECE * (kind + 1)], w_all.at[kind, OWN, OWN], own_sem.at[kind]
        )
        for kind in range(2)
    ]
    for copy in loads + own:
        copy.start()

    pl.semaphore_wait(barrier, len(greeted))

    def first(kind, direction, step):
        lane = 0 if direction == 1 else 1
        into = origin(direction, step)
        if step == 1:
            src, dst = w_ref.at[PIECE * kind : PIECE * (kind + 1)], w_all.at[kind, OWN, into]
        elif step < 4:
            src, dst = w_all.at[kind, OWN, origin(direction, step - 1)], w_all.at[kind, OWN, into]
        else:
            half = pl.ds(lane * (PIECE // 2), PIECE // 2)
            src = w_all.at[kind, OWN, origin(direction, 3), half]
            dst = w_all.at[kind, OWN, into, half]
        at = kind, lane, step - 1
        return remote(src, dst, s1.at[at], r1.at[at], minor_at[kind](direction))

    def second(kind, direction, step, pack):
        lane = 0 if direction == 1 else 1
        lo, hi = PACKS[pack]
        into = origin(direction, step)
        if step == 1 and pack == 0:
            src, dst = w_ref.at[PIECE * kind : PIECE * (kind + 1)], w_all.at[kind, into, OWN]
        else:
            came = OWN if step == 1 else origin(direction, step - 1)
            src = w_all.at[kind, came, pl.ds(lo, hi - lo)]
            dst = w_all.at[kind, into, pl.ds(lo, hi - lo)]
        at = kind, lane, step - 1, pack
        return remote(src, dst, s2.at[at], r2.at[at], major_at[kind](direction))

    def lanes_of(kind, step, pack):
        if step < 4:
            return (1, -1)
        return (1,) if pack in FAR_UP[kind] else (-1,)

    def first_arrives(step):
        for kind in range(2):
            for direction in (1, -1):
                first(kind, direction, step).wait_recv()
                if step < 4:
                    go(first(kind, direction, step + 1))
        for kind in range(2):
            for direction in (1, -1):
                go(second(kind, direction, 1, step))

    def second_arrives(step, pack):
        for kind in range(2):
            for direction in lanes_of(kind, step, pack):
                second(kind, direction, step, pack).wait_recv()
                if step < 4 and direction in lanes_of(kind, step + 1, pack):
                    go(second(kind, direction, step + 1, pack))

    events = [(2.2 * k, first_arrives, (k,)) for k in range(1, 5)]
    events += [
        (2.6 + 10.5 * (k - 1) + 2.4 * g, second_arrives, (k, g)) for k in range(1, 4) for g in range(5)
    ]
    events.sort(key=lambda e: e[0])
    events = [(at, fn, args) for at, fn, args in events]
    clock = [0.0]
    seen = set()

    def take_event():
        at, fn, args = events.pop(0)
        fn(*args)
        if fn is second_arrives:
            seen.add(args)
        else:
            seen.add(args[0])
        clock[0] = max(clock[0], at)

    def work(cost, fn, *args):
        while events and events[0][0] <= clock[0]:
            take_event()
        fn(*args)
        clock[0] += cost

    def need(step):
        wanted = {(step, g) for g in range(5)}
        while not wanted <= seen:
            take_event()

    halo_copy = remote(
        qkv_ref.at[:, ROWS - HALO : ROWS], halo, halo_sem.at[0], halo_sem.at[1], seq_at(1)
    )
    for kind in range(2):
        for direction in (1, -1):
            go(first(kind, direction, 1))
    for kind in range(2):
        for direction in (1, -1):
            go(second(kind, direction, 1, 0))
    go(halo_copy)

    def widen(strip):
        at = pl.ds(pl.multiple_of(strip * LANES, LANES), LANES)
        for i in range(3):
            ext[i, strip, PAD:, :] = qkv_v[i, :, at].astype(F32)

    def widen_halo(strip):
        at = pl.ds(pl.multiple_of(strip * LANES, LANES), LANES)
        for i in range(3):
            before = halo[i, :, at].astype(F32)[HALO - PAD :]
            ext[i, strip, :PAD, :] = jnp.where(s == 0, 0.0, before)

    def feature(i, block, strip, at):
        total = None
        for j in range(FTAPS):
            term = taps_ref[i, j : j + 1, at] * ext[i, strip, pl.ds(PAD + SPAN * block - j, SPAN), :]
            total = term if total is None else total + term
        return total

    def features(block, strips):
        def body(strip, carry):
            at = pl.ds(pl.multiple_of(strip * LANES, LANES), LANES)
            u = (feature(1, block, strip, at) * feature(2, block, strip, at)).astype(BF16).astype(F32)
            ut[block + 1, at, :] = u.T.astype(BF16)
            qt[block, at, :] = feature(0, block, strip, at).T
            return carry

        lax.fori_loop(strips[0], strips[1], body, 0)

    def widen_all():
        for copy in loads:
            copy.wait()

        def body(strip, carry):
            widen(strip)
            return carry

        lax.fori_loop(0, STRIPS, body, 0)
        hf[...] = filt_ref[...].astype(F32)

    def halo_arrives():
        halo_copy.wait_recv()

        def body(strip, carry):
            widen_halo(strip)
            at = pl.ds(pl.multiple_of(strip * LANES, LANES), LANES)
            skt[at, :] = jnp.broadcast_to(skip_ref[:, at], (LANES, LANES)).T
            return carry

        lax.fori_loop(0, STRIPS, body, 0)

    tail_copy = remote(ut.at[BLOCKS], ut.at[0], tail_sem.at[0], tail_sem.at[1], seq_at(1))

    def send_tail():
        go(tail_copy)

    def tail_arrives():
        tail_copy.wait_recv()

        @pl.when(s == 0)
        def clear():
            ut[0] = jnp.zeros((WIDTH, SPAN), BF16)

    def conv(lo, hi):
        def body(g, carry):
            row = lax.broadcasted_iota(jnp.int32, (SPAN, SPAN), 0)
            col = lax.broadcasted_iota(jnp.int32, (SPAN, SPAN), 1)
            taps = jnp.broadcast_to(hf[pl.ds(g, 1), :], (SPAN, SPAN))
            ring = pltpu.roll(taps, 0, 1, stride=1, stride_axis=0)
            here = jnp.where(row <= col, ring, 0.0)
            before = jnp.where(row > col, ring, 0.0)
            matrix = jnp.concatenate([before, here], axis=0).astype(BF16)
            at = pl.ds(pl.multiple_of(g * GROUP, GROUP), GROUP)
            parts = [ut[b, at, :] for b in range(BLOCKS + 1)]
            window = jnp.concatenate(
                [jnp.concatenate(parts[:BLOCKS], axis=0), jnp.concatenate(parts[1:], axis=0)], axis=1
            )
            mixed = jnp.dot(window, matrix, preferred_element_type=F32)
            for b in range(BLOCKS):
                field = mixed[GROUP * b : GROUP * (b + 1)] + skt[at, :] * parts[b + 1].astype(F32)
                yt[at, SPAN * b : SPAN * (b + 1)] = (qt[b, at, :] * field).astype(BF16)
            return carry

        lax.fori_loop(lo, hi, body, 0, unroll=4)

    def project(pieces):
        rows = jnp.concatenate(pieces, axis=0) if len(pieces) > 1 else pieces[0]
        return jnp.dot(rows, yt[...], preferred_element_type=F32)

    def two(kind, major, batch, half):
        return w_all[kind, major, pl.ds(4 * batch + 2 * half, 2)].reshape(2 * PIECE, WIDTH)

    def four(kind, major, half):
        return [two(kind, major, batch, half) for batch in range(2)]

    def target(slot):
        return lax.rem(y + OFF[slot] + RING, RING)

    delivered = []

    def deliver(src, dst, send, recv, to):
        copy = remote(src, dst, send, recv, {"chan": to})

        @pl.when(to == c)
        def keep():
            pltpu.make_async_copy(src, dst, recv).start()

        @pl.when(to != c)
        def post():
            copy.start()

        delivered.append((to, copy))

    STARTS = (0, 256, 768, 1280, 1792, 1856, 1920, 1984)
    COUNTS = (256, 512, 512, 512, 64, 64, 64, 64)

    def b_rows(turn, half):
        return w_all[1, 2 * turn + half].reshape(RING * PIECE, WIDTH)

    def pieces(bundle, half):
        if bundle == 0:
            return four(0, OWN, half) + four(1, OWN, half)
        if bundle < 4:
            low = 2 * (bundle - 1)
            return four(0, low, half) + four(0, low + 1, half) + [b_rows(bundle - 1, half)]
        return [two(bundle % 2, FAR, bundle // 2 - 2, half)]

    def rows_of(bundle):
        return slice(STARTS[bundle], STARTS[bundle] + COUNTS[bundle])

    def swap(bundle):
        at = pl.ds(STARTS[bundle], COUNTS[bundle])
        return remote(ta.at[at], sa.at[at], as1.at[bundle], ar1.at[bundle], sibling)

    def give(bundle):
        ta[rows_of(bundle)] = project(pieces(bundle, 1 - p)).astype(BF16)
        copy = swap(bundle)
        go(copy)

    def post_row(slot, at, many, batch):
        deliver(
            qa.at[at : at + many], ra.at[x, p, pl.ds(2 * PIECE * batch, many)],
            as2.at[slot, batch], ar2.at[x, p], target(slot),
        )

    def post_single(single, batch, at):
        for i in range(2):
            to = lax.rem(y + jnp.where(p == 0, OFF[4 * batch + i], OFF[4 * batch + 2 + i]) + RING, RING)
            deliver(
                qa.at[at + PIECE * i : at + PIECE * (i + 1)], rc.at[single, x],
                cs2.at[single, batch, i], cr2.at[single, x], to,
            )

    def take(bundle):
        got = project(pieces(bundle, p))
        swap(bundle).wait_recv()
        at = rows_of(bundle)
        qa[at] = (got + sa[at].astype(F32)).astype(BF16)
        start = STARTS[bundle]
        if bundle == 0:
            post_row(OWN, start, 4 * PIECE, 0)
            for batch in range(2):
                post_single(0, batch, start + 4 * PIECE + 2 * PIECE * batch)
        elif bundle < 4:
            turn = bundle - 1
            for i in range(2):
                post_row(2 * turn + i, start + 4 * PIECE * i, 4 * PIECE, 0)
            for m in range(RING):
                from_row = start + 8 * PIECE + PIECE * m
                deliver(
                    qa.at[from_row : from_row + PIECE], rb.at[turn, x, p],
                    bs2.at[turn, m], br2.at[turn, x, p], target(m),
                )
        elif bundle % 2 == 0:
            post_row(FAR, start, 2 * PIECE, bundle // 2 - 2)
        else:
            post_single(1, bundle // 2 - 2, start)

    def own_wait():
        for copy in own:
            copy.wait()

    def place(kind, slot, rows):
        at = lax.rem(z + OFF[slot] + RING, RING) * (2 * PIECE) + kind * PIECE
        out_ref[pl.ds(pl.multiple_of(at, PIECE), PIECE), :] = rows.astype(BF16)

    def total(refs):
        found = None
        for ref in refs:
            term = ref[...].astype(F32)
            found = term if found is None else found + term
        return found

    def arrived(ref, sem):
        remote(ref, ref, cs2.at[0, 0, 0], sem, sibling).wait_recv()

    def pair_sums(turn):
        for half in range(2):
            for chip in range(4):
                arrived(rb.at[turn, chip, half], br2.at[turn, chip, half])
            place(1, 2 * turn + half, total([rb.at[turn, chip, half] for chip in range(4)]))

    def single_sums(single, slot):
        for chip in range(4):
            arrived(rc.at[single, chip], cr2.at[single, chip])
        place(1, slot, total([rc.at[single, chip] for chip in range(4)]))

    def row_sums():
        for half in range(2):
            for chip in range(4):
                arrived(ra.at[chip, half], ar2.at[chip, half])
            found = total([ra.at[chip, half] for chip in range(4)])
            for i in range(4):
                slot = 4 * (i // 2) + 2 * half + i % 2
                place(0, slot, found[PIECE * i : PIECE * (i + 1)])

    work(1.0, widen_all)
    for lo in (0, 4):
        work(1.4, features, BLOCKS - 1, (lo, lo + 4))
    work(0.1, send_tail)
    for lo in (0, 4):
        work(1.4, features, 1, (lo, lo + 4))
    work(0.3, halo_arrives)
    for lo in (0, 4):
        work(1.4, features, 0, (lo, lo + 4))
    work(0.1, tail_arrives)
    for lo in range(0, 64, 16):
        work(1.5, conv, lo, lo + 16)
    work(0.1, own_wait)
    work(1.0, give, 0)
    work(1.0, take, 0)
    for k in (1, 2, 3):
        need(k)
        work(1.8, give, k)
        work(2.2, take, k)
    def farthest(kind, packs):
        for pack in packs:
            for direction in lanes_of(kind, 4, pack):
                second(kind, direction, 4, pack).wait_recv()

    for kind in range(2):
        farthest(kind, (1, 2))
        give(4 + kind)
    take(4)
    take(5)
    for kind in range(2):
        farthest(kind, (0, 3, 4))
        give(6 + kind)
    pair_sums(0)
    take(6)
    pair_sums(1)
    take(7)
    single_sums(0, OWN)
    pair_sums(2)
    single_sums(1, FAR)
    row_sums()

    for copy in started:
        copy.wait_send()
    for to, copy in delivered:
        @pl.when(to != c)
        def drain(copy=copy):
            copy.wait_send()


def local(qkv, feat_taps, long_filter, skip_gain, out_weight):
    vmem = pl.BlockSpec(memory_space=pltpu.VMEM)
    anywhere = pl.BlockSpec(memory_space=pl.ANY)
    dma = pltpu.SemaphoreType.DMA
    half_piece = (4 * PIECE, ROWS)
    return pl.pallas_call(
        kernel,
        out_shape=jax.ShapeDtypeStruct((512, ROWS), BF16),
        in_specs=[anywhere] * 5,
        out_specs=vmem,
        scratch_shapes=[
            pltpu.VMEM((3, FTAPS, WIDTH), F32),
            pltpu.VMEM((WIDTH // GROUP, SPAN), BF16),
            pltpu.VMEM((1, WIDTH), F32),
            pltpu.VMEM((2, RING, RING, PIECE, WIDTH), BF16),
            pltpu.VMEM((3, ROWS, WIDTH), BF16),
            pltpu.VMEM((3, HALO, WIDTH), BF16),
            pltpu.VMEM((3, STRIPS, PAD + ROWS, LANES), F32),
            pltpu.VMEM((BLOCKS + 1, WIDTH, SPAN), BF16),
            pltpu.VMEM((BLOCKS, WIDTH, SPAN), F32),
            pltpu.VMEM((WIDTH, SPAN), F32),
            pltpu.VMEM((WIDTH // GROUP, SPAN), F32),
            pltpu.VMEM((WIDTH, ROWS), BF16),
            pltpu.VMEM((2048, ROWS), BF16),
            pltpu.VMEM((2048, ROWS), BF16),
            pltpu.VMEM((2048, ROWS), BF16),
            pltpu.VMEM((4, 2) + half_piece, BF16),
            pltpu.VMEM((PAIRS, 4, 2, PIECE, ROWS), BF16),
            pltpu.VMEM((2, 4, PIECE, ROWS), BF16),
            dma((6,)), dma((2,)), dma((2,)), dma((2,)),
            dma((2, 2, 4)), dma((2, 2, 4)),
            dma((2, 2, 4, 5)), dma((2, 2, 4, 5)),
            dma((8,)), dma((8,)), dma((RING, 2)), dma((4, 2)),
            dma((PAIRS, RING)), dma((PAIRS, 4, 2)), dma((2, 2, 2)), dma((2, 4)),
        ],
        compiler_params=pltpu.CompilerParams(
            collective_id=0, has_side_effects=True, vmem_limit_bytes=56 * 2**20
        ),
    )(qkv, feat_taps, long_filter.T, skip_gain.reshape(1, WIDTH), out_weight.T).T


def solution(mesh):
    return jax.shard_map(
        local,
        mesh=mesh,
        in_specs=(
            P(None, "seq", "chan"),
            P(None, None, "chan"),
            P(None, "chan"),
            P("chan"),
            P("chan", "seq"),
        ),
        out_specs=P("seq", "chan"),
        check_vma=False,
    )
```

```python
import jax
import jax.numpy as jnp
from jax import lax
from jax.experimental import pallas as pl
from jax.experimental.pallas import tpu as pltpu
from jax.sharding import PartitionSpec as P

MESH = pl.DeviceIdType.MESH
F32 = jnp.float32
BF16 = jnp.bfloat16

RING = 8
GROUP = 16
SPAN = 128
FTAPS = 7
ROWS = 384
WIDTH = 1024
BLOCKS = ROWS // SPAN
LANES = 128
STRIPS = WIDTH // LANES
PIECE = 32
HALO = 16
PAD = 8

OFF = (1, -1, 2, -2, 3, -3, 4, 0)
SLOT = {off: slot for slot, off in enumerate(OFF)}
PACKS = ((7, 8), (0, 2), (2, 4), (4, 6), (6, 7))
FAR_UP = ((0, 4), (0,))
OWN = SLOT[0]
FAR = SLOT[4]
PAIRS = 3


def origin(direction, step):
    return SLOT[4 if step == 4 else -direction * step]


def kernel(
    qkv_ref, taps_hbm, filt_hbm, skip_hbm, w_ref, out_ref,
    taps_ref, filt_ref, skip_ref,
    w_all, qkv_v, halo, ext, ut, qt, skt, hf, yt,
    ta, sa, qa, ra, rb, rc,
    load_sem, own_sem, halo_sem, tail_sem,
    s1, r1, s2, r2, as1, ar1, as2, ar2, bs2, br2, cs2, cr2,
):
    s = lax.axis_index("seq")
    c = lax.axis_index("chan")
    y = lax.div(s, RING)
    z = lax.rem(s, RING)
    x = lax.div(c, 2)
    p = lax.rem(c, 2)

    def y_at(d):
        return {"seq": lax.rem(y + d + RING, RING) * RING + z}

    def z_at(d):
        return {"seq": y * RING + lax.rem(z + d + RING, RING)}

    def seq_at(d):
        return {"seq": lax.rem(s + d + RING * RING, RING * RING)}

    sibling = {"chan": c + 1 - 2 * p}
    minor_at = (z_at, y_at)
    major_at = (y_at, z_at)
    started = []

    def remote(src, dst, send, recv, to):
        return pltpu.make_async_remote_copy(
            src_ref=src, dst_ref=dst, send_sem=send, recv_sem=recv, device_id=to, device_id_type=MESH
        )

    def go(copy):
        copy.start()
        started.append(copy)

    barrier = pltpu.get_barrier_semaphore()
    greeted = [{"chan": lax.rem(c + d, 8)} for d in range(1, 8)]
    greeted += [z_at(1), z_at(-1), y_at(1), y_at(-1), seq_at(1), seq_at(-1)]
    for to in greeted:
        pl.semaphore_signal(barrier, inc=1, device_id=to, device_id_type=MESH)

    loads = [
        pltpu.make_async_copy(qkv_ref.at[i], qkv_v.at[i], load_sem.at[i]) for i in (1, 2, 0)
    ]
    loads += [
        pltpu.make_async_copy(taps_hbm, taps_ref, load_sem.at[3]),
        pltpu.make_async_copy(filt_hbm, filt_ref, load_sem.at[4]),
        pltpu.make_async_copy(skip_hbm, skip_ref, load_sem.at[5]),
    ]
    own = [
        pltpu.make_async_copy(
            w_ref.at[PIECE * kind : PIECE * (kind + 1)], w_all.at[kind, OWN, OWN], own_sem.at[kind]
        )
        for kind in range(2)
    ]
    for copy in loads + own:
        copy.start()

    pl.semaphore_wait(barrier, len(greeted))

    def first(kind, direction, step):
        lane = 0 if direction == 1 else 1
        into = origin(direction, step)
        if step == 1:
            src, dst = w_ref.at[PIECE * kind : PIECE * (kind + 1)], w_all.at[kind, OWN, into]
        elif step < 4:
            src, dst = w_all.at[kind, OWN, origin(direction, step - 1)], w_all.at[kind, OWN, into]
        else:
            half = pl.ds(lane * (PIECE // 2), PIECE // 2)
            src = w_all.at[kind, OWN, origin(direction, 3), half]
            dst = w_all.at[kind, OWN, into, half]
        at = kind, lane, step - 1
        return remote(src, dst, s1.at[at], r1.at[at], minor_at[kind](direction))

    def second(kind, direction, step, pack):
        lane = 0 if direction == 1 else 1
        lo, hi = PACKS[pack]
        into = origin(direction, step)
        if step == 1 and pack == 0:
            src, dst = w_ref.at[PIECE * kind : PIECE * (kind + 1)], w_all.at[kind, into, OWN]
        else:
            came = OWN if step == 1 else origin(direction, step - 1)
            src = w_all.at[kind, came, pl.ds(lo, hi - lo)]
            dst = w_all.at[kind, into, pl.ds(lo, hi - lo)]
        at = kind, lane, step - 1, pack
        return remote(src, dst, s2.at[at], r2.at[at], major_at[kind](direction))

    def lanes_of(kind, step, pack):
        if step < 4:
            return (1, -1)
        return (1,) if pack in FAR_UP[kind] else (-1,)

    def first_arrives(step):
        for kind in range(2):
            for direction in (1, -1):
                first(kind, direction, step).wait_recv()
                if step < 4:
                    go(first(kind, direction, step + 1))
        for kind in range(2):
            for direction in (1, -1):
                go(second(kind, direction, 1, step))

    def second_arrives(step, pack):
        for kind in range(2):
            for direction in lanes_of(kind, step, pack):
                second(kind, direction, step, pack).wait_recv()
                if step < 4 and direction in lanes_of(kind, step + 1, pack):
                    go(second(kind, direction, step + 1, pack))

    events = [(at, first_arrives, (k,)) for k, at in enumerate((0.9, 3.5, 5.0, 6.6), 1)]
    events += [
        (2.6 + 10.5 * (k - 1) + 2.4 * g, second_arrives, (k, g)) for k in range(1, 5) for g in range(5)
    ]
    events.sort(key=lambda e: e[0])
    events = [(at, fn, args) for at, fn, args in events]
    clock = [0.0]
    seen = set()

    def take_event():
        at, fn, args = events.pop(0)
        fn(*args)
        if fn is second_arrives:
            seen.add(args)
        else:
            seen.add(args[0])
        clock[0] = max(clock[0], at)

    def work(cost, fn, *args):
        while events and events[0][0] <= clock[0]:
            take_event()
        fn(*args)
        clock[0] += cost

    def need(step):
        wanted = {(step, g) for g in range(5)}
        while not wanted <= seen:
            take_event()

    halo_copy = remote(
        qkv_ref.at[:, ROWS - HALO : ROWS], halo, halo_sem.at[0], halo_sem.at[1], seq_at(1)
    )
    for kind in range(2):
        for direction in (1, -1):
            go(first(kind, direction, 1))
    for kind in range(2):
        for direction in (1, -1):
            go(second(kind, direction, 1, 0))

    def widen(strip):
        at = pl.ds(pl.multiple_of(strip * LANES, LANES), LANES)
        for i in range(3):
            ext[i, strip, PAD:, :] = qkv_v[i, :, at].astype(F32)

    def widen_halo(strip):
        at = pl.ds(pl.multiple_of(strip * LANES, LANES), LANES)
        for i in range(3):
            before = halo[i, :, at].astype(F32)[HALO - PAD :]
            ext[i, strip, :PAD, :] = jnp.where(s == 0, 0.0, before)

    def feature(i, block, strip, at):
        total = None
        for j in range(FTAPS):
            term = taps_ref[i, j : j + 1, at] * ext[i, strip, pl.ds(PAD + SPAN * block - j, SPAN), :]
            total = term if total is None else total + term
        return total

    def features(block, strips):
        def body(strip, carry):
            at = pl.ds(pl.multiple_of(strip * LANES, LANES), LANES)
            u = (feature(1, block, strip, at) * feature(2, block, strip, at)).astype(BF16).astype(F32)
            ut[block + 1, at, :] = u.T.astype(BF16)
            qt[block, at, :] = feature(0, block, strip, at).T
            return carry

        lax.fori_loop(strips[0], strips[1], body, 0)

    def widen_all():
        for copy in loads:
            copy.wait()

        def body(strip, carry):
            widen(strip)
            return carry

        lax.fori_loop(0, STRIPS, body, 0)
        hf[...] = filt_ref[...].astype(F32)

    def halo_arrives():
        halo_copy.wait_recv()

        def body(strip, carry):
            widen_halo(strip)
            at = pl.ds(pl.multiple_of(strip * LANES, LANES), LANES)
            skt[at, :] = jnp.broadcast_to(skip_ref[:, at], (LANES, LANES)).T
            return carry

        lax.fori_loop(0, STRIPS, body, 0)

    tail_copy = remote(ut.at[BLOCKS], ut.at[0], tail_sem.at[0], tail_sem.at[1], seq_at(1))

    def send_tail():
        go(tail_copy)

    def tail_arrives():
        tail_copy.wait_recv()

        @pl.when(s == 0)
        def clear():
            ut[0] = jnp.zeros((WIDTH, SPAN), BF16)

    def conv(lo, hi):
        def body(g, carry):
            row = lax.broadcasted_iota(jnp.int32, (SPAN, SPAN), 0)
            col = lax.broadcasted_iota(jnp.int32, (SPAN, SPAN), 1)
            taps = jnp.broadcast_to(hf[pl.ds(g, 1), :], (SPAN, SPAN))
            ring = pltpu.roll(taps, 0, 1, stride=1, stride_axis=0)
            here = jnp.where(row <= col, ring, 0.0)
            before = jnp.where(row > col, ring, 0.0)
            matrix = jnp.concatenate([before, here], axis=0).astype(BF16)
            at = pl.ds(pl.multiple_of(g * GROUP, GROUP), GROUP)
            parts = [ut[b, at, :] for b in range(BLOCKS + 1)]
            window = jnp.concatenate(
                [jnp.concatenate(parts[:BLOCKS], axis=0), jnp.concatenate(parts[1:], axis=0)], axis=1
            )
            mixed = jnp.dot(window, matrix, preferred_element_type=F32)
            for b in range(BLOCKS):
                field = mixed[GROUP * b : GROUP * (b + 1)] + skt[at, :] * parts[b + 1].astype(F32)
                yt[at, SPAN * b : SPAN * (b + 1)] = (qt[b, at, :] * field).astype(BF16)
            return carry

        lax.fori_loop(lo, hi, body, 0, unroll=4)

    def project(pieces):
        rows = jnp.concatenate(pieces, axis=0) if len(pieces) > 1 else pieces[0]
        return jnp.dot(rows, yt[...], preferred_element_type=F32)

    def two(kind, major, batch, half):
        return w_all[kind, major, pl.ds(4 * batch + 2 * half, 2)].reshape(2 * PIECE, WIDTH)

    def four(kind, major, half):
        return [two(kind, major, batch, half) for batch in range(2)]

    def target(slot):
        return lax.rem(y + OFF[slot] + RING, RING)

    delivered = []

    def deliver(src, dst, send, recv, to):
        copy = remote(src, dst, send, recv, {"chan": to})

        @pl.when(to == c)
        def keep():
            pltpu.make_async_copy(src, dst, recv).start()

        @pl.when(to != c)
        def post():
            copy.start()

        delivered.append((to, copy))

    STARTS = (0, 256, 768, 1280, 1792, 1920)
    COUNTS = (256, 512, 512, 512, 128, 128)

    def b_rows(turn, half):
        return w_all[1, 2 * turn + half].reshape(RING * PIECE, WIDTH)

    def pieces(bundle, half):
        if bundle == 0:
            return four(0, OWN, half) + four(1, OWN, half)
        if bundle < 4:
            low = 2 * (bundle - 1)
            return four(0, low, half) + four(0, low + 1, half) + [b_rows(bundle - 1, half)]
        return [two(kind, FAR, bundle - 4, half) for kind in range(2)]

    def rows_of(bundle):
        return slice(STARTS[bundle], STARTS[bundle] + COUNTS[bundle])

    def swap(bundle):
        at = pl.ds(STARTS[bundle], COUNTS[bundle])
        return remote(ta.at[at], sa.at[at], as1.at[bundle], ar1.at[bundle], sibling)

    def give(bundle):
        ta[rows_of(bundle)] = project(pieces(bundle, 1 - p)).astype(BF16)
        copy = swap(bundle)
        go(copy)

    def post_row(slot, at, many, batch):
        deliver(
            qa.at[at : at + many], ra.at[x, p, pl.ds(2 * PIECE * batch, many)],
            as2.at[slot, batch], ar2.at[x, p], target(slot),
        )

    def post_single(single, batch, at):
        for i in range(2):
            to = lax.rem(y + jnp.where(p == 0, OFF[4 * batch + i], OFF[4 * batch + 2 + i]) + RING, RING)
            deliver(
                qa.at[at + PIECE * i : at + PIECE * (i + 1)], rc.at[single, x],
                cs2.at[single, batch, i], cr2.at[single, x], to,
            )

    def take(bundle):
        got = project(pieces(bundle, p))
        swap(bundle).wait_recv()
        at = rows_of(bundle)
        qa[at] = (got + sa[at].astype(F32)).astype(BF16)
        start = STARTS[bundle]
        if bundle == 0:
            post_row(OWN, start, 4 * PIECE, 0)
            for batch in range(2):
                post_single(0, batch, start + 4 * PIECE + 2 * PIECE * batch)
        elif bundle < 4:
            turn = bundle - 1
            for i in range(2):
                post_row(2 * turn + i, start + 4 * PIECE * i, 4 * PIECE, 0)
            for m in range(RING):
                from_row = start + 8 * PIECE + PIECE * m
                deliver(
                    qa.at[from_row : from_row + PIECE], rb.at[turn, x, p],
                    bs2.at[turn, m], br2.at[turn, x, p], target(m),
                )
        else:
            post_row(FAR, start, 2 * PIECE, bundle - 4)
            post_single(1, bundle - 4, start + 2 * PIECE)

    def own_wait():
        for copy in own:
            copy.wait()

    def place(kind, slot, rows):
        at = lax.rem(z + OFF[slot] + RING, RING) * (2 * PIECE) + kind * PIECE
        out_ref[pl.ds(pl.multiple_of(at, PIECE), PIECE), :] = rows.astype(BF16)

    def total(refs):
        found = None
        for ref in refs:
            term = ref[...].astype(F32)
            found = term if found is None else found + term
        return found

    def arrived(ref, sem):
        remote(ref, ref, cs2.at[0, 0, 0], sem, sibling).wait_recv()

    def pair_sums(turn):
        for half in range(2):
            for chip in range(4):
                arrived(rb.at[turn, chip, half], br2.at[turn, chip, half])
            place(1, 2 * turn + half, total([rb.at[turn, chip, half] for chip in range(4)]))

    def single_sums(single, slot):
        for chip in range(4):
            arrived(rc.at[single, chip], cr2.at[single, chip])
        place(1, slot, total([rc.at[single, chip] for chip in range(4)]))

    def row_sums():
        for half in range(2):
            for chip in range(4):
                arrived(ra.at[chip, half], ar2.at[chip, half])
            found = total([ra.at[chip, half] for chip in range(4)])
            for i in range(4):
                slot = 4 * (i // 2) + 2 * half + i % 2
                place(0, slot, found[PIECE * i : PIECE * (i + 1)])

    work(1.0, widen_all)
    take_event()
    go(halo_copy)
    for lo in (0, 4):
        work(1.4, features, BLOCKS - 1, (lo, lo + 4))
    work(0.1, send_tail)
    for lo in (0, 4):
        work(1.4, features, 1, (lo, lo + 4))
    work(0.3, halo_arrives)
    for lo in (0, 4):
        work(1.4, features, 0, (lo, lo + 4))
    work(0.1, tail_arrives)
    for lo in range(0, 64, 16):
        work(1.5, conv, lo, lo + 16)
    work(0.1, own_wait)
    work(1.0, give, 0)
    work(1.0, take, 0)
    for k in (1, 2, 3):
        need(k)
        work(1.8, give, k)
        work(2.2, take, k)
    while not {(4, g) for g in (0, 1, 2)} <= seen:
        take_event()
    give(4)
    take(4)
    need(4)
    give(5)
    pair_sums(0)
    pair_sums(1)
    single_sums(0, OWN)
    take(5)
    pair_sums(2)
    single_sums(1, FAR)
    row_sums()

    for copy in started:
        copy.wait_send()
    for to, copy in delivered:
        @pl.when(to != c)
        def drain(copy=copy):
            copy.wait_send()


def local(qkv, feat_taps, long_filter, skip_gain, out_weight):
    vmem = pl.BlockSpec(memory_space=pltpu.VMEM)
    anywhere = pl.BlockSpec(memory_space=pl.ANY)
    dma = pltpu.SemaphoreType.DMA
    half_piece = (4 * PIECE, ROWS)
    return pl.pallas_call(
        kernel,
        out_shape=jax.ShapeDtypeStruct((512, ROWS), BF16),
        in_specs=[anywhere] * 5,
        out_specs=vmem,
        scratch_shapes=[
            pltpu.VMEM((3, FTAPS, WIDTH), F32),
            pltpu.VMEM((WIDTH // GROUP, SPAN), BF16),
            pltpu.VMEM((1, WIDTH), F32),
            pltpu.VMEM((2, RING, RING, PIECE, WIDTH), BF16),
            pltpu.VMEM((3, ROWS, WIDTH), BF16),
            pltpu.VMEM((3, HALO, WIDTH), BF16),
            pltpu.VMEM((3, STRIPS, PAD + ROWS, LANES), F32),
            pltpu.VMEM((BLOCKS + 1, WIDTH, SPAN), BF16),
            pltpu.VMEM((BLOCKS, WIDTH, SPAN), F32),
            pltpu.VMEM((WIDTH, SPAN), F32),
            pltpu.VMEM((WIDTH // GROUP, SPAN), F32),
            pltpu.VMEM((WIDTH, ROWS), BF16),
            pltpu.VMEM((2048, ROWS), BF16),
            pltpu.VMEM((2048, ROWS), BF16),
            pltpu.VMEM((2048, ROWS), BF16),
            pltpu.VMEM((4, 2) + half_piece, BF16),
            pltpu.VMEM((PAIRS, 4, 2, PIECE, ROWS), BF16),
            pltpu.VMEM((2, 4, PIECE, ROWS), BF16),
            dma((6,)), dma((2,)), dma((2,)), dma((2,)),
            dma((2, 2, 4)), dma((2, 2, 4)),
            dma((2, 2, 4, 5)), dma((2, 2, 4, 5)),
            dma((6,)), dma((6,)), dma((RING, 2)), dma((4, 2)),
            dma((PAIRS, RING)), dma((PAIRS, 4, 2)), dma((2, 2, 2)), dma((2, 4)),
        ],
        compiler_params=pltpu.CompilerParams(
            collective_id=0, has_side_effects=True, vmem_limit_bytes=56 * 2**20
        ),
    )(qkv, feat_taps, long_filter.T, skip_gain.reshape(1, WIDTH), out_weight.T).T


def solution(mesh):
    return jax.shard_map(
        local,
        mesh=mesh,
        in_specs=(
            P(None, "seq", "chan"),
            P(None, None, "chan"),
            P(None, "chan"),
            P("chan"),
            P("chan", "seq"),
        ),
        out_specs=P("seq", "chan"),
        check_vma=False,
    )
```
